32 devices in a mesh: row: 4 (over y, x), col: 4 (over z), layer: 2 (over core).
Axes of the slice: x: 2, y: 2, z: 4, core: 2. Of those that a mesh axis runs over, the one named last changes fastest.
Arguments:
- trailing: float32 [4, 4, 256, 4, 4, 256], P(None, 'row', None, None, 'col'), may hold values from -6 to 6
- panel: float32 [4, 4, 256, 256], P(None, 'row', 'col'), may hold values from -0.6 to 0.6
- inverse_factor: float32 [256, 256], replicated, may hold values from -1 to 2, as said below
Outputs:
- updated: float32 [4, 4, 256, 4, 4, 256], P('layer', 'row', None, None, 'col')
The draws below stay inside these ranges and needn't reach their ends.
Inputs may be any that keep to these rules, and one draw needn't show every extreme that they name: inverse_factor is lower triangular; its diagonal lies between 1 and 2.
All inputs are finite; a program needn't handle non-finite values.
Results may differ from the reference program's by a relative error of at most 0.0025.
Values may be sent and summed in bfloat16 or wider, within the bound.
No kernel may reach another device: no remote copies, remote signals or barrier semaphores. Data moves between devices by JAX's collectives and lax.ppermute only.
A program may use at most 64 MiB of HBM per device.

```python
import jax
import jax.numpy as jnp
from jax import lax

B = 256
KR = 4
KC = 4
ORDER = 4096
N_ROW = 4
N_COL = 4


def draw_inverse_factor(key, part):
    key = jax.random.fold_in(key, 7)
    key_lower, key_diag = jax.random.split(key)
    lower = jax.random.normal(key_lower, (B, B), jnp.float32) * (0.35 / B ** 0.5)
    diagonal = jax.random.uniform(key_diag, (B,), jnp.float32, 1.0, 2.0)
    row_ids = lax.broadcasted_iota(jnp.int32, (B, B), 0)
    col_ids = lax.broadcasted_iota(jnp.int32, (B, B), 1)
    return jnp.where(row_ids > col_ids, lower, 0.0) + jnp.where(row_ids == col_ids, diagonal[:, None], 0.0)


def block_levels(own_key, dims, pieces, low, high):
    def one(axis_at, shards_of):
        heights = jax.random.uniform(jax.random.fold_in(jax.random.fold_in(own_key, 6), axis_at), (shards_of,), jnp.float32, low / len(pieces), high / len(pieces))
        return jnp.repeat(jnp.exp(heights), dims[axis_at] // shards_of).reshape((-1,) + (1,) * (len(dims) - axis_at - 1))

    loudness = one(*pieces[0])
    for cut in pieces[1:]:
        loudness = loudness * one(*cut)
    return loudness


def gaussian(rng, extent, deviation, limit, cuts=(), dtype=jnp.bfloat16):
    values = jax.random.normal(rng, extent, jnp.float32) * deviation
    if len(cuts) > 0:
        values = block_levels(rng, extent, cuts, -0.22, 0.18) * values
    return jnp.clip(values, min=-limit, max=limit).astype(dtype)


def setup_inputs(seed: int = 0) -> dict:
    splits = jax.random.split(jax.random.key(seed), 4)
    trailing = gaussian(splits[0], (KR, N_ROW, B, KC, N_COL, B), 1.0, 6.0, ((1, 4), (4, 4)), jnp.float32)
    panel = gaussian(splits[1], (KR, N_ROW, B, B), 0.1, 0.6, ((1, 4), (2, 4)), jnp.float32)
    inverse_factor = draw_inverse_factor(jax.random.fold_in(splits[3], 71), 0)
    return dict(trailing=trailing, panel=panel, inverse_factor=inverse_factor)


def reference(trailing, panel, inverse_factor):
    product = jnp.dot(panel.reshape(ORDER, B), inverse_factor.T, precision=lax.Precision.HIGHEST, preferred_element_type=jnp.float32)
    factor = product.astype(jnp.bfloat16)
    update = jnp.dot(factor, factor.T, preferred_element_type=jnp.float32)
    result = trailing.reshape(ORDER, ORDER) - update
    return result.reshape(KR, N_ROW, B, KC, N_COL, B)
```

```python
import jax
import jax.numpy as jnp
from jax import lax
from jax.experimental import pallas as pl
from jax.experimental.pallas import tpu as pltpu
from jax.sharding import PartitionSpec as P

LANES = 128
VMEM_BYTES = 24 * 1024 * 1024
AXES = ("row", "col", "layer")


def factor_kernel(panel_ref, inverse_ref, factor_ref, panel_buf, inverse_buf, sems):
    half = factor_ref.shape[0]
    tile_rows = factor_ref.shape[1]
    width = factor_ref.shape[2]
    layer = lax.axis_index("layer")
    copies = [
        pltpu.make_async_copy(panel_ref.at[pl.ds(layer * half, half), 0], panel_buf, sems.at[0]),
        pltpu.make_async_copy(inverse_ref, inverse_buf, sems.at[1]),
    ]
    for copy in copies:
        copy.start()
    for copy in copies:
        copy.wait()
    product = lax.dot_general(
        panel_buf[...].reshape(half * tile_rows, width),
        inverse_buf[...],
        (((1,), (1,)), ((), ())),
        precision=lax.Precision.HIGHEST,
        preferred_element_type=jnp.float32,
    )
    factor_ref[...] = product.astype(jnp.bfloat16).reshape(factor_ref.shape)


def make_factor(panel, inverse_factor, half):
    _, _, tile_rows, width = panel.shape
    return pl.pallas_call(
        factor_kernel,
        out_shape=jax.ShapeDtypeStruct((half, tile_rows, width), jnp.bfloat16),
        in_specs=[pl.BlockSpec(memory_space=pl.ANY)] * 2,
        out_specs=pl.BlockSpec(memory_space=pltpu.VMEM),
        scratch_shapes=[
            pltpu.VMEM((half, tile_rows, width), jnp.float32),
            pltpu.VMEM((width, width), jnp.float32),
            pltpu.SemaphoreType.DMA((2,)),
        ],
        compiler_params=pltpu.CompilerParams(vmem_limit_bytes=VMEM_BYTES),
        name="factor",
    )(panel, inverse_factor)


def partner(index, step, count):
    return index ^ step if count & (count - 1) == 0 else (index + step) % count


def update_kernel(pieces, layers, half, tile, tile_rows, col_tiles, *refs):
    row_refs = refs[:pieces]
    col_refs = refs[pieces : pieces * (1 + layers)]
    trailing_ref, out_ref, row_buf, col_buf, in_buf, out_buf, in_sems, out_sems = refs[pieces * (1 + layers) :]
    r, c, layer = (lax.axis_index(axis) for axis in AXES)
    lines = tile * col_tiles * tile // LANES
    per_row = col_tiles * tile // LANES
    loads = [
        pltpu.make_async_copy(
            trailing_ref.at[pl.ds((layer * half + k) * lines, lines)], in_buf.at[k], in_sems.at[k]
        )
        for k in range(half)
    ]
    for load in loads:
        load.start()
    for step in range(pieces):
        row_at = pl.multiple_of(partner(c, step, pieces) * tile_rows, tile_rows)
        col_at = pl.multiple_of(partner(r, step, pieces) * tile_rows, tile_rows)
        for k in range(half):
            row_buf[k, pl.ds(row_at, tile_rows), :] = row_refs[step][k]
        for shift in range(layers):
            owner = lax.rem(layer + shift, layers)
            for k in range(half):
                col_buf[owner * half + k, pl.ds(col_at, tile_rows), :] = col_refs[shift * pieces + step][k]
    stores = []
    for k in range(half):
        loads[k].wait()
        for j in range(col_tiles):
            update = lax.dot_general(
                row_buf[k], col_buf[j], (((1,), (1,)), ((), ())), preferred_element_type=jnp.float32
            )
            for part in range(tile // LANES):
                lines_at = pl.ds(j * (tile // LANES) + part, tile, stride=per_row)
                out_buf[k, lines_at, :] = in_buf[k, lines_at, :] - update[:, part * LANES : (part + 1) * LANES]
        store = pltpu.make_async_copy(out_buf.at[k], out_ref.at[pl.ds(k * lines, lines)], out_sems.at[k])
        store.start()
        stores.append(store)
    for store in stores:
        store.wait()


def update_trailing(row_pieces, col_pieces, trailing, half, layers):
    row_tiles, _, tile, col_tiles, _, _ = trailing.shape
    pieces = len(row_pieces)
    tile_rows = row_pieces[0].shape[1]
    width = row_pieces[0].shape[2]
    lines = tile * col_tiles * tile // LANES

    def body(*refs):
        update_kernel(pieces, layers, half, tile, tile_rows, col_tiles, *refs)

    result = pl.pallas_call(
        body,
        out_shape=jax.ShapeDtypeStruct((half * lines, LANES), jnp.float32),
        in_specs=[pl.BlockSpec(memory_space=pltpu.VMEM)] * (pieces * (1 + layers))
        + [pl.BlockSpec(memory_space=pl.ANY)],
        out_specs=pl.BlockSpec(memory_space=pl.ANY),
        scratch_shapes=[
            pltpu.VMEM((half, tile, width), jnp.bfloat16),
            pltpu.VMEM((half * layers, tile, width), jnp.bfloat16),
            pltpu.VMEM((half, lines, LANES), jnp.float32),
            pltpu.VMEM((half, lines, LANES), jnp.float32),
            pltpu.SemaphoreType.DMA((half,)),
            pltpu.SemaphoreType.DMA((half,)),
        ],
        compiler_params=pltpu.CompilerParams(vmem_limit_bytes=VMEM_BYTES),
        name="update",
    )(*row_pieces, *col_pieces, trailing.reshape(row_tiles * lines, LANES))
    return result.reshape(half, 1, tile, col_tiles, 1, tile)


def per_device(trailing, panel, inverse_factor):
    layers = lax.axis_size("layer")
    count = lax.axis_size("row")
    half = trailing.shape[0] // layers
    factor = make_factor(panel, inverse_factor, half)
    swapped = lax.ppermute(
        factor, ("row", "col"), [(a * count + b, b * count + a) for a in range(count) for b in range(count)]
    )
    plane = [swapped]
    for step in range(1, count):
        plane.append(lax.ppermute(swapped, "row", [(a, partner(a, step, count)) for a in range(count)]))
    line = [factor]
    for step in range(1, count):
        line.append(lax.ppermute(factor, "col", [(partner(b, step, count), b) for b in range(count)]))
    others = []
    for shift in range(1, layers):
        pairs = [((l + shift) % layers, l) for l in range(layers)]
        others += [lax.ppermute(piece, "layer", pairs) for piece in plane]
    return update_trailing(line, plane + others, trailing, half, layers)


def solution(mesh):
    assert mesh.shape["row"] == mesh.shape["col"]
    return jax.shard_map(
        per_device,
        mesh=mesh,
        in_specs=(P(None, "row", None, None, "col", None), P(None, "row", "col", None), P()),
        out_specs=P("layer", "row", None, None, "col", None),
        check_vma=False,
    )
```

```python
import jax
import jax.numpy as jnp
from jax import lax
from jax.experimental import pallas as pl
from jax.experimental.pallas import tpu as pltpu
from jax.sharding import PartitionSpec as P

LANES = 128
VMEM_BYTES = 24 * 1024 * 1024
FACTOR_VMEM_BYTES = 56 * 1024 * 1024
AXES = ("row", "col", "layer")


def factor_kernel(panel_ref, inverse_ref, factor_ref, panel_buf, inverse_buf, sems):
    half = factor_ref.shape[0]
    tile_rows = factor_ref.shape[1]
    width = factor_ref.shape[2]
    layer = lax.axis_index("layer")
    copies = [
        pltpu.make_async_copy(panel_ref.at[pl.ds(layer * half, half), 0], panel_buf, sems.at[0]),
        pltpu.make_async_copy(inverse_ref, inverse_buf, sems.at[1]),
    ]
    for copy in copies:
        copy.start()
    for copy in copies:
        copy.wait()
    product = lax.dot_general(
        panel_buf[...].reshape(half * tile_rows, width),
        inverse_buf[...],
        (((1,), (1,)), ((), ())),
        precision=lax.Precision.HIGHEST,
        preferred_element_type=jnp.float32,
    )
    factor_ref[...] = product.astype(jnp.bfloat16).reshape(factor_ref.shape)


def make_factor(panel, inverse_factor, half):
    _, _, tile_rows, width = panel.shape
    return pl.pallas_call(
        factor_kernel,
        out_shape=jax.ShapeDtypeStruct((half, tile_rows, width), jnp.bfloat16),
        in_specs=[pl.BlockSpec(memory_space=pltpu.HBM)] * 2,
        out_specs=pl.BlockSpec(memory_space=pltpu.VMEM),
        scratch_shapes=[
            pltpu.VMEM((half, tile_rows, width), jnp.float32),
            pltpu.VMEM((width, width), jnp.float32),
            pltpu.SemaphoreType.DMA((2,)),
        ],
        compiler_params=pltpu.CompilerParams(vmem_limit_bytes=FACTOR_VMEM_BYTES),
        name="factor",
    )(panel, inverse_factor)


def partner(index, step, count):
    return index ^ step if count & (count - 1) == 0 else (index + step) % count


def plane_slots(count):
    if count == 4:
        return ((1, 3, 2, 0), (0, 2, 1, 3), (2, 0, 3, 1), (3, 1, 0, 2))
    return tuple(tuple(count - 1 - b for b in range(count)) for _ in range(count))


def slab_of(slots, plane, place):
    slab = jnp.int32(0)
    for at, row in enumerate(slots):
        for b, slot in enumerate(row):
            slab = jnp.where((plane == at) & (place == slot), b, slab)
    return slab


def update_kernel(pieces, layers, half, tile, tile_rows, col_tiles, *refs):
    row_refs = refs[:pieces]
    col_refs = refs[pieces : pieces * (1 + layers)]
    share_ref, out_ref, row_buf, col_buf, out_buf, out_sems = refs[pieces * (1 + layers) :]
    r, c, layer = (lax.axis_index(axis) for axis in AXES)
    slots = plane_slots(pieces)
    lines = tile * col_tiles * tile // LANES
    per_row = col_tiles * tile // LANES
    for step in range(pieces):
        row_at = pl.multiple_of(partner(c, step, pieces) * tile_rows, tile_rows)
        slab = slab_of(slots, c, partner(r, step, pieces))
        col_at = pl.multiple_of(slab * tile_rows, tile_rows)
        for k in range(half):
            row_buf[k, pl.ds(row_at, tile_rows), :] = row_refs[step][k]
        for shift in range(layers):
            owner = lax.rem(layer + shift, layers)
            for k in range(half):
                col_buf[owner * half + k, pl.ds(col_at, tile_rows), :] = col_refs[shift * pieces + step][k]
    stores = []
    for k in range(half):
        for j in range(col_tiles):
            update = lax.dot_general(
                row_buf[k], col_buf[j], (((1,), (1,)), ((), ())), preferred_element_type=jnp.float32
            )
            for part in range(tile // LANES):
                first = j * (tile // LANES) + part
                out_buf[pl.ds(k * lines + first, tile, stride=per_row), :] = (
                    share_ref[pl.ds(k * lines + first, tile, stride=per_row), :]
                    - update[:, part * LANES : (part + 1) * LANES]
                )
        share = pl.ds(k * lines, lines)
        store = pltpu.make_async_copy(out_buf.at[share], out_ref.at[share], out_sems.at[k])
        store.start()
        stores.append(store)
    for store in stores:
        store.wait()


def update_trailing(row_pieces, col_pieces, share, half, layers, tile, col_tiles):
    pieces = len(row_pieces)
    tile_rows = row_pieces[0].shape[1]
    width = row_pieces[0].shape[2]

    def body(*refs):
        update_kernel(pieces, layers, half, tile, tile_rows, col_tiles, *refs)

    result = pl.pallas_call(
        body,
        out_shape=jax.ShapeDtypeStruct(share.shape, jnp.float32),
        in_specs=[pl.BlockSpec(memory_space=pltpu.VMEM)] * (pieces * (1 + layers) + 1),
        out_specs=pl.BlockSpec(memory_space=pltpu.HBM),
        scratch_shapes=[
            pltpu.VMEM((half, tile, width), jnp.bfloat16),
            pltpu.VMEM((half * layers, tile, width), jnp.bfloat16),
            pltpu.VMEM(share.shape, jnp.float32),
            pltpu.SemaphoreType.DMA((half,)),
        ],
        compiler_params=pltpu.CompilerParams(vmem_limit_bytes=VMEM_BYTES),
        name="update",
    )(*row_pieces, *col_pieces, share)
    return result.reshape(half, 1, tile, col_tiles, 1, tile)


def per_device(trailing, panel, inverse_factor):
    layers = lax.axis_size("layer")
    count = lax.axis_size("row")
    row_tiles, _, tile, col_tiles, _, _ = trailing.shape
    half = row_tiles // layers
    slots = plane_slots(count)
    factor = make_factor(panel, inverse_factor, half)
    moved = lax.ppermute(
        factor, ("row", "col"), [(a * count + b, slots[a][b] * count + a) for a in range(count) for b in range(count)]
    )
    line = [factor] + [None] * (count - 1)
    for step in reversed(range(1, count)):
        line[step] = lax.ppermute(factor, "col", [(partner(b, step, count), b) for b in range(count)])
    lines = trailing.reshape(-1, LANES)
    share_lines = lines.shape[0] // layers
    share = lax.dynamic_slice_in_dim(lines, lax.axis_index("layer") * share_lines, share_lines, 0)
    moved, share = lax.optimization_barrier((moved, share))
    plane = [moved] + [None] * (count - 1)
    for step in reversed(range(1, count)):
        plane[step] = lax.ppermute(moved, "row", [(partner(a, step, count), a) for a in range(count)])
    others = []
    for shift in range(1, layers):
        pairs = [((l + shift) % layers, l) for l in range(layers)]
        others += [lax.ppermute(piece, "layer", pairs) for piece in plane]
    return update_trailing(line, plane + others, share, half, layers, tile, col_tiles)


def solution(mesh):
    assert mesh.shape["row"] == mesh.shape["col"]
    return jax.shard_map(
        per_device,
        mesh=mesh,
        in_specs=(P(None, "row", None, None, "col", None), P(None, "row", "col", None), P()),
        out_specs=P("layer", "row", None, None, "col", None),
        check_vma=False,
    )
```

```python
import jax
import jax.numpy as jnp
from jax import lax
from jax.experimental import pallas as pl
from jax.experimental.pallas import tpu as pltpu
from jax.sharding import PartitionSpec as P

LANES = 128
VMEM_BYTES = 24 * 1024 * 1024
FACTOR_VMEM_BYTES = 56 * 1024 * 1024
AXES = ("row", "col", "layer")


def factor_kernel(panel_ref, inverse_ref, factor_ref, panel_buf, inverse_buf, sems):
    half = factor_ref.shape[0]
    tile_rows = factor_ref.shape[1]
    width = factor_ref.shape[2]
    layer = lax.axis_index("layer")
    copies = [
        pltpu.make_async_copy(panel_ref.at[pl.ds(layer * half, half), 0], panel_buf, sems.at[0]),
        pltpu.make_async_copy(inverse_ref, inverse_buf, sems.at[1]),
    ]
    for copy in copies:
        copy.start()
    for copy in copies:
        copy.wait()
    product = lax.dot_general(
        panel_buf[...].reshape(half * tile_rows, width),
        inverse_buf[...],
        (((1,), (1,)), ((), ())),
        precision=lax.Precision.HIGHEST,
        preferred_element_type=jnp.float32,
    )
    factor_ref[...] = product.astype(jnp.bfloat16).reshape(factor_ref.shape)


def make_factor(panel, inverse_factor, half):
    _, _, tile_rows, width = panel.shape
    return pl.pallas_call(
        factor_kernel,
        out_shape=jax.ShapeDtypeStruct((half, tile_rows, width), jnp.bfloat16),
        in_specs=[pl.BlockSpec(memory_space=pltpu.HBM)] * 2,
        out_specs=pl.BlockSpec(memory_space=pltpu.VMEM),
        scratch_shapes=[
            pltpu.VMEM((half, tile_rows, width), jnp.float32),
            pltpu.VMEM((width, width), jnp.float32),
            pltpu.SemaphoreType.DMA((2,)),
        ],
        compiler_params=pltpu.CompilerParams(vmem_limit_bytes=FACTOR_VMEM_BYTES),
        name="factor",
    )(panel, inverse_factor)


def partner(index, step, count):
    return index ^ step if count & (count - 1) == 0 else (index + step) % count


def plane_slots(count):
    if count == 4:
        return ((1, 3, 2, 0), (0, 2, 1, 3), (2, 0, 3, 1), (3, 1, 0, 2))
    return tuple(tuple(count - 1 - b for b in range(count)) for _ in range(count))


def slab_of(slots, plane, place):
    slab = jnp.int32(0)
    for at, row in enumerate(slots):
        for b, slot in enumerate(row):
            slab = jnp.where((plane == at) & (place == slot), b, slab)
    return slab


def gather_line(factor, count):
    everywhere = range(count)
    if count != 4:
        pairs = {step: [(partner(b, step, count), b) for b in everywhere] for step in range(1, count)}
        moves = [(lax.ppermute(factor, "col", pairs[step]), {b: a for a, b in pairs[step]}) for step in pairs]
        return [(factor, {b: b for b in everywhere})] + moves
    near = [(0, 1), (1, 0), (2, 3), (3, 2)]
    far = [(0, 2), (2, 0), (1, 3), (3, 1)]
    inner = [(1, 2), (2, 1)]
    outer = [(1, 0), (2, 3)]
    from_far = lax.ppermute(factor, "col", far)
    from_near = lax.ppermute(factor, "col", near)
    from_inner = lax.ppermute(factor, "col", inner)
    from_outer = lax.ppermute(from_far, "col", outer)
    return [
        (factor, {b: b for b in everywhere}),
        (from_near, {b: a for a, b in near}),
        (from_far, {b: a for a, b in far}),
        (from_inner, {b: a for a, b in inner}),
        (from_outer, {0: 3, 3: 0}),
    ]


def lookup(table, index):
    value = jnp.int32(0)
    for key, entry in table.items():
        value = jnp.where(index == key, entry, value)
    return value


def update_kernel(sources, pieces, layers, half, tile, tile_rows, col_tiles, *refs):
    rows = len(sources)
    row_refs = refs[:rows]
    col_refs = refs[rows : rows + pieces * layers]
    share_ref, out_ref, row_buf, col_buf, out_buf, out_sems = refs[rows + pieces * layers :]
    r, c, layer = (lax.axis_index(axis) for axis in AXES)
    slots = plane_slots(pieces)
    lines = tile * col_tiles * tile // LANES
    per_row = col_tiles * tile // LANES
    for source, row_ref in zip(sources, row_refs):
        row_at = pl.multiple_of(lookup(source, c) * tile_rows, tile_rows)

        def place_rows(row_ref=row_ref, row_at=row_at):
            for k in range(half):
                row_buf[k, pl.ds(row_at, tile_rows), :] = row_ref[k]

        if len(source) == pieces:
            place_rows()
        else:
            here = c == next(iter(source))
            for key in source:
                here = here | (c == key)
            pl.when(here)(place_rows)
    for step in range(pieces):
        slab = slab_of(slots, c, partner(r, step, pieces))
        col_at = pl.multiple_of(slab * tile_rows, tile_rows)
        for shift in range(layers):
            owner = lax.rem(layer + shift, layers)
            for k in range(half):
                col_buf[owner * half + k, pl.ds(col_at, tile_rows), :] = col_refs[shift * pieces + step][k]
    stores = []
    for k in range(half):
        for j in range(col_tiles):
            update = lax.dot_general(
                row_buf[k], col_buf[j], (((1,), (1,)), ((), ())), preferred_element_type=jnp.float32
            )
            for part in range(tile // LANES):
                first = j * (tile // LANES) + part
                out_buf[pl.ds(k * lines + first, tile, stride=per_row), :] = (
                    share_ref[pl.ds(k * lines + first, tile, stride=per_row), :]
                    - update[:, part * LANES : (part + 1) * LANES]
                )
        share = pl.ds(k * lines, lines)
        store = pltpu.make_async_copy(out_buf.at[share], out_ref.at[share], out_sems.at[k])
        store.start()
        stores.append(store)
    for store in stores:
        store.wait()


def update_trailing(line, col_pieces, share, half, layers, tile, col_tiles):
    row_pieces, sources = zip(*line)
    pieces = len(col_pieces) // layers
    tile_rows = row_pieces[0].shape[1]
    width = row_pieces[0].shape[2]

    def body(*refs):
        update_kernel(sources, pieces, layers, half, tile, tile_rows, col_tiles, *refs)

    result = pl.pallas_call(
        body,
        out_shape=jax.ShapeDtypeStruct(share.shape, jnp.float32),
        in_specs=[pl.BlockSpec(memory_space=pltpu.VMEM)] * (len(row_pieces) + len(col_pieces) + 1),
        out_specs=pl.BlockSpec(memory_space=pltpu.HBM),
        scratch_shapes=[
            pltpu.VMEM((half, tile, width), jnp.bfloat16),
            pltpu.VMEM((half * layers, tile, width), jnp.bfloat16),
            pltpu.VMEM(share.shape, jnp.float32),
            pltpu.SemaphoreType.DMA((half,)),
        ],
        compiler_params=pltpu.CompilerParams(vmem_limit_bytes=VMEM_BYTES),
        name="update",
    )(*row_pieces, *col_pieces, share)
    return result.reshape(half, 1, tile, col_tiles, 1, tile)


def per_device(trailing, panel, inverse_factor):
    layers = lax.axis_size("layer")
    count = lax.axis_size("row")
    row_tiles, _, tile, col_tiles, _, _ = trailing.shape
    half = row_tiles // layers
    slots = plane_slots(count)
    factor = make_factor(panel, inverse_factor, half)
    moved = lax.ppermute(
        factor, ("row", "col"), [(a * count + b, slots[a][b] * count + a) for a in range(count) for b in range(count)]
    )
    line = gather_line(factor, count)
    lines = trailing.reshape(-1, LANES)
    share_lines = lines.shape[0] // layers
    share = lax.dynamic_slice_in_dim(lines, lax.axis_index("layer") * share_lines, share_lines, 0)
    moved, share = lax.optimization_barrier((moved, share))
    plane = [moved] + [None] * (count - 1)
    for step in reversed(range(1, count)):
        plane[step] = lax.ppermute(moved, "row", [(partner(a, step, count), a) for a in range(count)])
    others = []
    for shift in range(1, layers):
        pairs = [((l + shift) % layers, l) for l in range(layers)]
        others += [lax.ppermute(piece, "layer", pairs) for piece in plane]
    return update_trailing(line, plane + others, share, half, layers, tile, col_tiles)


def solution(mesh):
    assert mesh.shape["row"] == mesh.shape["col"]
    return jax.shard_map(
        per_device,
        mesh=mesh,
        in_specs=(P(None, "row", None, None, "col", None), P(None, "row", "col", None), P()),
        out_specs=P("layer", "row", None, None, "col", None),
        check_vma=False,
    )
```

```python
import jax
import jax.numpy as jnp
from jax import lax
from jax.experimental import pallas as pl
from jax.experimental.pallas import tpu as pltpu
from jax.sharding import PartitionSpec as P

LANES = 128
VMEM_BYTES = 24 * 1024 * 1024
LOAD_VMEM_BYTES = 52000 * 1024
FACTOR_VMEM_BYTES = 55040 * 1024
AXES = ("row", "col", "layer")


def factor_kernel(panel_ref, inverse_ref, factor_ref, panel_buf, inverse_buf, sems):
    half = factor_ref.shape[0]
    tile_rows = factor_ref.shape[1]
    width = factor_ref.shape[2]
    layer = lax.axis_index("layer")
    copies = [
        pltpu.make_async_copy(panel_ref.at[pl.ds(layer * half, half), 0], panel_buf, sems.at[0]),
        pltpu.make_async_copy(inverse_ref, inverse_buf, sems.at[1]),
    ]
    for copy in copies:
        copy.start()
    for copy in copies:
        copy.wait()
    product = lax.dot_general(
        panel_buf[...].reshape(half * tile_rows, width),
        inverse_buf[...],
        (((1,), (1,)), ((), ())),
        precision=lax.Precision.HIGHEST,
        preferred_element_type=jnp.float32,
    )
    factor_ref[...] = product.astype(jnp.bfloat16).reshape(factor_ref.shape)


def make_factor(panel, inverse_factor, half):
    _, _, tile_rows, width = panel.shape
    return pl.pallas_call(
        factor_kernel,
        out_shape=jax.ShapeDtypeStruct((half, tile_rows, width), jnp.bfloat16),
        in_specs=[pl.BlockSpec(memory_space=pltpu.HBM)] * 2,
        out_specs=pl.BlockSpec(memory_space=pltpu.VMEM),
        scratch_shapes=[
            pltpu.VMEM((half, tile_rows, width), jnp.float32),
            pltpu.VMEM((width, width), jnp.float32),
            pltpu.SemaphoreType.DMA((2,)),
        ],
        compiler_params=pltpu.CompilerParams(vmem_limit_bytes=FACTOR_VMEM_BYTES),
        name="factor",
    )(panel, inverse_factor)


def partner(index, step, count):
    return index ^ step if count & (count - 1) == 0 else (index + step) % count


def plane_slots(count):
    if count == 4:
        return ((1, 3, 2, 0), (0, 2, 1, 3), (2, 0, 3, 1), (3, 1, 0, 2))
    return tuple(tuple(count - 1 - b for b in range(count)) for _ in range(count))


def slab_of(slots, plane, place):
    slab = jnp.int32(0)
    for at, row in enumerate(slots):
        for b, slot in enumerate(row):
            slab = jnp.where((plane == at) & (place == slot), b, slab)
    return slab


def gather_line(factor, count):
    if count != 4:
        line = [factor]
        for step in range(1, count):
            line.append(lax.ppermute(factor, "col", [(partner(b, step, count), b) for b in range(count)]))
        return line
    far = lax.ppermute(factor, "col", [(b ^ 2, b) for b in range(count)])
    near = lax.ppermute(factor, "col", [(b ^ 1, b) for b in range(count)])
    both = lax.ppermute(far, "col", [(b ^ 1, b) for b in range(count)])
    return [factor, near, far, both]


def load_kernel(after_ref, lines_ref, share_ref, sem):
    rows = share_ref.shape[0]
    layer = lax.axis_index("layer")
    load = pltpu.make_async_copy(lines_ref.at[pl.ds(layer * rows, rows)], share_ref, sem)
    load.start()
    load.wait()


def load_share(after, lines, layers):
    rows = lines.shape[0] // layers
    return pl.pallas_call(
        load_kernel,
        out_shape=jax.ShapeDtypeStruct((rows, LANES), jnp.float32),
        in_specs=[pl.BlockSpec(memory_space=pl.ANY), pl.BlockSpec(memory_space=pltpu.HBM)],
        out_specs=pl.BlockSpec(memory_space=pltpu.VMEM),
        scratch_shapes=[pltpu.SemaphoreType.DMA],
        compiler_params=pltpu.CompilerParams(vmem_limit_bytes=LOAD_VMEM_BYTES),
        cost_estimate=pl.CostEstimate(flops=0, bytes_accessed=rows * LANES * 8, transcendentals=0),
        name="load_share",
    )(after, lines)


def update_kernel(pieces, layers, half, tile, tile_rows, col_tiles, *refs):
    row_refs = refs[:pieces]
    col_refs = refs[pieces : pieces * (1 + layers)]
    share_ref, out_ref, row_buf, col_buf, out_buf, out_sems = refs[pieces * (1 + layers) :]
    r, c, layer = (lax.axis_index(axis) for axis in AXES)
    slots = plane_slots(pieces)
    lines = tile * col_tiles * tile // LANES
    per_row = col_tiles * tile // LANES
    for step in range(pieces):
        row_at = pl.multiple_of(partner(c, step, pieces) * tile_rows, tile_rows)
        slab = slab_of(slots, c, partner(r, step, pieces))
        col_at = pl.multiple_of(slab * tile_rows, tile_rows)
        for k in range(half):
            row_buf[k, pl.ds(row_at, tile_rows), :] = row_refs[step][k]
        for shift in range(layers):
            owner = lax.rem(layer + shift, layers)
            for k in range(half):
                col_buf[owner * half + k, pl.ds(col_at, tile_rows), :] = col_refs[shift * pieces + step][k]
    stores = []
    for k in range(half):
        for j in range(col_tiles):
            update = lax.dot_general(
                row_buf[k], col_buf[j], (((1,), (1,)), ((), ())), preferred_element_type=jnp.float32
            )
            for part in range(tile // LANES):
                first = j * (tile // LANES) + part
                out_buf[pl.ds(k * lines + first, tile, stride=per_row), :] = (
                    share_ref[pl.ds(k * lines + first, tile, stride=per_row), :]
                    - update[:, part * LANES : (part + 1) * LANES]
                )
        share = pl.ds(k * lines, lines)
        store = pltpu.make_async_copy(out_buf.at[share], out_ref.at[share], out_sems.at[k])
        store.start()
        stores.append(store)
    for store in stores:
        store.wait()


def update_trailing(row_pieces, col_pieces, share, half, layers, tile, col_tiles):
    pieces = len(row_pieces)
    tile_rows = row_pieces[0].shape[1]
    width = row_pieces[0].shape[2]

    def body(*refs):
        update_kernel(pieces, layers, half, tile, tile_rows, col_tiles, *refs)

    result = pl.pallas_call(
        body,
        out_shape=jax.ShapeDtypeStruct(share.shape, jnp.float32),
        in_specs=[pl.BlockSpec(memory_space=pltpu.VMEM)] * (pieces * (1 + layers) + 1),
        out_specs=pl.BlockSpec(memory_space=pltpu.HBM),
        scratch_shapes=[
            pltpu.VMEM((half, tile, width), jnp.bfloat16),
            pltpu.VMEM((half * layers, tile, width), jnp.bfloat16),
            pltpu.VMEM(share.shape, jnp.float32),
            pltpu.SemaphoreType.DMA((half,)),
        ],
        compiler_params=pltpu.CompilerParams(vmem_limit_bytes=VMEM_BYTES),
        name="update",
    )(*row_pieces, *col_pieces, share)
    return result.reshape(half, 1, tile, col_tiles, 1, tile)


def per_device(trailing, panel, inverse_factor):
    layers = lax.axis_size("layer")
    count = lax.axis_size("row")
    row_tiles, _, tile, col_tiles, _, _ = trailing.shape
    half = row_tiles // layers
    slots = plane_slots(count)
    factor = make_factor(panel, inverse_factor, half)
    moved = lax.ppermute(
        factor, ("row", "col"), [(a * count + b, slots[a][b] * count + a) for a in range(count) for b in range(count)]
    )
    line = gather_line(factor, count)
    share = load_share(factor, trailing.reshape(-1, LANES), layers)
    moved, share = lax.optimization_barrier((moved, share))
    plane = [moved] + [None] * (count - 1)
    for step in reversed(range(1, count)):
        plane[step] = lax.ppermute(moved, "row", [(partner(a, step, count), a) for a in range(count)])
    others = []
    for shift in range(1, layers):
        pairs = [((l + shift) % layers, l) for l in range(layers)]
        others += [lax.ppermute(piece, "layer", pairs) for piece in plane]
    return update_trailing(line, plane + others, share, half, layers, tile, col_tiles)


def solution(mesh):
    assert mesh.shape["row"] == mesh.shape["col"]
    return jax.shard_map(
        per_device,
        mesh=mesh,
        in_specs=(P(None, "row", None, None, "col", None), P(None, "row", "col", None), P()),
        out_specs=P("layer", "row", None, None, "col", None),
        check_vma=False,
    )
```

```python
import jax
import jax.numpy as jnp
from jax import lax
from jax.experimental import pallas as pl
from jax.experimental.pallas import tpu as pltpu
from jax.sharding import PartitionSpec as P

LANES = 128
CHUNK_ROWS = 128
VMEM_BYTES = 24 * 1024 * 1024
LOAD_VMEM_BYTES = 52000 * 1024
FACTOR_VMEM_BYTES = 55040 * 1024
AXES = ("row", "col", "layer")


def factor_kernel(panel_ref, inverse_ref, factor_ref, panel_buf, inverse_buf, sems):
    half = factor_ref.shape[0]
    tile_rows = factor_ref.shape[1]
    width = factor_ref.shape[2]
    layer = lax.axis_index("layer")
    copies = [
        pltpu.make_async_copy(panel_ref.at[pl.ds(layer * half, half), 0], panel_buf, sems.at[0]),
        pltpu.make_async_copy(inverse_ref, inverse_buf, sems.at[1]),
    ]
    for copy in copies:
        copy.start()
    for copy in copies:
        copy.wait()
    product = lax.dot_general(
        panel_buf[...].reshape(half * tile_rows, width),
        inverse_buf[...],
        (((1,), (1,)), ((), ())),
        precision=lax.Precision.HIGHEST,
        preferred_element_type=jnp.float32,
    )
    factor_ref[...] = product.astype(jnp.bfloat16).reshape(factor_ref.shape)


def make_factor(panel, inverse_factor, half):
    _, _, tile_rows, width = panel.shape
    return pl.pallas_call(
        factor_kernel,
        out_shape=jax.ShapeDtypeStruct((half, tile_rows, width), jnp.bfloat16),
        in_specs=[pl.BlockSpec(memory_space=pltpu.HBM)] * 2,
        out_specs=pl.BlockSpec(memory_space=pltpu.VMEM),
        scratch_shapes=[
            pltpu.VMEM((half, tile_rows, width), jnp.float32),
            pltpu.VMEM((width, width), jnp.float32),
            pltpu.SemaphoreType.DMA((2,)),
        ],
        compiler_params=pltpu.CompilerParams(vmem_limit_bytes=FACTOR_VMEM_BYTES),
        name="factor",
    )(panel, inverse_factor)


def partner(index, step, count):
    return index ^ step if count & (count - 1) == 0 else (index + step) % count


def plane_slots(count):
    if count == 4:
        return ((1, 3, 2, 0), (0, 2, 1, 3), (2, 0, 3, 1), (3, 1, 0, 2))
    return tuple(tuple(count - 1 - b for b in range(count)) for _ in range(count))


def slab_of(slots, plane, place):
    slab = jnp.int32(0)
    for at, row in enumerate(slots):
        for b, slot in enumerate(row):
            slab = jnp.where((plane == at) & (place == slot), b, slab)
    return slab


def gather_line(factor, count):
    if count != 4:
        line = [factor]
        for step in range(1, count):
            line.append(lax.ppermute(factor, "col", [(partner(b, step, count), b) for b in range(count)]))
        return line
    far = lax.ppermute(factor, "col", [(b ^ 2, b) for b in range(count)])
    near = lax.ppermute(factor, "col", [(b ^ 1, b) for b in range(count)])
    both = lax.ppermute(far, "col", [(b ^ 1, b) for b in range(count)])
    return [factor, near, far, both]


def load_kernel(after_ref, lines_ref, share_ref, sem):
    rows = share_ref.shape[0]
    layer = lax.axis_index("layer")
    load = pltpu.make_async_copy(lines_ref.at[pl.ds(layer * rows, rows)], share_ref, sem)
    load.start()
    load.wait()


def load_share(after, lines, layers):
    rows = lines.shape[0] // layers
    return pl.pallas_call(
        load_kernel,
        out_shape=jax.ShapeDtypeStruct((rows, LANES), jnp.float32),
        in_specs=[pl.BlockSpec(memory_space=pl.ANY), pl.BlockSpec(memory_space=pltpu.HBM)],
        out_specs=pl.BlockSpec(memory_space=pltpu.VMEM),
        scratch_shapes=[pltpu.SemaphoreType.DMA],
        compiler_params=pltpu.CompilerParams(vmem_limit_bytes=LOAD_VMEM_BYTES),
        cost_estimate=pl.CostEstimate(flops=0, bytes_accessed=rows * LANES * 8, transcendentals=0),
        name="load_share",
    )(after, lines)


def update_kernel(pieces, layers, half, tile, tile_rows, col_tiles, *refs):
    row_refs = refs[:pieces]
    col_refs = refs[pieces : pieces * (1 + layers)]
    share_ref, out_ref, row_buf, col_buf, out_buf, out_sems = refs[pieces * (1 + layers) :]
    r, c, layer = (lax.axis_index(axis) for axis in AXES)
    slots = plane_slots(pieces)
    per_row = col_tiles * tile // LANES
    for step in range(pieces):
        row_at = pl.multiple_of(partner(c, step, pieces) * tile_rows, tile_rows)
        slab = slab_of(slots, c, partner(r, step, pieces))
        col_at = pl.multiple_of(slab * tile_rows, tile_rows)
        for k in range(half):
            row_buf[k, pl.ds(row_at, tile_rows), :] = row_refs[step][k]
        for shift in range(layers):
            owner = lax.rem(layer + shift, layers)
            for k in range(half):
                col_buf[owner * half + k, pl.ds(col_at, tile_rows), :] = col_refs[shift * pieces + step][k]
    chunks = half * (tile // CHUNK_ROWS)
    chunk_lines = CHUNK_ROWS * per_row
    stores = []
    for chunk in range(chunks):
        k, first_row = divmod(chunk * CHUNK_ROWS, tile)
        for j in range(col_tiles):
            update = lax.dot_general(
                row_buf[k, first_row : first_row + CHUNK_ROWS, :],
                col_buf[j],
                (((1,), (1,)), ((), ())),
                preferred_element_type=jnp.float32,
            )
            for part in range(tile // LANES):
                first = chunk * chunk_lines + j * (tile // LANES) + part
                at = pl.ds(first, CHUNK_ROWS, stride=per_row)
                out_buf[at, :] = share_ref[at, :] - update[:, part * LANES : (part + 1) * LANES]
        written = pl.ds(chunk * chunk_lines, chunk_lines)
        store = pltpu.make_async_copy(out_buf.at[written], out_ref.at[written], out_sems.at[chunk])
        store.start()
        stores.append(store)
    for store in stores:
        store.wait()


def update_trailing(row_pieces, col_pieces, share, half, layers, tile, col_tiles):
    pieces = len(row_pieces)
    tile_rows = row_pieces[0].shape[1]
    width = row_pieces[0].shape[2]

    def body(*refs):
        update_kernel(pieces, layers, half, tile, tile_rows, col_tiles, *refs)

    result = pl.pallas_call(
        body,
        out_shape=jax.ShapeDtypeStruct(share.shape, jnp.float32),
        in_specs=[pl.BlockSpec(memory_space=pltpu.VMEM)] * (pieces * (1 + layers) + 1),
        out_specs=pl.BlockSpec(memory_space=pltpu.HBM),
        scratch_shapes=[
            pltpu.VMEM((half, tile, width), jnp.bfloat16),
            pltpu.VMEM((half * layers, tile, width), jnp.bfloat16),
            pltpu.VMEM(share.shape, jnp.float32),
            pltpu.SemaphoreType.DMA((half * (tile // CHUNK_ROWS),)),
        ],
        compiler_params=pltpu.CompilerParams(vmem_limit_bytes=VMEM_BYTES),
        name="update",
    )(*row_pieces, *col_pieces, share)
    return result.reshape(half, 1, tile, col_tiles, 1, tile)


def per_device(trailing, panel, inverse_factor):
    layers = lax.axis_size("layer")
    count = lax.axis_size("row")
    row_tiles, _, tile, col_tiles, _, _ = trailing.shape
    half = row_tiles // layers
    slots = plane_slots(count)
    factor = make_factor(panel, inverse_factor, half)
    moved = lax.ppermute(
        factor, ("row", "col"), [(a * count + b, slots[a][b] * count + a) for a in range(count) for b in range(count)]
    )
    share = load_share(factor, trailing.reshape(-1, LANES), layers)
    loaded_factor, share = lax.optimization_barrier((factor, share))
    line = gather_line(loaded_factor, count)
    plane = [moved] + [None] * (count - 1)
    for step in reversed(range(1, count)):
        plane[step] = lax.ppermute(moved, "row", [(partner(a, step, count), a) for a in range(count)])
    others = []
    for shift in range(1, layers):
        pairs = [((l + shift) % layers, l) for l in range(layers)]
        others += [lax.ppermute(piece, "layer", pairs) for piece in plane]
    return update_trailing(line, plane + others, share, half, layers, tile, col_tiles)


def solution(mesh):
    assert mesh.shape["row"] == mesh.shape["col"]
    return jax.shard_map(
        per_device,
        mesh=mesh,
        in_specs=(P(None, "row", None, None, "col", None), P(None, "row", "col", None), P()),
        out_specs=P("layer", "row", None, None, "col", None),
        check_vma=False,
    )
```

```python
import jax
import jax.numpy as jnp
from jax import lax
from jax.experimental import pallas as pl
from jax.experimental.pallas import tpu as pltpu
from jax.sharding import PartitionSpec as P

LANES = 128
CHUNK_ROWS = 128
VMEM_BYTES = 24 * 1024 * 1024
LOAD_VMEM_BYTES = 52000 * 1024
FACTOR_VMEM_BYTES = 55040 * 1024
AXES = ("row", "col", "layer")


def factor_kernel(panel_ref, inverse_ref, factor_ref, panel_buf, inverse_buf, sems):
    half = factor_ref.shape[0]
    tile_rows = factor_ref.shape[1]
    width = factor_ref.shape[2]
    layer = lax.axis_index("layer")
    copies = [
        pltpu.make_async_copy(panel_ref.at[pl.ds(layer * half, half), 0], panel_buf, sems.at[0]),
        pltpu.make_async_copy(inverse_ref, inverse_buf, sems.at[1]),
    ]
    for copy in copies:
        copy.start()
    for copy in copies:
        copy.wait()
    product = lax.dot_general(
        panel_buf[...].reshape(half * tile_rows, width),
        inverse_buf[...],
        (((1,), (1,)), ((), ())),
        precision=lax.Precision.HIGHEST,
        preferred_element_type=jnp.float32,
    )
    factor_ref[...] = product.astype(jnp.bfloat16).reshape(factor_ref.shape)


def make_factor(panel, inverse_factor, half):
    _, _, tile_rows, width = panel.shape
    return pl.pallas_call(
        factor_kernel,
        out_shape=jax.ShapeDtypeStruct((half, tile_rows, width), jnp.bfloat16),
        in_specs=[pl.BlockSpec(memory_space=pltpu.HBM)] * 2,
        out_specs=pl.BlockSpec(memory_space=pltpu.VMEM),
        scratch_shapes=[
            pltpu.VMEM((half, tile_rows, width), jnp.float32),
            pltpu.VMEM((width, width), jnp.float32),
            pltpu.SemaphoreType.DMA((2,)),
        ],
        compiler_params=pltpu.CompilerParams(vmem_limit_bytes=FACTOR_VMEM_BYTES),
        name="factor",
    )(panel, inverse_factor)


def partner(index, step, count):
    return index ^ step if count & (count - 1) == 0 else (index + step) % count


def plane_slots(count):
    if count == 4:
        return ((1, 3, 2, 0), (0, 2, 1, 3), (2, 0, 3, 1), (3, 1, 0, 2))
    return tuple(tuple(count - 1 - b for b in range(count)) for _ in range(count))


def slab_of(slots, plane, place):
    slab = jnp.int32(0)
    for at, row in enumerate(slots):
        for b, slot in enumerate(row):
            slab = jnp.where((plane == at) & (place == slot), b, slab)
    return slab


def gather_line(factor, count):
    if count != 4:
        line = [factor]
        for step in range(1, count):
            line.append(lax.ppermute(factor, "col", [(partner(b, step, count), b) for b in range(count)]))
        return line
    far = lax.ppermute(factor, "col", [(b ^ 2, b) for b in range(count)])
    near = lax.ppermute(factor, "col", [(b ^ 1, b) for b in range(count)])
    return [factor, near, far]


def load_kernel(after_ref, lines_ref, share_ref, sem):
    rows = share_ref.shape[0]
    layer = lax.axis_index("layer")
    load = pltpu.make_async_copy(lines_ref.at[pl.ds(layer * rows, rows)], share_ref, sem)
    load.start()
    load.wait()


def load_share(after, lines, layers):
    rows = lines.shape[0] // layers
    return pl.pallas_call(
        load_kernel,
        out_shape=jax.ShapeDtypeStruct((rows, LANES), jnp.float32),
        in_specs=[pl.BlockSpec(memory_space=pl.ANY), pl.BlockSpec(memory_space=pltpu.HBM)],
        out_specs=pl.BlockSpec(memory_space=pltpu.VMEM),
        scratch_shapes=[pltpu.SemaphoreType.DMA],
        compiler_params=pltpu.CompilerParams(vmem_limit_bytes=LOAD_VMEM_BYTES),
        cost_estimate=pl.CostEstimate(flops=0, bytes_accessed=rows * LANES * 8, transcendentals=0),
        name="load_share",
    )(after, lines)


def update_kernel(pieces, layers, half, tile, tile_rows, col_tiles, *refs):
    row_refs = refs[:pieces]
    plane_refs = refs[pieces : pieces + layers]
    share_ref, out_ref, row_buf, col_buf, out_buf, out_sems = refs[pieces + layers :]
    r, c, layer = (lax.axis_index(axis) for axis in AXES)
    slots = plane_slots(pieces)
    per_row = col_tiles * tile // LANES
    for step in range(pieces):
        row_at = pl.multiple_of(partner(c, step, pieces) * tile_rows, tile_rows)
        slab = slab_of(slots, c, step)
        col_at = pl.multiple_of(slab * tile_rows, tile_rows)
        for k in range(half):
            row_buf[k, pl.ds(row_at, tile_rows), :] = row_refs[step][k]
        for shift in range(layers):
            owner = lax.rem(layer + shift, layers)
            for k in range(half):
                col_buf[owner * half + k, pl.ds(col_at, tile_rows), :] = plane_refs[shift][step, k]
    chunks = half * (tile // CHUNK_ROWS)
    chunk_lines = CHUNK_ROWS * per_row
    stores = []
    for chunk in range(chunks):
        k, first_row = divmod(chunk * CHUNK_ROWS, tile)
        for j in range(col_tiles):
            update = lax.dot_general(
                row_buf[k, first_row : first_row + CHUNK_ROWS, :],
                col_buf[j],
                (((1,), (1,)), ((), ())),
                preferred_element_type=jnp.float32,
            )
            for part in range(tile // LANES):
                first = chunk * chunk_lines + j * (tile // LANES) + part
                at = pl.ds(first, CHUNK_ROWS, stride=per_row)
                out_buf[at, :] = share_ref[at, :] - update[:, part * LANES : (part + 1) * LANES]
        written = pl.ds(chunk * chunk_lines, chunk_lines)
        store = pltpu.make_async_copy(out_buf.at[written], out_ref.at[written], out_sems.at[chunk])
        store.start()
        stores.append(store)
    for store in stores:
        store.wait()


def update_trailing(row_pieces, planes, share, half, layers, tile, col_tiles):
    pieces = len(row_pieces)
    tile_rows = row_pieces[0].shape[1]
    width = row_pieces[0].shape[2]

    def body(*refs):
        update_kernel(pieces, layers, half, tile, tile_rows, col_tiles, *refs)

    result = pl.pallas_call(
        body,
        out_shape=jax.ShapeDtypeStruct(share.shape, jnp.float32),
        in_specs=[pl.BlockSpec(memory_space=pltpu.VMEM)] * (pieces + layers + 1),
        out_specs=pl.BlockSpec(memory_space=pltpu.HBM),
        scratch_shapes=[
            pltpu.VMEM((half, tile, width), jnp.bfloat16),
            pltpu.VMEM((half * layers, tile, width), jnp.bfloat16),
            pltpu.VMEM(share.shape, jnp.float32),
            pltpu.SemaphoreType.DMA((half * (tile // CHUNK_ROWS),)),
        ],
        compiler_params=pltpu.CompilerParams(vmem_limit_bytes=VMEM_BYTES),
        name="update",
    )(*row_pieces, *planes, share)
    return result.reshape(half, 1, tile, col_tiles, 1, tile)


def per_device(trailing, panel, inverse_factor):
    layers = lax.axis_size("layer")
    count = lax.axis_size("row")
    row_tiles, _, tile, col_tiles, _, _ = trailing.shape
    half = row_tiles // layers
    slots = plane_slots(count)
    factor = make_factor(panel, inverse_factor, half)
    moved = lax.ppermute(
        factor, ("row", "col"), [(a * count + b, slots[a][b] * count + a) for a in range(count) for b in range(count)]
    )
    share = load_share(factor, trailing.reshape(-1, LANES), layers)
    loaded_factor, share = lax.optimization_barrier((factor, share))
    line = gather_line(loaded_factor, count)
    copies = jnp.broadcast_to(moved[None], (count,) + moved.shape)
    copies, share, line[1:3] = lax.optimization_barrier((copies, share, line[1:3]))
    if count == 4:
        line.append(lax.ppermute(line[2], "col", [(b ^ 1, b) for b in range(count)]))
    plane = lax.all_to_all(copies, "row", 0, 0)
    planes = [plane]
    for shift in range(1, layers):
        planes.append(lax.ppermute(plane, "layer", [((l + shift) % layers, l) for l in range(layers)]))
    return update_trailing(line, planes, share, half, layers, tile, col_tiles)


def solution(mesh):
    assert mesh.shape["row"] == mesh.shape["col"]
    return jax.shard_map(
        per_device,
        mesh=mesh,
        in_specs=(P(None, "row", None, None, "col", None), P(None, "row", "col", None), P()),
        out_specs=P("layer", "row", None, None, "col", None),
        check_vma=False,
    )
```

```python
import jax
import jax.numpy as jnp
from jax import lax
from jax.experimental import pallas as pl
from jax.experimental.pallas import tpu as pltpu
from jax.sharding import PartitionSpec as P

LANES = 128
CHUNK_ROWS = 128
VMEM_BYTES = 24 * 1024 * 1024
LOAD_VMEM_BYTES = 52000 * 1024
FACTOR_VMEM_BYTES = 55040 * 1024
AXES = ("row", "col", "layer")


def factor_kernel(panel_ref, inverse_ref, factor_ref, panel_buf, inverse_buf, sems):
    half = factor_ref.shape[0]
    tile_rows = factor_ref.shape[1]
    width = factor_ref.shape[2]
    layer = lax.axis_index("layer")
    copies = [
        pltpu.make_async_copy(panel_ref.at[pl.ds(layer * half, half), 0], panel_buf, sems.at[0]),
        pltpu.make_async_copy(inverse_ref, inverse_buf, sems.at[1]),
    ]
    for copy in copies:
        copy.start()
    for copy in copies:
        copy.wait()
    product = lax.dot_general(
        panel_buf[...].reshape(half * tile_rows, width),
        inverse_buf[...],
        (((1,), (1,)), ((), ())),
        precision=lax.Precision.HIGHEST,
        preferred_element_type=jnp.float32,
    )
    factor_ref[...] = product.astype(jnp.bfloat16).reshape(factor_ref.shape)


def make_factor(panel, inverse_factor, half):
    _, _, tile_rows, width = panel.shape
    return pl.pallas_call(
        factor_kernel,
        out_shape=jax.ShapeDtypeStruct((half, tile_rows, width), jnp.bfloat16),
        in_specs=[pl.BlockSpec(memory_space=pltpu.HBM)] * 2,
        out_specs=pl.BlockSpec(memory_space=pltpu.VMEM),
        scratch_shapes=[
            pltpu.VMEM((half, tile_rows, width), jnp.float32),
            pltpu.VMEM((width, width), jnp.float32),
            pltpu.SemaphoreType.DMA((2,)),
        ],
        compiler_params=pltpu.CompilerParams(vmem_limit_bytes=FACTOR_VMEM_BYTES),
        name="factor",
    )(panel, inverse_factor)


def partner(index, step, count):
    return index ^ step if count & (count - 1) == 0 else (index + step) % count


def plane_slots(count):
    if count == 4:
        return ((3, 1, 2, 0), (3, 2, 0, 1), (2, 3, 1, 0), (3, 1, 2, 0))
    return tuple(tuple(count - 1 - b for b in range(count)) for _ in range(count))


def slab_of(slots, plane, place):
    slab = jnp.int32(0)
    for at, row in enumerate(slots):
        for b, slot in enumerate(row):
            slab = jnp.where((plane == at) & (place == slot), b, slab)
    return slab


def gather_line(factor, count):
    if count != 4:
        line = [factor]
        for step in range(1, count):
            line.append(lax.ppermute(factor, "col", [(partner(b, step, count), b) for b in range(count)]))
        return line
    far = lax.ppermute(factor, "col", [(b ^ 2, b) for b in range(count)])
    near = lax.ppermute(factor, "col", [(b ^ 1, b) for b in range(count)])
    both = lax.ppermute(far, "col", [(b ^ 1, b) for b in range(count)])
    return [factor, near, far, both]


def load_kernel(after_ref, lines_ref, share_ref, sem):
    rows = share_ref.shape[0]
    layer = lax.axis_index("layer")
    load = pltpu.make_async_copy(lines_ref.at[pl.ds(layer * rows, rows)], share_ref, sem)
    load.start()
    load.wait()


def load_share(after, lines, layers):
    rows = lines.shape[0] // layers
    return pl.pallas_call(
        load_kernel,
        out_shape=jax.ShapeDtypeStruct((rows, LANES), jnp.float32),
        in_specs=[pl.BlockSpec(memory_space=pl.ANY), pl.BlockSpec(memory_space=pltpu.HBM)],
        out_specs=pl.BlockSpec(memory_space=pltpu.VMEM),
        scratch_shapes=[pltpu.SemaphoreType.DMA],
        compiler_params=pltpu.CompilerParams(vmem_limit_bytes=LOAD_VMEM_BYTES),
        cost_estimate=pl.CostEstimate(flops=0, bytes_accessed=rows * LANES * 8, transcendentals=0),
        name="load_share",
    )(after, lines)


def update_kernel(pieces, layers, half, tile, tile_rows, col_tiles, *refs):
    row_refs = refs[:pieces]
    col_refs = refs[pieces : pieces * (1 + layers)]
    share_ref, out_ref, row_buf, col_buf, out_buf, out_sems = refs[pieces * (1 + layers) :]
    r, c, layer = (lax.axis_index(axis) for axis in AXES)
    slots = plane_slots(pieces)
    per_row = col_tiles * tile // LANES
    for step in range(pieces):
        row_at = pl.multiple_of(partner(c, step, pieces) * tile_rows, tile_rows)
        slab = slab_of(slots, c, partner(r, step, pieces))
        col_at = pl.multiple_of(slab * tile_rows, tile_rows)
        for k in range(half):
            row_buf[k, pl.ds(row_at, tile_rows), :] = row_refs[step][k]
        for shift in range(layers):
            owner = lax.rem(layer + shift, layers)
            for k in range(half):
                col_buf[owner * half + k, pl.ds(col_at, tile_rows), :] = col_refs[shift * pieces + step][k]
    chunks = half * (tile // CHUNK_ROWS)
    chunk_lines = CHUNK_ROWS * per_row
    stores = []
    for chunk in range(chunks):
        k, first_row = divmod(chunk * CHUNK_ROWS, tile)
        update = lax.dot_general(
            row_buf[k, first_row : first_row + CHUNK_ROWS, :],
            col_buf[...].reshape(col_tiles * tile, -1),
            (((1,), (1,)), ((), ())),
            preferred_element_type=jnp.float32,
        )
        written = pl.ds(chunk * chunk_lines, chunk_lines)
        out_buf[written, :] = share_ref[written, :] - update.reshape(chunk_lines, LANES)
        store = pltpu.make_async_copy(out_buf.at[written], out_ref.at[written], out_sems.at[chunk])
        store.start()
        stores.append(store)
    for store in stores:
        store.wait()


def update_trailing(row_pieces, col_pieces, share, half, layers, tile, col_tiles):
    pieces = len(row_pieces)
    tile_rows = row_pieces[0].shape[1]
    width = row_pieces[0].shape[2]

    def body(*refs):
        update_kernel(pieces, layers, half, tile, tile_rows, col_tiles, *refs)

    result = pl.pallas_call(
        body,
        out_shape=jax.ShapeDtypeStruct(share.shape, jnp.float32),
        in_specs=[pl.BlockSpec(memory_space=pltpu.VMEM)] * (pieces * (1 + layers) + 1),
        out_specs=pl.BlockSpec(memory_space=pltpu.HBM),
        scratch_shapes=[
            pltpu.VMEM((half, tile, width), jnp.bfloat16),
            pltpu.VMEM((half * layers, tile, width), jnp.bfloat16),
            pltpu.VMEM(share.shape, jnp.float32),
            pltpu.SemaphoreType.DMA((half * (tile // CHUNK_ROWS),)),
        ],
        compiler_params=pltpu.CompilerParams(vmem_limit_bytes=VMEM_BYTES),
        name="update",
    )(*row_pieces, *col_pieces, share)
    return result.reshape(half, 1, tile, col_tiles, 1, tile)


def per_device(trailing, panel, inverse_factor):
    layers = lax.axis_size("layer")
    count = lax.axis_size("row")
    row_tiles, _, tile, col_tiles, _, _ = trailing.shape
    half = row_tiles // layers
    slots = plane_slots(count)
    factor = make_factor(panel, inverse_factor, half)
    moved = lax.ppermute(
        factor, ("row", "col"), [(a * count + b, slots[a][b] * count + a) for a in range(count) for b in range(count)]
    )
    share = load_share(factor, trailing.reshape(-1, LANES), layers)
    loaded_factor, share = lax.optimization_barrier((factor, share))
    line = gather_line(loaded_factor, count)
    plane = [moved] + [None] * (count - 1)
    for step in reversed(range(1, count)):
        plane[step] = lax.ppermute(moved, "row", [(partner(a, step, count), a) for a in range(count)])
    others = []
    for shift in range(1, layers):
        pairs = [((l + shift) % layers, l) for l in range(layers)]
        others += [lax.ppermute(piece, "layer", pairs) for piece in plane]
    return update_trailing(line, plane + others, share, half, layers, tile, col_tiles)


def solution(mesh):
    assert mesh.shape["row"] == mesh.shape["col"]
    return jax.shard_map(
        per_device,
        mesh=mesh,
        in_specs=(P(None, "row", None, None, "col", None), P(None, "row", "col", None), P()),
        out_specs=P("layer", "row", None, None, "col", None),
        check_vma=False,
    )
```

```python
import jax
import jax.numpy as jnp
from jax import lax
from jax.experimental import pallas as pl
from jax.experimental.pallas import tpu as pltpu
from jax.sharding import PartitionSpec as P

LANES = 128
CHUNK_ROWS = 128
LOADS = 8
VMEM_BYTES = 24 * 1024 * 1024
LOAD_VMEM_BYTES = 52000 * 1024
FACTOR_VMEM_BYTES = 55040 * 1024
AXES = ("row", "col", "layer")


def factor_kernel(panel_ref, inverse_ref, factor_ref, panel_buf, inverse_buf, sems):
    half = factor_ref.shape[0]
    tile_rows = factor_ref.shape[1]
    width = factor_ref.shape[2]
    layer = lax.axis_index("layer")
    copies = [
        pltpu.make_async_copy(panel_ref.at[pl.ds(layer * half, half), 0], panel_buf, sems.at[0]),
        pltpu.make_async_copy(inverse_ref, inverse_buf, sems.at[1]),
    ]
    for copy in copies:
        copy.start()
    for copy in copies:
        copy.wait()
    product = lax.dot_general(
        panel_buf[...].reshape(half * tile_rows, width),
        inverse_buf[...],
        (((1,), (1,)), ((), ())),
        precision=lax.Precision.HIGHEST,
        preferred_element_type=jnp.float32,
    )
    factor_ref[...] = product.astype(jnp.bfloat16).reshape(factor_ref.shape)


def make_factor(panel, inverse_factor, half):
    _, _, tile_rows, width = panel.shape
    return pl.pallas_call(
        factor_kernel,
        out_shape=jax.ShapeDtypeStruct((half, tile_rows, width), jnp.bfloat16),
        in_specs=[pl.BlockSpec(memory_space=pltpu.HBM)] * 2,
        out_specs=pl.BlockSpec(memory_space=pltpu.VMEM),
        scratch_shapes=[
            pltpu.VMEM((half, tile_rows, width), jnp.float32),
            pltpu.VMEM((width, width), jnp.float32),
            pltpu.SemaphoreType.DMA((2,)),
        ],
        compiler_params=pltpu.CompilerParams(vmem_limit_bytes=FACTOR_VMEM_BYTES),
        name="factor",
    )(panel, inverse_factor)


def partner(index, step, count):
    return index ^ step if count & (count - 1) == 0 else (index + step) % count


def plane_slots(count):
    if count == 4:
        return ((3, 1, 2, 0), (3, 2, 0, 1), (2, 3, 1, 0), (3, 1, 2, 0))
    return tuple(tuple(count - 1 - b for b in range(count)) for _ in range(count))


def slab_of(slots, plane, place):
    slab = jnp.int32(0)
    for at, row in enumerate(slots):
        for b, slot in enumerate(row):
            slab = jnp.where((plane == at) & (place == slot), b, slab)
    return slab


def gather_line(factor, count):
    if count != 4:
        line = [factor]
        for step in range(1, count):
            line.append(lax.ppermute(factor, "col", [(partner(b, step, count), b) for b in range(count)]))
        return line
    far = lax.ppermute(factor, "col", [(b ^ 2, b) for b in range(count)])
    near = lax.ppermute(factor, "col", [(b ^ 1, b) for b in range(count)])
    both = lax.ppermute(far, "col", [(b ^ 1, b) for b in range(count)])
    return [factor, near, far, both]


def load_kernel(after_ref, lines_ref, share_ref, sems):
    rows = share_ref.shape[0]
    part = rows // LOADS
    layer = lax.axis_index("layer")
    loads = [
        pltpu.make_async_copy(
            lines_ref.at[pl.ds(layer * rows + i * part, part)], share_ref.at[pl.ds(i * part, part)], sems.at[i]
        )
        for i in range(LOADS)
    ]
    for load in loads:
        load.start()
    for load in loads:
        load.wait()


def load_share(after, lines, layers):
    rows = lines.shape[0] // layers
    return pl.pallas_call(
        load_kernel,
        out_shape=jax.ShapeDtypeStruct((rows, LANES), jnp.float32),
        in_specs=[pl.BlockSpec(memory_space=pl.ANY), pl.BlockSpec(memory_space=pltpu.HBM)],
        out_specs=pl.BlockSpec(memory_space=pltpu.VMEM),
        scratch_shapes=[pltpu.SemaphoreType.DMA((LOADS,))],
        compiler_params=pltpu.CompilerParams(vmem_limit_bytes=LOAD_VMEM_BYTES),
        cost_estimate=pl.CostEstimate(flops=0, bytes_accessed=rows * LANES * 8, transcendentals=0),
        name="load_share",
    )(after, lines)


def update_kernel(pieces, layers, half, tile, tile_rows, col_tiles, *refs):
    row_refs = refs[:pieces]
    col_refs = refs[pieces : pieces * (1 + layers)]
    share_ref, out_ref, row_buf, col_buf, out_buf, out_sems = refs[pieces * (1 + layers) :]
    r, c, layer = (lax.axis_index(axis) for axis in AXES)
    slots = plane_slots(pieces)
    per_row = col_tiles * tile // LANES
    for step in range(pieces):
        row_at = pl.multiple_of(partner(c, step, pieces) * tile_rows, tile_rows)
        slab = slab_of(slots, c, partner(r, step, pieces))
        col_at = pl.multiple_of(slab * tile_rows, tile_rows)
        for k in range(half):
            row_buf[k, pl.ds(row_at, tile_rows), :] = row_refs[step][k]
        for shift in range(layers):
            owner = lax.rem(layer + shift, layers)
            for k in range(half):
                col_buf[owner * half + k, pl.ds(col_at, tile_rows), :] = col_refs[shift * pieces + step][k]
    chunks = half * (tile // CHUNK_ROWS)
    chunk_lines = CHUNK_ROWS * per_row
    stores = []
    for chunk in range(chunks):
        k, first_row = divmod(chunk * CHUNK_ROWS, tile)
        update = lax.dot_general(
            row_buf[k, first_row : first_row + CHUNK_ROWS, :],
            col_buf[...].reshape(col_tiles * tile, -1),
            (((1,), (1,)), ((), ())),
            preferred_element_type=jnp.float32,
        )
        written = pl.ds(chunk * chunk_lines, chunk_lines)
        out_buf[written, :] = share_ref[written, :] - update.reshape(chunk_lines, LANES)
        store = pltpu.make_async_copy(out_buf.at[written], out_ref.at[written], out_sems.at[chunk])
        store.start()
        stores.append(store)
    for store in stores:
        store.wait()


def update_trailing(row_pieces, col_pieces, share, half, layers, tile, col_tiles):
    pieces = len(row_pieces)
    tile_rows = row_pieces[0].shape[1]
    width = row_pieces[0].shape[2]

    def body(*refs):
        update_kernel(pieces, layers, half, tile, tile_rows, col_tiles, *refs)

    result = pl.pallas_call(
        body,
        out_shape=jax.ShapeDtypeStruct(share.shape, jnp.float32),
        in_specs=[pl.BlockSpec(memory_space=pltpu.VMEM)] * (pieces * (1 + layers) + 1),
        out_specs=pl.BlockSpec(memory_space=pltpu.HBM),
        scratch_shapes=[
            pltpu.VMEM((half, tile, width), jnp.bfloat16),
            pltpu.VMEM((half * layers, tile, width), jnp.bfloat16),
            pltpu.VMEM(share.shape, jnp.float32),
            pltpu.SemaphoreType.DMA((half * (tile // CHUNK_ROWS),)),
        ],
        compiler_params=pltpu.CompilerParams(vmem_limit_bytes=VMEM_BYTES),
        name="update",
    )(*row_pieces, *col_pieces, share)
    return result.reshape(half, 1, tile, col_tiles, 1, tile)


def per_device(trailing, panel, inverse_factor):
    layers = lax.axis_size("layer")
    count = lax.axis_size("row")
    row_tiles, _, tile, col_tiles, _, _ = trailing.shape
    half = row_tiles // layers
    slots = plane_slots(count)
    factor = make_factor(panel, inverse_factor, half)
    moved = lax.ppermute(
        factor, ("row", "col"), [(a * count + b, slots[a][b] * count + a) for a in range(count) for b in range(count)]
    )
    share = load_share(factor, trailing.reshape(-1, LANES), layers)
    loaded_factor, share = lax.optimization_barrier((factor, share))
    line = gather_line(loaded_factor, count)
    plane = [moved] + [None] * (count - 1)
    for step in (count - 1, *range(1, count - 1)):
        plane[step] = lax.ppermute(moved, "row", [(partner(a, step, count), a) for a in range(count)])
    others = []
    for shift in range(1, layers):
        pairs = [((l + shift) % layers, l) for l in range(layers)]
        others += [lax.ppermute(piece, "layer", pairs) for piece in plane]
    return update_trailing(line, plane + others, share, half, layers, tile, col_tiles)


def solution(mesh):
    assert mesh.shape["row"] == mesh.shape["col"]
    return jax.shard_map(
        per_device,
        mesh=mesh,
        in_specs=(P(None, "row", None, None, "col", None), P(None, "row", "col", None), P()),
        out_specs=P("layer", "row", None, None, "col", None),
        check_vma=False,
    )
```

```python
import jax
import jax.numpy as jnp
from jax import lax
from jax.experimental import pallas as pl
from jax.experimental.pallas import tpu as pltpu
from jax.sharding import PartitionSpec as P

LANES = 128
CHUNK_ROWS = 128
VMEM_BYTES = 24 * 1024 * 1024
LOAD_VMEM_BYTES = 52000 * 1024
FACTOR_VMEM_BYTES = 55040 * 1024
AXES = ("row", "col", "layer")


def factor_kernel(panel_ref, inverse_ref, factor_ref, panel_buf, inverse_buf, sems):
    half = factor_ref.shape[0]
    tile_rows = factor_ref.shape[1]
    width = factor_ref.shape[2]
    layer = lax.axis_index("layer")
    copies = [
        pltpu.make_async_copy(panel_ref.at[pl.ds(layer * half, half), 0], panel_buf, sems.at[0]),
        pltpu.make_async_copy(inverse_ref, inverse_buf, sems.at[1]),
    ]
    for copy in copies:
        copy.start()
    for copy in copies:
        copy.wait()
    product = lax.dot_general(
        panel_buf[...].reshape(half * tile_rows, width),
        inverse_buf[...],
        (((1,), (1,)), ((), ())),
        precision=lax.Precision.HIGHEST,
        preferred_element_type=jnp.float32,
    )
    factor_ref[...] = product.astype(jnp.bfloat16).reshape(factor_ref.shape)


def make_factor(panel, inverse_factor, half):
    _, _, tile_rows, width = panel.shape
    return pl.pallas_call(
        factor_kernel,
        out_shape=jax.ShapeDtypeStruct((half, tile_rows, width), jnp.bfloat16),
        in_specs=[pl.BlockSpec(memory_space=pltpu.HBM)] * 2,
        out_specs=pl.BlockSpec(memory_space=pltpu.VMEM),
        scratch_shapes=[
            pltpu.VMEM((half, tile_rows, width), jnp.float32),
            pltpu.VMEM((width, width), jnp.float32),
            pltpu.SemaphoreType.DMA((2,)),
        ],
        compiler_params=pltpu.CompilerParams(vmem_limit_bytes=FACTOR_VMEM_BYTES),
        name="factor",
    )(panel, inverse_factor)


def partner(index, step, count):
    return index ^ step if count & (count - 1) == 0 else (index + step) % count


def plane_slots(count):
    if count == 4:
        return ((3, 1, 2, 0), (3, 2, 0, 1), (2, 3, 1, 0), (3, 1, 2, 0))
    return tuple(tuple(count - 1 - b for b in range(count)) for _ in range(count))


def plane_steps(count):
    return (0, 2, 1, 3) if count == 4 else tuple(range(count))


def slab_of(slots, plane, place):
    slab = jnp.int32(0)
    for at, row in enumerate(slots):
        for b, slot in enumerate(row):
            slab = jnp.where((plane == at) & (place == slot), b, slab)
    return slab


def gather_line(factor, count):
    if count != 4:
        line = [factor]
        for step in range(1, count):
            line.append(lax.ppermute(factor, "col", [(partner(b, step, count), b) for b in range(count)]))
        return line
    far = lax.ppermute(factor, "col", [(b ^ 2, b) for b in range(count)])
    near = lax.ppermute(factor, "col", [(b ^ 1, b) for b in range(count)])
    both = lax.ppermute(far, "col", [(b ^ 1, b) for b in range(count)])
    return [factor, near, far, both]


def load_kernel(after_ref, lines_ref, share_ref, sem):
    rows = share_ref.shape[0]
    layer = lax.axis_index("layer")
    load = pltpu.make_async_copy(lines_ref.at[pl.ds(layer * rows, rows)], share_ref, sem)
    load.start()
    load.wait()


def load_share(after, lines, layers):
    rows = lines.shape[0] // layers
    return pl.pallas_call(
        load_kernel,
        out_shape=jax.ShapeDtypeStruct((rows, LANES), jnp.float32),
        in_specs=[pl.BlockSpec(memory_space=pl.ANY), pl.BlockSpec(memory_space=pltpu.HBM)],
        out_specs=pl.BlockSpec(memory_space=pltpu.VMEM),
        scratch_shapes=[pltpu.SemaphoreType.DMA],
        compiler_params=pltpu.CompilerParams(vmem_limit_bytes=LOAD_VMEM_BYTES),
        cost_estimate=pl.CostEstimate(flops=0, bytes_accessed=rows * LANES * 8, transcendentals=0),
        name="load_share",
    )(after, lines)


def update_kernel(pieces, layers, half, tile, tile_rows, col_tiles, *refs):
    row_refs = refs[:pieces]
    col_refs = refs[pieces : pieces * (1 + layers)]
    share_ref, out_ref, row_buf, col_buf, out_buf, out_sems = refs[pieces * (1 + layers) :]
    r, c, layer = (lax.axis_index(axis) for axis in AXES)
    slots = plane_slots(pieces)
    per_row = col_tiles * tile // LANES
    for step, plane_step in enumerate(plane_steps(pieces)):
        row_at = pl.multiple_of(partner(c, step, pieces) * tile_rows, tile_rows)
        slab = slab_of(slots, c, partner(r, plane_step, pieces))
        col_at = pl.multiple_of(slab * tile_rows, tile_rows)
        for k in range(half):
            row_buf[k, pl.ds(row_at, tile_rows), :] = row_refs[step][k]
        for shift in range(layers):
            owner = lax.rem(layer + shift, layers)
            for k in range(half):
                col_buf[owner * half + k, pl.ds(col_at, tile_rows), :] = col_refs[shift * pieces + step][k]
    chunks = half * (tile // CHUNK_ROWS)
    chunk_lines = CHUNK_ROWS * per_row
    stores = []
    for chunk in range(chunks):
        k, first_row = divmod(chunk * CHUNK_ROWS, tile)
        update = lax.dot_general(
            row_buf[k, first_row : first_row + CHUNK_ROWS, :],
            col_buf[...].reshape(col_tiles * tile, -1),
            (((1,), (1,)), ((), ())),
            preferred_element_type=jnp.float32,
        )
        written = pl.ds(chunk * chunk_lines, chunk_lines)
        out_buf[written, :] = share_ref[written, :] - update.reshape(chunk_lines, LANES)
        store = pltpu.make_async_copy(out_buf.at[written], out_ref.at[written], out_sems.at[chunk])
        store.start()
        stores.append(store)
    for store in stores:
        store.wait()


def update_trailing(row_pieces, col_pieces, share, half, layers, tile, col_tiles):
    pieces = len(row_pieces)
    tile_rows = row_pieces[0].shape[1]
    width = row_pieces[0].shape[2]

    def body(*refs):
        update_kernel(pieces, layers, half, tile, tile_rows, col_tiles, *refs)

    result = pl.pallas_call(
        body,
        out_shape=jax.ShapeDtypeStruct(share.shape, jnp.float32),
        in_specs=[pl.BlockSpec(memory_space=pltpu.VMEM)] * (pieces * (1 + layers) + 1),
        out_specs=pl.BlockSpec(memory_space=pltpu.HBM),
        scratch_shapes=[
            pltpu.VMEM((half, tile, width), jnp.bfloat16),
            pltpu.VMEM((half * layers, tile, width), jnp.bfloat16),
            pltpu.VMEM(share.shape, jnp.float32),
            pltpu.SemaphoreType.DMA((half * (tile // CHUNK_ROWS),)),
        ],
        compiler_params=pltpu.CompilerParams(vmem_limit_bytes=VMEM_BYTES),
        name="update",
    )(*row_pieces, *col_pieces, share)
    return result.reshape(half, 1, tile, col_tiles, 1, tile)


def per_device(trailing, panel, inverse_factor):
    layers = lax.axis_size("layer")
    count = lax.axis_size("row")
    row_tiles, _, tile, col_tiles, _, _ = trailing.shape
    half = row_tiles // layers
    slots = plane_slots(count)
    factor = make_factor(panel, inverse_factor, half)
    moved = lax.ppermute(
        factor, ("row", "col"), [(a * count + b, slots[a][b] * count + a) for a in range(count) for b in range(count)]
    )
    share = load_share(factor, trailing.reshape(-1, LANES), layers)
    loaded_factor, share = lax.optimization_barrier((factor, share))
    line = gather_line(loaded_factor, count)
    plane = [moved]
    for step in plane_steps(count)[1:]:
        plane.append(lax.ppermute(moved, "row", [(partner(a, step, count), a) for a in range(count)]))
    others = []
    for shift in range(1, layers):
        pairs = [((l + shift) % layers, l) for l in range(layers)]
        others += [lax.ppermute(piece, "layer", pairs) for piece in plane]
    return update_trailing(line, plane + others, share, half, layers, tile, col_tiles)


def solution(mesh):
    assert mesh.shape["row"] == mesh.shape["col"]
    return jax.shard_map(
        per_device,
        mesh=mesh,
        in_specs=(P(None, "row", None, None, "col", None), P(None, "row", "col", None), P()),
        out_specs=P("layer", "row", None, None, "col", None),
        check_vma=False,
    )
```

```python
import jax
import jax.numpy as jnp
from jax import lax
from jax.experimental import pallas as pl
from jax.experimental.pallas import tpu as pltpu
from jax.sharding import PartitionSpec as P

LANES = 128
CHUNK_ROWS = 128
VMEM_BYTES = 24 * 1024 * 1024
LOAD_VMEM_BYTES = 52000 * 1024
FACTOR_VMEM_BYTES = 55040 * 1024
AXES = ("row", "col", "layer")


def factor_kernel(panel_ref, inverse_ref, factor_ref, panel_buf, inverse_buf, sems):
    half = factor_ref.shape[0]
    tile_rows = factor_ref.shape[1]
    width = factor_ref.shape[2]
    layer = lax.axis_index("layer")
    copies = [
        pltpu.make_async_copy(panel_ref.at[pl.ds(layer * half, half), 0], panel_buf, sems.at[0]),
        pltpu.make_async_copy(inverse_ref, inverse_buf, sems.at[1]),
    ]
    for copy in copies:
        copy.start()
    for copy in copies:
        copy.wait()
    product = lax.dot_general(
        panel_buf[...].reshape(half * tile_rows, width),
        inverse_buf[...],
        (((1,), (1,)), ((), ())),
        precision=lax.Precision.HIGHEST,
        preferred_element_type=jnp.float32,
    )
    factor_ref[...] = product.astype(jnp.bfloat16).reshape(factor_ref.shape)


def make_factor(panel, inverse_factor, half):
    _, _, tile_rows, width = panel.shape
    return pl.pallas_call(
        factor_kernel,
        out_shape=jax.ShapeDtypeStruct((half, tile_rows, width), jnp.bfloat16),
        in_specs=[pl.BlockSpec(memory_space=pltpu.HBM)] * 2,
        out_specs=pl.BlockSpec(memory_space=pltpu.VMEM),
        scratch_shapes=[
            pltpu.VMEM((half, tile_rows, width), jnp.float32),
            pltpu.VMEM((width, width), jnp.float32),
            pltpu.SemaphoreType.DMA((2,)),
        ],
        compiler_params=pltpu.CompilerParams(vmem_limit_bytes=FACTOR_VMEM_BYTES),
        name="factor",
    )(panel, inverse_factor)


def partner(index, step, count):
    return index ^ step if count & (count - 1) == 0 else (index + step) % count


def plane_slots(count):
    if count == 4:
        return ((3, 1, 2, 0), (3, 2, 0, 1), (2, 3, 1, 0), (3, 1, 2, 0))
    return tuple(tuple(count - 1 - b for b in range(count)) for _ in range(count))


def plane_mates(count, layer):
    if count == 4:
        return (0, 2, 1, 3) if layer % 2 == 0 else (0, 1, 2, 3)
    return tuple(range(count))


def slab_of(slots, plane, place):
    slab = jnp.int32(0)
    for at, row in enumerate(slots):
        for b, slot in enumerate(row):
            slab = jnp.where((plane == at) & (place == slot), b, slab)
    return slab


def gather_line(factor, count):
    if count != 4:
        line = [factor]
        for step in range(1, count):
            line.append(lax.ppermute(factor, "col", [(partner(b, step, count), b) for b in range(count)]))
        return line
    far = lax.ppermute(factor, "col", [(b ^ 2, b) for b in range(count)])
    near = lax.ppermute(factor, "col", [(b ^ 1, b) for b in range(count)])
    both = lax.ppermute(far, "col", [(b ^ 1, b) for b in range(count)])
    return [factor, near, far, both]


def load_kernel(after_ref, lines_ref, share_ref, sem):
    rows = share_ref.shape[0]
    layer = lax.axis_index("layer")
    load = pltpu.make_async_copy(lines_ref.at[pl.ds(layer * rows, rows)], share_ref, sem)
    load.start()
    load.wait()


def load_share(after, lines, layers):
    rows = lines.shape[0] // layers
    return pl.pallas_call(
        load_kernel,
        out_shape=jax.ShapeDtypeStruct((rows, LANES), jnp.float32),
        in_specs=[pl.BlockSpec(memory_space=pl.ANY), pl.BlockSpec(memory_space=pltpu.HBM)],
        out_specs=pl.BlockSpec(memory_space=pltpu.VMEM),
        scratch_shapes=[pltpu.SemaphoreType.DMA],
        compiler_params=pltpu.CompilerParams(vmem_limit_bytes=LOAD_VMEM_BYTES),
        cost_estimate=pl.CostEstimate(flops=0, bytes_accessed=rows * LANES * 8, transcendentals=0),
        name="load_share",
    )(after, lines)


def update_kernel(pieces, layers, half, tile, tile_rows, col_tiles, *refs):
    row_refs = refs[:pieces]
    col_refs = refs[pieces : pieces * (1 + layers)]
    share_ref, out_ref, row_buf, col_buf, out_buf, out_sems = refs[pieces * (1 + layers) :]
    r, c, layer = (lax.axis_index(axis) for axis in AXES)
    slots = plane_slots(pieces)
    per_row = col_tiles * tile // LANES
    mates = [plane_mates(pieces, l) for l in range(layers)]
    for step in range(pieces):
        row_at = pl.multiple_of(partner(c, step, pieces) * tile_rows, tile_rows)
        for k in range(half):
            row_buf[k, pl.ds(row_at, tile_rows), :] = row_refs[step][k]
        for shift in range(layers):
            owner = lax.rem(layer + shift, layers)
            mate = jnp.int32(mates[0][step])
            for l in range(1, layers):
                mate = jnp.where(owner == l, mates[l][step], mate)
            slab = slab_of(slots, c, partner(r, mate, pieces))
            col_at = pl.multiple_of(slab * tile_rows, tile_rows)
            for k in range(half):
                col_buf[owner * half + k, pl.ds(col_at, tile_rows), :] = col_refs[shift * pieces + step][k]
    chunks = half * (tile // CHUNK_ROWS)
    chunk_lines = CHUNK_ROWS * per_row
    stores = []
    for chunk in range(chunks):
        k, first_row = divmod(chunk * CHUNK_ROWS, tile)
        update = lax.dot_general(
            row_buf[k, first_row : first_row + CHUNK_ROWS, :],
            col_buf[...].reshape(col_tiles * tile, -1),
            (((1,), (1,)), ((), ())),
            preferred_element_type=jnp.float32,
        )
        written = pl.ds(chunk * chunk_lines, chunk_lines)
        out_buf[written, :] = share_ref[written, :] - update.reshape(chunk_lines, LANES)
        store = pltpu.make_async_copy(out_buf.at[written], out_ref.at[written], out_sems.at[chunk])
        store.start()
        stores.append(store)
    for store in stores:
        store.wait()


def update_trailing(row_pieces, col_pieces, share, half, layers, tile, col_tiles):
    pieces = len(row_pieces)
    tile_rows = row_pieces[0].shape[1]
    width = row_pieces[0].shape[2]

    def body(*refs):
        update_kernel(pieces, layers, half, tile, tile_rows, col_tiles, *refs)

    result = pl.pallas_call(
        body,
        out_shape=jax.ShapeDtypeStruct(share.shape, jnp.float32),
        in_specs=[pl.BlockSpec(memory_space=pltpu.VMEM)] * (pieces * (1 + layers) + 1),
        out_specs=pl.BlockSpec(memory_space=pltpu.HBM),
        scratch_shapes=[
            pltpu.VMEM((half, tile, width), jnp.bfloat16),
            pltpu.VMEM((half * layers, tile, width), jnp.bfloat16),
            pltpu.VMEM(share.shape, jnp.float32),
            pltpu.SemaphoreType.DMA((half * (tile // CHUNK_ROWS),)),
        ],
        compiler_params=pltpu.CompilerParams(vmem_limit_bytes=VMEM_BYTES),
        name="update",
    )(*row_pieces, *col_pieces, share)
    return result.reshape(half, 1, tile, col_tiles, 1, tile)


def per_device(trailing, panel, inverse_factor):
    layers = lax.axis_size("layer")
    count = lax.axis_size("row")
    row_tiles, _, tile, col_tiles, _, _ = trailing.shape
    half = row_tiles // layers
    slots = plane_slots(count)
    factor = make_factor(panel, inverse_factor, half)
    moved = lax.ppermute(
        factor, ("row", "col"), [(a * count + b, slots[a][b] * count + a) for a in range(count) for b in range(count)]
    )
    share = load_share(factor, trailing.reshape(-1, LANES), layers)
    loaded_factor, share = lax.optimization_barrier((factor, share))
    line = gather_line(loaded_factor, count)
    plane = [moved]
    for step in range(1, count):
        pairs = [
            (partner(a, plane_mates(count, l)[step], count) * layers + l, a * layers + l)
            for a in range(count)
            for l in range(layers)
        ]
        plane.append(lax.ppermute(moved, ("row", "layer"), pairs))
    others = []
    for shift in range(1, layers):
        pairs = [((l + shift) % layers, l) for l in range(layers)]
        others += [lax.ppermute(piece, "layer", pairs) for piece in plane]
    return update_trailing(line, plane + others, share, half, layers, tile, col_tiles)


def solution(mesh):
    assert mesh.shape["row"] == mesh.shape["col"]
    return jax.shard_map(
        per_device,
        mesh=mesh,
        in_specs=(P(None, "row", None, None, "col", None), P(None, "row", "col", None), P()),
        out_specs=P("layer", "row", None, None, "col", None),
        check_vma=False,
    )
```

```python
import jax
import jax.numpy as jnp
from jax import lax
from jax.experimental import pallas as pl
from jax.experimental.pallas import tpu as pltpu
from jax.sharding import PartitionSpec as P

LANES = 128
CHUNK_ROWS = 128
VMEM_BYTES = 24 * 1024 * 1024
LOAD_VMEM_BYTES = 52000 * 1024
FACTOR_VMEM_BYTES = 55040 * 1024
AXES = ("row", "col", "layer")


def factor_kernel(panel_ref, inverse_ref, factor_ref, panel_buf, inverse_buf, sems):
    half = factor_ref.shape[0]
    tile_rows = factor_ref.shape[1]
    width = factor_ref.shape[2]
    layer = lax.axis_index("layer")
    copies = [
        pltpu.make_async_copy(panel_ref.at[pl.ds(layer * half, half), 0], panel_buf, sems.at[0]),
        pltpu.make_async_copy(inverse_ref, inverse_buf, sems.at[1]),
    ]
    for copy in copies:
        copy.start()
    for copy in copies:
        copy.wait()
    product = lax.dot_general(
        panel_buf[...].reshape(half * tile_rows, width),
        inverse_buf[...],
        (((1,), (1,)), ((), ())),
        precision=lax.Precision.HIGHEST,
        preferred_element_type=jnp.float32,
    )
    factor_ref[...] = product.astype(jnp.bfloat16).reshape(factor_ref.shape)


def make_factor(panel, inverse_factor, half):
    _, _, tile_rows, width = panel.shape
    return pl.pallas_call(
        factor_kernel,
        out_shape=jax.ShapeDtypeStruct((half, tile_rows, width), jnp.bfloat16),
        in_specs=[pl.BlockSpec(memory_space=pltpu.HBM)] * 2,
        out_specs=pl.BlockSpec(memory_space=pltpu.VMEM),
        scratch_shapes=[
            pltpu.VMEM((half, tile_rows, width), jnp.float32),
            pltpu.VMEM((width, width), jnp.float32),
            pltpu.SemaphoreType.DMA((2,)),
        ],
        compiler_params=pltpu.CompilerParams(vmem_limit_bytes=FACTOR_VMEM_BYTES),
        name="factor",
    )(panel, inverse_factor)


def partner(index, step, count):
    return index ^ step if count & (count - 1) == 0 else (index + step) % count


def plane_slots(count):
    if count == 4:
        return ((3, 0, 1, 2), (3, 2, 1, 0), (0, 2, 1, 3), (3, 1, 2, 0))
    return tuple(tuple(count - 1 - b for b in range(count)) for _ in range(count))


def plane_steps(count):
    return (0, 2, 1, 3) if count == 4 else tuple(range(count))


def slab_of(slots, plane, place):
    slab = jnp.int32(0)
    for at, row in enumerate(slots):
        for b, slot in enumerate(row):
            slab = jnp.where((plane == at) & (place == slot), b, slab)
    return slab


def gather_line(factor, count):
    if count != 4:
        line = [factor]
        for step in range(1, count):
            line.append(lax.ppermute(factor, "col", [(partner(b, step, count), b) for b in range(count)]))
        return line
    far = lax.ppermute(factor, "col", [(b ^ 2, b) for b in range(count)])
    near = lax.ppermute(factor, "col", [(b ^ 1, b) for b in range(count)])
    both = lax.ppermute(far, "col", [(b ^ 1, b) for b in range(count)])
    return [factor, near, far, both]


def load_kernel(after_ref, lines_ref, share_ref, sem):
    rows = share_ref.shape[0]
    layer = lax.axis_index("layer")
    load = pltpu.make_async_copy(lines_ref.at[pl.ds(layer * rows, rows)], share_ref, sem)
    load.start()
    load.wait()


def load_share(after, lines, layers):
    rows = lines.shape[0] // layers
    return pl.pallas_call(
        load_kernel,
        out_shape=jax.ShapeDtypeStruct((rows, LANES), jnp.float32),
        in_specs=[pl.BlockSpec(memory_space=pl.ANY), pl.BlockSpec(memory_space=pltpu.HBM)],
        out_specs=pl.BlockSpec(memory_space=pltpu.VMEM),
        scratch_shapes=[pltpu.SemaphoreType.DMA],
        compiler_params=pltpu.CompilerParams(vmem_limit_bytes=LOAD_VMEM_BYTES),
        cost_estimate=pl.CostEstimate(flops=0, bytes_accessed=rows * LANES * 8, transcendentals=0),
        name="load_share",
    )(after, lines)


def update_kernel(pieces, layers, half, tile, tile_rows, col_tiles, *refs):
    col_refs = refs[: pieces * layers]
    row_refs = refs[pieces * layers : pieces * (1 + layers)]
    share_ref, out_ref, row_buf, col_buf, out_buf, out_sems = refs[pieces * (1 + layers) :]
    r, c, layer = (lax.axis_index(axis) for axis in AXES)
    slots = plane_slots(pieces)
    per_row = col_tiles * tile // LANES
    for step, plane_step in enumerate(plane_steps(pieces)):
        row_at = pl.multiple_of(partner(c, step, pieces) * tile_rows, tile_rows)
        slab = slab_of(slots, c, partner(r, plane_step, pieces))
        col_at = pl.multiple_of(slab * tile_rows, tile_rows)
        for k in range(half):
            row_buf[k, pl.ds(row_at, tile_rows), :] = row_refs[step][k]
        for shift in range(layers):
            owner = lax.rem(layer + shift, layers)
            for k in range(half):
                col_buf[owner * half + k, pl.ds(col_at, tile_rows), :] = col_refs[shift * pieces + step][k]
    chunks = half * (tile // CHUNK_ROWS)
    chunk_lines = CHUNK_ROWS * per_row
    stores = []
    for chunk in range(chunks):
        k, first_row = divmod(chunk * CHUNK_ROWS, tile)
        update = lax.dot_general(
            row_buf[k, first_row : first_row + CHUNK_ROWS, :],
            col_buf[...].reshape(col_tiles * tile, -1),
            (((1,), (1,)), ((), ())),
            preferred_element_type=jnp.float32,
        )
        written = pl.ds(chunk * chunk_lines, chunk_lines)
        out_buf[written, :] = share_ref[written, :] - update.reshape(chunk_lines, LANES)
        store = pltpu.make_async_copy(out_buf.at[written], out_ref.at[written], out_sems.at[chunk])
        store.start()
        stores.append(store)
    for store in stores:
        store.wait()


def update_trailing(row_pieces, col_pieces, share, half, layers, tile, col_tiles):
    pieces = len(row_pieces)
    tile_rows = row_pieces[0].shape[1]
    width = row_pieces[0].shape[2]

    def body(*refs):
        update_kernel(pieces, layers, half, tile, tile_rows, col_tiles, *refs)

    result = pl.pallas_call(
        body,
        out_shape=jax.ShapeDtypeStruct(share.shape, jnp.float32),
        in_specs=[pl.BlockSpec(memory_space=pltpu.VMEM)] * (pieces * (1 + layers) + 1),
        out_specs=pl.BlockSpec(memory_space=pltpu.HBM),
        scratch_shapes=[
            pltpu.VMEM((half, tile, width), jnp.bfloat16),
            pltpu.VMEM((half * layers, tile, width), jnp.bfloat16),
            pltpu.VMEM(share.shape, jnp.float32),
            pltpu.SemaphoreType.DMA((half * (tile // CHUNK_ROWS),)),
        ],
        compiler_params=pltpu.CompilerParams(vmem_limit_bytes=VMEM_BYTES),
        name="update",
    )(*col_pieces, *row_pieces, share)
    return result.reshape(half, 1, tile, col_tiles, 1, tile)


def per_device(trailing, panel, inverse_factor):
    layers = lax.axis_size("layer")
    count = lax.axis_size("row")
    row_tiles, _, tile, col_tiles, _, _ = trailing.shape
    half = row_tiles // layers
    slots = plane_slots(count)
    factor = make_factor(panel, inverse_factor, half)
    moved = lax.ppermute(
        factor, ("row", "col"), [(a * count + b, slots[a][b] * count + a) for a in range(count) for b in range(count)]
    )
    share = load_share(factor, trailing.reshape(-1, LANES), layers)
    loaded_factor, share = lax.optimization_barrier((factor, share))
    line = gather_line(loaded_factor, count)
    plane = [moved]
    for step in plane_steps(count)[1:]:
        plane.append(lax.ppermute(moved, "row", [(partner(a, step, count), a) for a in range(count)]))
    first, plane[-1] = lax.optimization_barrier((moved, plane[-1]))
    others = []
    for shift in range(1, layers):
        pairs = [((l + shift) % layers, l) for l in range(layers)]
        others += [lax.ppermute(piece, "layer", pairs) for piece in [first] + plane[1:]]
    return update_trailing(line, plane + others, share, half, layers, tile, col_tiles)


def solution(mesh):
    assert mesh.shape["row"] == mesh.shape["col"]
    return jax.shard_map(
        per_device,
        mesh=mesh,
        in_specs=(P(None, "row", None, None, "col", None), P(None, "row", "col", None), P()),
        out_specs=P("layer", "row", None, None, "col", None),
        check_vma=False,
    )
```

```python
import jax
import jax.numpy as jnp
from jax import lax
from jax.experimental import pallas as pl
from jax.experimental.pallas import tpu as pltpu
from jax.sharding import PartitionSpec as P

LANES = 128
CHUNK_ROWS = 128
VMEM_BYTES = 24 * 1024 * 1024
LOAD_VMEM_BYTES = 52000 * 1024
FACTOR_VMEM_BYTES = 55040 * 1024
AXES = ("row", "col", "layer")


def factor_kernel(panel_ref, inverse_ref, factor_ref, panel_buf, inverse_buf, sems):
    half = factor_ref.shape[0]
    tile_rows = factor_ref.shape[1]
    width = factor_ref.shape[2]
    layer = lax.axis_index("layer")
    copies = [
        pltpu.make_async_copy(panel_ref.at[pl.ds(layer * half, half), 0], panel_buf, sems.at[0]),
        pltpu.make_async_copy(inverse_ref, inverse_buf, sems.at[1]),
    ]
    for copy in copies:
        copy.start()
    for copy in copies:
        copy.wait()
    product = lax.dot_general(
        panel_buf[...].reshape(half * tile_rows, width),
        inverse_buf[...],
        (((1,), (1,)), ((), ())),
        precision=lax.Precision.HIGHEST,
        preferred_element_type=jnp.float32,
    )
    factor_ref[...] = product.astype(jnp.bfloat16).reshape(factor_ref.shape)


def make_factor(panel, inverse_factor, half):
    _, _, tile_rows, width = panel.shape
    return pl.pallas_call(
        factor_kernel,
        out_shape=jax.ShapeDtypeStruct((half, tile_rows, width), jnp.bfloat16),
        in_specs=[pl.BlockSpec(memory_space=pltpu.HBM)] * 2,
        out_specs=pl.BlockSpec(memory_space=pltpu.VMEM),
        scratch_shapes=[
            pltpu.VMEM((half, tile_rows, width), jnp.float32),
            pltpu.VMEM((width, width), jnp.float32),
            pltpu.SemaphoreType.DMA((2,)),
        ],
        compiler_params=pltpu.CompilerParams(vmem_limit_bytes=FACTOR_VMEM_BYTES),
        name="factor",
    )(panel, inverse_factor)


def partner(index, step, count):
    return index ^ step if count & (count - 1) == 0 else (index + step) % count


def plane_slots(count):
    if count == 4:
        return ((3, 0, 1, 2), (3, 2, 1, 0), (0, 2, 1, 3), (3, 1, 2, 0))
    return tuple(tuple(count - 1 - b for b in range(count)) for _ in range(count))


def plane_steps(count):
    return (0, 2, 1, 3) if count == 4 else tuple(range(count))


def slab_of(slots, plane, place):
    slab = jnp.int32(0)
    for at, row in enumerate(slots):
        for b, slot in enumerate(row):
            slab = jnp.where((plane == at) & (place == slot), b, slab)
    return slab


def gather_line(factor, count):
    if count != 4:
        line = [factor]
        for step in range(1, count):
            line.append(lax.ppermute(factor, "col", [(partner(b, step, count), b) for b in range(count)]))
        return line
    far = lax.ppermute(factor, "col", [(b ^ 2, b) for b in range(count)])
    near = lax.ppermute(factor, "col", [(b ^ 1, b) for b in range(count)])
    both = lax.ppermute(far, "col", [(b ^ 1, b) for b in range(count)])
    return [factor, near, far, both]


def load_kernel(after_ref, lines_ref, share_ref, sem):
    rows = share_ref.shape[0]
    layer = lax.axis_index("layer")
    load = pltpu.make_async_copy(lines_ref.at[pl.ds(layer * rows, rows)], share_ref, sem)
    load.start()
    load.wait()


def load_share(after, lines, layers):
    rows = lines.shape[0] // layers
    return pl.pallas_call(
        load_kernel,
        out_shape=jax.ShapeDtypeStruct((rows, LANES), jnp.float32),
        in_specs=[pl.BlockSpec(memory_space=pl.ANY), pl.BlockSpec(memory_space=pltpu.HBM)],
        out_specs=pl.BlockSpec(memory_space=pltpu.VMEM),
        scratch_shapes=[pltpu.SemaphoreType.DMA],
        compiler_params=pltpu.CompilerParams(vmem_limit_bytes=LOAD_VMEM_BYTES),
        cost_estimate=pl.CostEstimate(flops=0, bytes_accessed=rows * LANES * 8, transcendentals=0),
        name="load_share",
    )(after, lines)


def update_kernel(pieces, layers, half, tile, tile_rows, col_tiles, *refs):
    row_refs = refs[:pieces]
    col_refs = refs[pieces : pieces * (1 + layers)]
    share_ref, out_ref, row_buf, col_buf, out_buf, out_sems = refs[pieces * (1 + layers) :]
    r, c, layer = (lax.axis_index(axis) for axis in AXES)
    slots = plane_slots(pieces)
    per_row = col_tiles * tile // LANES
    for step, plane_step in enumerate(plane_steps(pieces)):
        row_at = pl.multiple_of(partner(c, step, pieces) * tile_rows, tile_rows)
        slab = slab_of(slots, c, partner(r, plane_step, pieces))
        col_at = pl.multiple_of(slab * tile_rows, tile_rows)
        for k in range(half):
            row_buf[k, pl.ds(row_at, tile_rows), :] = row_refs[step][k]
        for shift in range(layers):
            owner = lax.rem(layer + shift, layers)
            for k in range(half):
                col_buf[owner * half + k, pl.ds(col_at, tile_rows), :] = col_refs[shift * pieces + step][k]
    chunks = half * (tile // CHUNK_ROWS)
    chunk_lines = CHUNK_ROWS * per_row
    stores = []
    for chunk in range(chunks):
        k, first_row = divmod(chunk * CHUNK_ROWS, tile)
        update = lax.dot_general(
            row_buf[k, first_row : first_row + CHUNK_ROWS, :],
            col_buf[...].reshape(col_tiles * tile, -1),
            (((1,), (1,)), ((), ())),
            preferred_element_type=jnp.float32,
        )
        written = pl.ds(chunk * chunk_lines, chunk_lines)
        out_buf[written, :] = share_ref[written, :] - update.reshape(chunk_lines, LANES)
        store = pltpu.make_async_copy(out_buf.at[written], out_ref.at[written], out_sems.at[chunk])
        store.start()
        stores.append(store)
    for store in stores:
        store.wait()


def update_trailing(row_pieces, col_pieces, share, half, layers, tile, col_tiles):
    pieces = len(row_pieces)
    tile_rows = row_pieces[0].shape[1]
    width = row_pieces[0].shape[2]

    def body(*refs):
        update_kernel(pieces, layers, half, tile, tile_rows, col_tiles, *refs)

    result = pl.pallas_call(
        body,
        out_shape=jax.ShapeDtypeStruct(share.shape, jnp.float32),
        in_specs=[pl.BlockSpec(memory_space=pltpu.VMEM)] * (pieces * (1 + layers) + 1),
        out_specs=pl.BlockSpec(memory_space=pltpu.HBM),
        scratch_shapes=[
            pltpu.VMEM((half, tile, width), jnp.bfloat16),
            pltpu.VMEM((half * layers, tile, width), jnp.bfloat16),
            pltpu.VMEM(share.shape, jnp.float32),
            pltpu.SemaphoreType.DMA((half * (tile // CHUNK_ROWS),)),
        ],
        compiler_params=pltpu.CompilerParams(vmem_limit_bytes=VMEM_BYTES),
        name="update",
    )(*row_pieces, *col_pieces, share)
    return result.reshape(half, 1, tile, col_tiles, 1, tile)


def per_device(trailing, panel, inverse_factor):
    layers = lax.axis_size("layer")
    count = lax.axis_size("row")
    row_tiles, _, tile, col_tiles, _, _ = trailing.shape
    half = row_tiles // layers
    slots = plane_slots(count)
    factor = make_factor(panel, inverse_factor, half)
    moved = lax.ppermute(
        factor, ("row", "col"), [(a * count + b, slots[a][b] * count + a) for a in range(count) for b in range(count)]
    )
    share = load_share(factor, trailing.reshape(-1, LANES), layers)
    loaded_factor, share = lax.optimization_barrier((factor, share))
    line = gather_line(loaded_factor, count)
    plane = [moved]
    for step in plane_steps(count)[1:]:
        plane.append(lax.ppermute(moved, "row", [(partner(a, step, count), a) for a in range(count)]))
    others = []
    for shift in range(1, layers):
        pairs = [((l + shift) % layers, l) for l in range(layers)]
        others += [lax.ppermute(piece, "layer", pairs) for piece in plane]
    return update_trailing(line, plane + others, share, half, layers, tile, col_tiles)


def solution(mesh):
    assert mesh.shape["row"] == mesh.shape["col"]
    return jax.shard_map(
        per_device,
        mesh=mesh,
        in_specs=(P(None, "row", None, None, "col", None), P(None, "row", "col", None), P()),
        out_specs=P("layer", "row", None, None, "col", None),
        check_vma=False,
    )
```

```python
import jax
import jax.numpy as jnp
from jax import lax
from jax.experimental import pallas as pl
from jax.experimental.pallas import tpu as pltpu
from jax.sharding import PartitionSpec as P

LANES = 128
CHUNK_ROWS = 128
VMEM_BYTES = 24 * 1024 * 1024
LOAD_VMEM_BYTES = 52000 * 1024
FACTOR_VMEM_BYTES = 55040 * 1024
AXES = ("row", "col", "layer")


def factor_kernel(panel_ref, inverse_ref, factor_ref, panel_buf, inverse_buf, sems):
    half = factor_ref.shape[0]
    tile_rows = factor_ref.shape[1]
    width = factor_ref.shape[2]
    layer = lax.axis_index("layer")
    copies = [
        pltpu.make_async_copy(panel_ref.at[pl.ds(layer * half, half), 0], panel_buf, sems.at[0]),
        pltpu.make_async_copy(inverse_ref, inverse_buf, sems.at[1]),
    ]
    for copy in copies:
        copy.start()
    for copy in copies:
        copy.wait()
    product = lax.dot_general(
        panel_buf[...].reshape(half * tile_rows, width),
        inverse_buf[...],
        (((1,), (1,)), ((), ())),
        precision=lax.Precision.HIGHEST,
        preferred_element_type=jnp.float32,
    )
    factor_ref[...] = product.astype(jnp.bfloat16).reshape(factor_ref.shape)


def make_factor(panel, inverse_factor, half):
    _, _, tile_rows, width = panel.shape
    return pl.pallas_call(
        factor_kernel,
        out_shape=jax.ShapeDtypeStruct((half, tile_rows, width), jnp.bfloat16),
        in_specs=[pl.BlockSpec(memory_space=pltpu.HBM)] * 2,
        out_specs=pl.BlockSpec(memory_space=pltpu.VMEM),
        scratch_shapes=[
            pltpu.VMEM((half, tile_rows, width), jnp.float32),
            pltpu.VMEM((width, width), jnp.float32),
            pltpu.SemaphoreType.DMA((2,)),
        ],
        compiler_params=pltpu.CompilerParams(vmem_limit_bytes=FACTOR_VMEM_BYTES),
        name="factor",
    )(panel, inverse_factor)


def partner(index, step, count):
    return index ^ step if count & (count - 1) == 0 else (index + step) % count


def plane_slots(count):
    if count == 4:
        return ((3, 0, 1, 2), (3, 2, 1, 0), (0, 2, 1, 3), (3, 1, 2, 0))
    return tuple(tuple(count - 1 - b for b in range(count)) for _ in range(count))


def plane_steps(count):
    return (0, 2, 1, 3) if count == 4 else tuple(range(count))


def slab_of(slots, plane, place):
    slab = jnp.int32(0)
    for at, row in enumerate(slots):
        for b, slot in enumerate(row):
            slab = jnp.where((plane == at) & (place == slot), b, slab)
    return slab


def gather_line(factor, late_factor, count):
    if count != 4:
        line = [factor]
        for step in range(1, count):
            line.append(lax.ppermute(factor, "col", [(partner(b, step, count), b) for b in range(count)]))
        return line
    near = lax.ppermute(factor, "col", [(b ^ 1, b) for b in range(count)])
    far = lax.ppermute(late_factor, "col", [(b ^ 2, b) for b in range(count)])
    both = lax.ppermute(far, "col", [(b ^ 1, b) for b in range(count)])
    return [factor, near, far, both]


def load_kernel(after_ref, lines_ref, share_ref, sem):
    rows = share_ref.shape[0]
    layer = lax.axis_index("layer")
    load = pltpu.make_async_copy(lines_ref.at[pl.ds(layer * rows, rows)], share_ref, sem)
    load.start()
    load.wait()


def load_share(after, lines, layers):
    rows = lines.shape[0] // layers
    return pl.pallas_call(
        load_kernel,
        out_shape=jax.ShapeDtypeStruct((rows, LANES), jnp.float32),
        in_specs=[pl.BlockSpec(memory_space=pl.ANY), pl.BlockSpec(memory_space=pltpu.HBM)],
        out_specs=pl.BlockSpec(memory_space=pltpu.VMEM),
        scratch_shapes=[pltpu.SemaphoreType.DMA],
        compiler_params=pltpu.CompilerParams(vmem_limit_bytes=LOAD_VMEM_BYTES),
        cost_estimate=pl.CostEstimate(flops=0, bytes_accessed=rows * LANES * 8, transcendentals=0),
        name="load_share",
    )(after, lines)


def update_kernel(pieces, layers, half, tile, tile_rows, col_tiles, *refs):
    row_refs = refs[:pieces]
    col_refs = refs[pieces : pieces * (1 + layers)]
    share_ref, out_ref, row_buf, col_buf, out_buf, out_sems = refs[pieces * (1 + layers) :]
    r, c, layer = (lax.axis_index(axis) for axis in AXES)
    slots = plane_slots(pieces)
    per_row = col_tiles * tile // LANES
    for step, plane_step in enumerate(plane_steps(pieces)):
        row_at = pl.multiple_of(partner(c, step, pieces) * tile_rows, tile_rows)
        slab = slab_of(slots, c, partner(r, plane_step, pieces))
        col_at = pl.multiple_of(slab * tile_rows, tile_rows)
        for k in range(half):
            row_buf[k, pl.ds(row_at, tile_rows), :] = row_refs[step][k]
        for shift in range(layers):
            owner = lax.rem(layer + shift, layers)
            for k in range(half):
                col_buf[owner * half + k, pl.ds(col_at, tile_rows), :] = col_refs[shift * pieces + step][k]
    chunks = half * (tile // CHUNK_ROWS)
    chunk_lines = CHUNK_ROWS * per_row
    stores = []
    for chunk in range(chunks):
        k, first_row = divmod(chunk * CHUNK_ROWS, tile)
        update = lax.dot_general(
            row_buf[k, first_row : first_row + CHUNK_ROWS, :],
            col_buf[...].reshape(col_tiles * tile, -1),
            (((1,), (1,)), ((), ())),
            preferred_element_type=jnp.float32,
        )
        written = pl.ds(chunk * chunk_lines, chunk_lines)
        out_buf[written, :] = share_ref[written, :] - update.reshape(chunk_lines, LANES)
        store = pltpu.make_async_copy(out_buf.at[written], out_ref.at[written], out_sems.at[chunk])
        store.start()
        stores.append(store)
    for store in stores:
        store.wait()


def update_trailing(row_pieces, col_pieces, share, half, layers, tile, col_tiles):
    pieces = len(row_pieces)
    tile_rows = row_pieces[0].shape[1]
    width = row_pieces[0].shape[2]

    def body(*refs):
        update_kernel(pieces, layers, half, tile, tile_rows, col_tiles, *refs)

    result = pl.pallas_call(
        body,
        out_shape=jax.ShapeDtypeStruct(share.shape, jnp.float32),
        in_specs=[pl.BlockSpec(memory_space=pltpu.VMEM)] * (pieces * (1 + layers) + 1),
        out_specs=pl.BlockSpec(memory_space=pltpu.HBM),
        scratch_shapes=[
            pltpu.VMEM((half, tile, width), jnp.bfloat16),
            pltpu.VMEM((half * layers, tile, width), jnp.bfloat16),
            pltpu.VMEM(share.shape, jnp.float32),
            pltpu.SemaphoreType.DMA((half * (tile // CHUNK_ROWS),)),
        ],
        compiler_params=pltpu.CompilerParams(vmem_limit_bytes=VMEM_BYTES),
        name="update",
    )(*row_pieces, *col_pieces, share)
    return result.reshape(half, 1, tile, col_tiles, 1, tile)


def per_device(trailing, panel, inverse_factor):
    layers = lax.axis_size("layer")
    count = lax.axis_size("row")
    row_tiles, _, tile, col_tiles, _, _ = trailing.shape
    half = row_tiles // layers
    slots = plane_slots(count)
    factor = make_factor(panel, inverse_factor, half)
    moved = lax.ppermute(
        factor, ("row", "col"), [(a * count + b, slots[a][b] * count + a) for a in range(count) for b in range(count)]
    )
    share = load_share(factor, trailing.reshape(-1, LANES), layers)
    loaded_factor, share = lax.optimization_barrier((factor, share))
    line = gather_line(factor, loaded_factor, count)
    plane = [moved]
    for step in plane_steps(count)[1:]:
        plane.append(lax.ppermute(moved, "row", [(partner(a, step, count), a) for a in range(count)]))
    others = []
    for shift in range(1, layers):
        pairs = [((l + shift) % layers, l) for l in range(layers)]
        others += [lax.ppermute(piece, "layer", pairs) for piece in plane]
    return update_trailing(line, plane + others, share, half, layers, tile, col_tiles)


def solution(mesh):
    assert mesh.shape["row"] == mesh.shape["col"]
    return jax.shard_map(
        per_device,
        mesh=mesh,
        in_specs=(P(None, "row", None, None, "col", None), P(None, "row", "col", None), P()),
        out_specs=P("layer", "row", None, None, "col", None),
        check_vma=False,
    )
```

```python
import jax
import jax.numpy as jnp
from jax import lax
from jax.experimental import pallas as pl
from jax.experimental.pallas import tpu as pltpu
from jax.sharding import PartitionSpec as P

LANES = 128
CHUNK_ROWS = 128
VMEM_BYTES = 24 * 1024 * 1024
LOAD_VMEM_BYTES = 52000 * 1024
FACTOR_VMEM_BYTES = 55040 * 1024
AXES = ("row", "col", "layer")


def factor_kernel(panel_ref, inverse_ref, factor_ref, panel_buf, inverse_buf, sems):
    half = factor_ref.shape[0]
    tile_rows = factor_ref.shape[1]
    width = factor_ref.shape[2]
    layer = lax.axis_index("layer")
    copies = [
        pltpu.make_async_copy(panel_ref.at[pl.ds(layer * half, half), 0], panel_buf, sems.at[0]),
        pltpu.make_async_copy(inverse_ref, inverse_buf, sems.at[1]),
    ]
    for copy in copies:
        copy.start()
    for copy in copies:
        copy.wait()
    product = lax.dot_general(
        panel_buf[...].reshape(half * tile_rows, width),
        inverse_buf[...],
        (((1,), (1,)), ((), ())),
        precision=lax.Precision.HIGHEST,
        preferred_element_type=jnp.float32,
    )
    factor_ref[...] = product.astype(jnp.bfloat16).reshape(factor_ref.shape)


def make_factor(panel, inverse_factor, half):
    _, _, tile_rows, width = panel.shape
    return pl.pallas_call(
        factor_kernel,
        out_shape=jax.ShapeDtypeStruct((half, tile_rows, width), jnp.bfloat16),
        in_specs=[pl.BlockSpec(memory_space=pltpu.HBM)] * 2,
        out_specs=pl.BlockSpec(memory_space=pltpu.VMEM),
        scratch_shapes=[
            pltpu.VMEM((half, tile_rows, width), jnp.float32),
            pltpu.VMEM((width, width), jnp.float32),
            pltpu.SemaphoreType.DMA((2,)),
        ],
        compiler_params=pltpu.CompilerParams(vmem_limit_bytes=FACTOR_VMEM_BYTES),
        name="factor",
    )(panel, inverse_factor)


def partner(index, step, count):
    return index ^ step if count & (count - 1) == 0 else (index + step) % count


def plane_slots(count):
    if count == 4:
        return ((3, 0, 1, 2), (3, 2, 1, 0), (0, 2, 1, 3), (3, 2, 1, 0))
    return tuple(tuple(count - 1 - b for b in range(count)) for _ in range(count))


def plane_steps(count):
    return (0, 2, 1, 3) if count == 4 else tuple(range(count))


def slab_of(slots, plane, place):
    slab = jnp.int32(0)
    for at, row in enumerate(slots):
        for b, slot in enumerate(row):
            slab = jnp.where((plane == at) & (place == slot), b, slab)
    return slab


def gather_line(factor, late_factor, count):
    if count != 4:
        line = [factor]
        for step in range(1, count):
            line.append(lax.ppermute(factor, "col", [(partner(b, step, count), b) for b in range(count)]))
        return line
    near = lax.ppermute(factor, "col", [(b ^ 1, b) for b in range(count)])
    far = lax.ppermute(late_factor, "col", [(b ^ 2, b) for b in range(count)])
    both = lax.ppermute(far, "col", [(b ^ 1, b) for b in range(count)])
    return [factor, near, far, both]


def load_kernel(after_ref, lines_ref, share_ref, sem):
    rows = share_ref.shape[0]
    layer = lax.axis_index("layer")
    load = pltpu.make_async_copy(lines_ref.at[pl.ds(layer * rows, rows)], share_ref, sem)
    load.start()
    load.wait()


def load_share(after, lines, layers):
    rows = lines.shape[0] // layers
    return pl.pallas_call(
        load_kernel,
        out_shape=jax.ShapeDtypeStruct((rows, LANES), jnp.float32),
        in_specs=[pl.BlockSpec(memory_space=pl.ANY), pl.BlockSpec(memory_space=pltpu.HBM)],
        out_specs=pl.BlockSpec(memory_space=pltpu.VMEM),
        scratch_shapes=[pltpu.SemaphoreType.DMA],
        compiler_params=pltpu.CompilerParams(vmem_limit_bytes=LOAD_VMEM_BYTES),
        cost_estimate=pl.CostEstimate(flops=0, bytes_accessed=rows * LANES * 8, transcendentals=0),
        name="load_share",
    )(after, lines)


def update_kernel(pieces, layers, half, tile, tile_rows, col_tiles, *refs):
    row_refs = refs[:pieces]
    col_refs = refs[pieces : pieces * (1 + layers)]
    share_ref, out_ref, row_buf, col_buf, out_buf, out_sems = refs[pieces * (1 + layers) :]
    r, c, layer = (lax.axis_index(axis) for axis in AXES)
    slots = plane_slots(pieces)
    per_row = col_tiles * tile // LANES
    for step, plane_step in enumerate(plane_steps(pieces)):
        row_at = pl.multiple_of(partner(c, step, pieces) * tile_rows, tile_rows)
        slab = slab_of(slots, c, partner(r, plane_step, pieces))
        col_at = pl.multiple_of(slab * tile_rows, tile_rows)
        for k in range(half):
            row_buf[k, pl.ds(row_at, tile_rows), :] = row_refs[step][k]
        for shift in range(layers):
            owner = lax.rem(layer + shift, layers)
            for k in range(half):
                col_buf[owner * half + k, pl.ds(col_at, tile_rows), :] = col_refs[shift * pieces + step][k]
    chunks = half * (tile // CHUNK_ROWS)
    chunk_lines = CHUNK_ROWS * per_row
    stores = []
    for chunk in range(chunks):
        k, first_row = divmod(chunk * CHUNK_ROWS, tile)
        update = lax.dot_general(
            row_buf[k, first_row : first_row + CHUNK_ROWS, :],
            col_buf[...].reshape(col_tiles * tile, -1),
            (((1,), (1,)), ((), ())),
            preferred_element_type=jnp.float32,
        )
        written = pl.ds(chunk * chunk_lines, chunk_lines)
        out_buf[written, :] = share_ref[written, :] - update.reshape(chunk_lines, LANES)
        store = pltpu.make_async_copy(out_buf.at[written], out_ref.at[written], out_sems.at[chunk])
        store.start()
        stores.append(store)
    for store in stores:
        store.wait()


def update_trailing(row_pieces, col_pieces, share, half, layers, tile, col_tiles):
    pieces = len(row_pieces)
    tile_rows = row_pieces[0].shape[1]
    width = row_pieces[0].shape[2]

    def body(*refs):
        update_kernel(pieces, layers, half, tile, tile_rows, col_tiles, *refs)

    result = pl.pallas_call(
        body,
        out_shape=jax.ShapeDtypeStruct(share.shape, jnp.float32),
        in_specs=[pl.BlockSpec(memory_space=pltpu.VMEM)] * (pieces * (1 + layers) + 1),
        out_specs=pl.BlockSpec(memory_space=pltpu.HBM),
        scratch_shapes=[
            pltpu.VMEM((half, tile, width), jnp.bfloat16),
            pltpu.VMEM((half * layers, tile, width), jnp.bfloat16),
            pltpu.VMEM(share.shape, jnp.float32),
            pltpu.SemaphoreType.DMA((half * (tile // CHUNK_ROWS),)),
        ],
        compiler_params=pltpu.CompilerParams(vmem_limit_bytes=VMEM_BYTES),
        name="update",
    )(*row_pieces, *col_pieces, share)
    return result.reshape(half, 1, tile, col_tiles, 1, tile)


def per_device(trailing, panel, inverse_factor):
    layers = lax.axis_size("layer")
    count = lax.axis_size("row")
    row_tiles, _, tile, col_tiles, _, _ = trailing.shape
    half = row_tiles // layers
    slots = plane_slots(count)
    factor = make_factor(panel, inverse_factor, half)
    moved = lax.ppermute(
        factor, ("row", "col"), [(a * count + b, slots[a][b] * count + a) for a in range(count) for b in range(count)]
    )
    share = load_share(factor, trailing.reshape(-1, LANES), layers)
    loaded_factor, share = lax.optimization_barrier((factor, share))
    line = gather_line(factor, loaded_factor, count)
    plane = [moved]
    for step in plane_steps(count)[1:]:
        plane.append(lax.ppermute(moved, "row", [(partner(a, step, count), a) for a in range(count)]))
    others = []
    for shift in range(1, layers):
        pairs = [((l + shift) % layers, l) for l in range(layers)]
        others += [lax.ppermute(piece, "layer", pairs) for piece in plane]
    return update_trailing(line, plane + others, share, half, layers, tile, col_tiles)


def solution(mesh):
    assert mesh.shape["row"] == mesh.shape["col"]
    return jax.shard_map(
        per_device,
        mesh=mesh,
        in_specs=(P(None, "row", None, None, "col", None), P(None, "row", "col", None), P()),
        out_specs=P("layer", "row", None, None, "col", None),
        check_vma=False,
    )
```

```python
import jax
import jax.numpy as jnp
from jax import lax
from jax.experimental import pallas as pl
from jax.experimental.pallas import tpu as pltpu
from jax.sharding import PartitionSpec as P

LANES = 128
CHUNK_ROWS = 256
VMEM_BYTES = 24 * 1024 * 1024
LOAD_VMEM_BYTES = 52000 * 1024
FACTOR_VMEM_BYTES = 55040 * 1024
AXES = ("row", "col", "layer")


def factor_kernel(panel_ref, inverse_ref, factor_ref, panel_buf, inverse_buf, sems):
    half = factor_ref.shape[0]
    tile_rows = factor_ref.shape[1]
    width = factor_ref.shape[2]
    layer = lax.axis_index("layer")
    copies = [
        pltpu.make_async_copy(panel_ref.at[pl.ds(layer * half, half), 0], panel_buf, sems.at[0]),
        pltpu.make_async_copy(inverse_ref, inverse_buf, sems.at[1]),
    ]
    for copy in copies:
        copy.start()
    for copy in copies:
        copy.wait()
    product = lax.dot_general(
        panel_buf[...].reshape(half * tile_rows, width),
        inverse_buf[...],
        (((1,), (1,)), ((), ())),
        precision=lax.Precision.HIGHEST,
        preferred_element_type=jnp.float32,
    )
    factor_ref[...] = product.astype(jnp.bfloat16).reshape(factor_ref.shape)


def make_factor(panel, inverse_factor, half):
    _, _, tile_rows, width = panel.shape
    return pl.pallas_call(
        factor_kernel,
        out_shape=jax.ShapeDtypeStruct((half, tile_rows, width), jnp.bfloat16),
        in_specs=[pl.BlockSpec(memory_space=pltpu.HBM)] * 2,
        out_specs=pl.BlockSpec(memory_space=pltpu.VMEM),
        scratch_shapes=[
            pltpu.VMEM((half, tile_rows, width), jnp.float32),
            pltpu.VMEM((width, width), jnp.float32),
            pltpu.SemaphoreType.DMA((2,)),
        ],
        compiler_params=pltpu.CompilerParams(vmem_limit_bytes=FACTOR_VMEM_BYTES),
        name="factor",
    )(panel, inverse_factor)


def partner(index, step, count):
    return index ^ step if count & (count - 1) == 0 else (index + step) % count


def plane_slots(count):
    if count == 4:
        return ((3, 0, 1, 2), (3, 2, 1, 0), (0, 2, 1, 3), (3, 2, 1, 0))
    return tuple(tuple(count - 1 - b for b in range(count)) for _ in range(count))


def plane_steps(count):
    return (0, 2, 1, 3) if count == 4 else tuple(range(count))


def slab_of(slots, plane, place):
    if len(slots) == 4:
        packed = sum(row.index(p) << 2 * (4 * at + p) for at, row in enumerate(slots) for p in range(4))
        packed -= (packed >> 31) << 32
        return (jnp.int32(packed) >> (2 * (4 * plane + place))) & 3
    slab = jnp.int32(0)
    for at, row in enumerate(slots):
        for b, slot in enumerate(row):
            slab = jnp.where((plane == at) & (place == slot), b, slab)
    return slab


def gather_line(factor, late_factor, count):
    if count != 4:
        line = [factor]
        for step in range(1, count):
            line.append(lax.ppermute(factor, "col", [(partner(b, step, count), b) for b in range(count)]))
        return line
    near = lax.ppermute(factor, "col", [(b ^ 1, b) for b in range(count)])
    far = lax.ppermute(late_factor, "col", [(b ^ 2, b) for b in range(count)])
    both = lax.ppermute(far, "col", [(b ^ 1, b) for b in range(count)])
    return [factor, near, far, both]


def load_kernel(after_ref, lines_ref, share_ref, sem):
    rows = share_ref.shape[0]
    layer = lax.axis_index("layer")
    load = pltpu.make_async_copy(lines_ref.at[pl.ds(layer * rows, rows)], share_ref, sem)
    load.start()
    load.wait()


def load_share(after, lines, layers):
    rows = lines.shape[0] // layers
    return pl.pallas_call(
        load_kernel,
        out_shape=jax.ShapeDtypeStruct((rows, LANES), jnp.float32),
        in_specs=[pl.BlockSpec(memory_space=pl.ANY), pl.BlockSpec(memory_space=pltpu.HBM)],
        out_specs=pl.BlockSpec(memory_space=pltpu.VMEM),
        scratch_shapes=[pltpu.SemaphoreType.DMA],
        compiler_params=pltpu.CompilerParams(vmem_limit_bytes=LOAD_VMEM_BYTES),
        cost_estimate=pl.CostEstimate(flops=0, bytes_accessed=rows * LANES * 8, transcendentals=0),
        name="load_share",
    )(after, lines)


def update_kernel(pieces, layers, half, tile, tile_rows, col_tiles, *refs):
    row_refs = refs[:pieces]
    col_refs = refs[pieces : pieces * (1 + layers)]
    share_ref, out_ref, row_buf, col_buf, out_buf, out_sems = refs[pieces * (1 + layers) :]
    r, c, layer = (lax.axis_index(axis) for axis in AXES)
    slots = plane_slots(pieces)
    per_row = col_tiles * tile // LANES
    for step, plane_step in enumerate(plane_steps(pieces)):
        row_at = pl.multiple_of(partner(c, step, pieces) * tile_rows, tile_rows)
        slab = slab_of(slots, c, partner(r, plane_step, pieces))
        col_at = pl.multiple_of(slab * tile_rows, tile_rows)
        for k in range(half):
            row_buf[k, pl.ds(row_at, tile_rows), :] = row_refs[step][k]
        for shift in range(layers):
            owner = lax.rem(layer + shift, layers)
            for k in range(half):
                col_buf[owner * half + k, pl.ds(col_at, tile_rows), :] = col_refs[shift * pieces + step][k]
    chunks = half * (tile // CHUNK_ROWS)
    chunk_lines = CHUNK_ROWS * per_row
    stores = []
    for chunk in range(chunks):
        k, first_row = divmod(chunk * CHUNK_ROWS, tile)
        update = lax.dot_general(
            row_buf[k, first_row : first_row + CHUNK_ROWS, :],
            col_buf[...].reshape(col_tiles * tile, -1),
            (((1,), (1,)), ((), ())),
            preferred_element_type=jnp.float32,
        )
        written = pl.ds(chunk * chunk_lines, chunk_lines)
        out_buf[written, :] = share_ref[written, :] - update.reshape(chunk_lines, LANES)
        store = pltpu.make_async_copy(out_buf.at[written], out_ref.at[written], out_sems.at[chunk])
        store.start()
        stores.append(store)
    for store in stores:
        store.wait()


def update_trailing(row_pieces, col_pieces, share, half, layers, tile, col_tiles):
    pieces = len(row_pieces)
    tile_rows = row_pieces[0].shape[1]
    width = row_pieces[0].shape[2]

    def body(*refs):
        update_kernel(pieces, layers, half, tile, tile_rows, col_tiles, *refs)

    result = pl.pallas_call(
        body,
        out_shape=jax.ShapeDtypeStruct(share.shape, jnp.float32),
        in_specs=[pl.BlockSpec(memory_space=pltpu.VMEM)] * (pieces * (1 + layers) + 1),
        out_specs=pl.BlockSpec(memory_space=pltpu.HBM),
        scratch_shapes=[
            pltpu.VMEM((half, tile, width), jnp.bfloat16),
            pltpu.VMEM((half * layers, tile, width), jnp.bfloat16),
            pltpu.VMEM(share.shape, jnp.float32),
            pltpu.SemaphoreType.DMA((half * (tile // CHUNK_ROWS),)),
        ],
        compiler_params=pltpu.CompilerParams(vmem_limit_bytes=VMEM_BYTES),
        name="update",
    )(*row_pieces, *col_pieces, share)
    return result.reshape(half, 1, tile, col_tiles, 1, tile)


def per_device(trailing, panel, inverse_factor):
    layers = lax.axis_size("layer")
    count = lax.axis_size("row")
    row_tiles, _, tile, col_tiles, _, _ = trailing.shape
    half = row_tiles // layers
    slots = plane_slots(count)
    factor = make_factor(panel, inverse_factor, half)
    moved = lax.ppermute(
        factor, ("row", "col"), [(a * count + b, slots[a][b] * count + a) for a in range(count) for b in range(count)]
    )
    share = load_share(factor, trailing.reshape(-1, LANES), layers)
    loaded_factor, share = lax.optimization_barrier((factor, share))
    line = gather_line(factor, loaded_factor, count)
    plane = [moved]
    for step in plane_steps(count)[1:]:
        plane.append(lax.ppermute(moved, "row", [(partner(a, step, count), a) for a in range(count)]))
    others = []
    for shift in range(1, layers):
        pairs = [((l + shift) % layers, l) for l in range(layers)]
        others += [lax.ppermute(piece, "layer", pairs) for piece in plane]
    return update_trailing(line, plane + others, share, half, layers, tile, col_tiles)


def solution(mesh):
    assert mesh.shape["row"] == mesh.shape["col"]
    return jax.shard_map(
        per_device,
        mesh=mesh,
        in_specs=(P(None, "row", None, None, "col", None), P(None, "row", "col", None), P()),
        out_specs=P("layer", "row", None, None, "col", None),
        check_vma=False,
    )
```

```python
import jax
import jax.numpy as jnp
from jax import lax
from jax.experimental import pallas as pl
from jax.experimental.pallas import tpu as pltpu
from jax.sharding import PartitionSpec as P

LANES = 128
CHUNK_ROWS = 256
VMEM_BYTES = 24 * 1024 * 1024
LOAD_VMEM_BYTES = 52000 * 1024
FACTOR_VMEM_BYTES = 55040 * 1024
AXES = ("row", "col", "layer")


def factor_kernel(panel_ref, inverse_ref, factor_ref, panel_buf, inverse_buf, sems):
    half = factor_ref.shape[0]
    tile_rows = factor_ref.shape[1]
    width = factor_ref.shape[2]
    layer = lax.axis_index("layer")
    copies = [
        pltpu.make_async_copy(panel_ref.at[pl.ds(layer * half, half), 0], panel_buf, sems.at[0]),
        pltpu.make_async_copy(inverse_ref, inverse_buf, sems.at[1]),
    ]
    for copy in copies:
        copy.start()
    for copy in copies:
        copy.wait()
    product = lax.dot_general(
        panel_buf[...].reshape(half * tile_rows, width),
        inverse_buf[...],
        (((1,), (1,)), ((), ())),
        precision=lax.Precision.HIGHEST,
        preferred_element_type=jnp.float32,
    )
    factor_ref[...] = product.astype(jnp.bfloat16).reshape(factor_ref.shape)


def make_factor(panel, inverse_factor, half):
    _, _, tile_rows, width = panel.shape
    return pl.pallas_call(
        factor_kernel,
        out_shape=jax.ShapeDtypeStruct((half, tile_rows, width), jnp.bfloat16),
        in_specs=[pl.BlockSpec(memory_space=pltpu.HBM)] * 2,
        out_specs=pl.BlockSpec(memory_space=pltpu.VMEM),
        scratch_shapes=[
            pltpu.VMEM((half, tile_rows, width), jnp.float32),
            pltpu.VMEM((width, width), jnp.float32),
            pltpu.SemaphoreType.DMA((2,)),
        ],
        compiler_params=pltpu.CompilerParams(vmem_limit_bytes=FACTOR_VMEM_BYTES),
        name="factor",
    )(panel, inverse_factor)


def partner(index, step, count):
    return index ^ step if count & (count - 1) == 0 else (index + step) % count


def plane_slots(count):
    if count == 4:
        return ((3, 0, 1, 2), (3, 2, 1, 0), (0, 2, 1, 3), (3, 2, 1, 0))
    return tuple(tuple(count - 1 - b for b in range(count)) for _ in range(count))


def plane_steps(count):
    return (0, 2, 1, 3) if count == 4 else tuple(range(count))


def slab_of(slots, plane, place):
    if len(slots) == 4:
        packed = sum(row.index(p) << 2 * (4 * at + p) for at, row in enumerate(slots) for p in range(4))
        packed -= (packed >> 31) << 32
        return (jnp.int32(packed) >> (2 * (4 * plane + place))) & 3
    slab = jnp.int32(0)
    for at, row in enumerate(slots):
        for b, slot in enumerate(row):
            slab = jnp.where((plane == at) & (place == slot), b, slab)
    return slab


def gather_line(factor, late_factor, count):
    if count != 4:
        line = [factor]
        for step in range(1, count):
            line.append(lax.ppermute(factor, "col", [(partner(b, step, count), b) for b in range(count)]))
        return line
    sources = {(r, c): (r ^ 1, c) if r == c else (r, c ^ 1) for r in range(count) for c in range(count)}
    near = lax.ppermute(
        factor, ("row", "col"), [(a * count + b, r * count + c) for (r, c), (a, b) in sources.items()]
    )
    far = lax.ppermute(late_factor, "col", [(b ^ 2, b) for b in range(count)])
    both = lax.ppermute(far, "col", [(b ^ 1, b) for b in range(count)])
    return [factor, near, far, both]


def load_kernel(after_ref, lines_ref, share_ref, sem):
    rows = share_ref.shape[0]
    layer = lax.axis_index("layer")
    load = pltpu.make_async_copy(lines_ref.at[pl.ds(layer * rows, rows)], share_ref, sem)
    load.start()
    load.wait()


def load_share(after, lines, layers):
    rows = lines.shape[0] // layers
    return pl.pallas_call(
        load_kernel,
        out_shape=jax.ShapeDtypeStruct((rows, LANES), jnp.float32),
        in_specs=[pl.BlockSpec(memory_space=pl.ANY), pl.BlockSpec(memory_space=pltpu.HBM)],
        out_specs=pl.BlockSpec(memory_space=pltpu.VMEM),
        scratch_shapes=[pltpu.SemaphoreType.DMA],
        compiler_params=pltpu.CompilerParams(vmem_limit_bytes=LOAD_VMEM_BYTES),
        cost_estimate=pl.CostEstimate(flops=0, bytes_accessed=rows * LANES * 8, transcendentals=0),
        name="load_share",
    )(after, lines)


def update_kernel(pieces, layers, half, tile, tile_rows, col_tiles, *refs):
    row_refs = refs[:pieces]
    col_refs = refs[pieces : pieces * (1 + layers)]
    share_ref, out_ref, row_buf, col_buf, out_buf, out_sems = refs[pieces * (1 + layers) :]
    r, c, layer = (lax.axis_index(axis) for axis in AXES)
    slots = plane_slots(pieces)
    per_row = col_tiles * tile // LANES
    for step, plane_step in enumerate(plane_steps(pieces)):
        row_at = pl.multiple_of(partner(c, step, pieces) * tile_rows, tile_rows)
        slab = slab_of(slots, c, partner(r, plane_step, pieces))
        col_at = pl.multiple_of(slab * tile_rows, tile_rows)
        for k in range(half):
            row_buf[k, pl.ds(row_at, tile_rows), :] = row_refs[step][k]
        for shift in range(layers):
            owner = lax.rem(layer + shift, layers)
            for k in range(half):
                col_buf[owner * half + k, pl.ds(col_at, tile_rows), :] = col_refs[shift * pieces + step][k]
    if pieces == 4:

        @pl.when(r == c)
        def _():
            row_buf[...] = col_buf[pl.ds(layer * half, half)]

    chunks = half * (tile // CHUNK_ROWS)
    chunk_lines = CHUNK_ROWS * per_row
    stores = []
    for chunk in range(chunks):
        k, first_row = divmod(chunk * CHUNK_ROWS, tile)
        update = lax.dot_general(
            row_buf[k, first_row : first_row + CHUNK_ROWS, :],
            col_buf[...].reshape(col_tiles * tile, -1),
            (((1,), (1,)), ((), ())),
            preferred_element_type=jnp.float32,
        )
        written = pl.ds(chunk * chunk_lines, chunk_lines)
        out_buf[written, :] = share_ref[written, :] - update.reshape(chunk_lines, LANES)
        store = pltpu.make_async_copy(out_buf.at[written], out_ref.at[written], out_sems.at[chunk])
        store.start()
        stores.append(store)
    for store in stores:
        store.wait()


def update_trailing(row_pieces, col_pieces, share, half, layers, tile, col_tiles):
    pieces = len(row_pieces)
    tile_rows = row_pieces[0].shape[1]
    width = row_pieces[0].shape[2]

    def body(*refs):
        update_kernel(pieces, layers, half, tile, tile_rows, col_tiles, *refs)

    result = pl.pallas_call(
        body,
        out_shape=jax.ShapeDtypeStruct(share.shape, jnp.float32),
        in_specs=[pl.BlockSpec(memory_space=pltpu.VMEM)] * (pieces * (1 + layers) + 1),
        out_specs=pl.BlockSpec(memory_space=pltpu.HBM),
        scratch_shapes=[
            pltpu.VMEM((half, tile, width), jnp.bfloat16),
            pltpu.VMEM((half * layers, tile, width), jnp.bfloat16),
            pltpu.VMEM(share.shape, jnp.float32),
            pltpu.SemaphoreType.DMA((half * (tile // CHUNK_ROWS),)),
        ],
        compiler_params=pltpu.CompilerParams(vmem_limit_bytes=VMEM_BYTES),
        name="update",
    )(*row_pieces, *col_pieces, share)
    return result.reshape(half, 1, tile, col_tiles, 1, tile)


def per_device(trailing, panel, inverse_factor):
    layers = lax.axis_size("layer")
    count = lax.axis_size("row")
    row_tiles, _, tile, col_tiles, _, _ = trailing.shape
    half = row_tiles // layers
    slots = plane_slots(count)
    factor = make_factor(panel, inverse_factor, half)
    moved = lax.ppermute(
        factor, ("row", "col"), [(a * count + b, slots[a][b] * count + a) for a in range(count) for b in range(count)]
    )
    share = load_share(factor, trailing.reshape(-1, LANES), layers)
    loaded_factor, share = lax.optimization_barrier((factor, share))
    line = gather_line(factor, loaded_factor, count)
    plane = [moved]
    for step in plane_steps(count)[1:]:
        plane.append(lax.ppermute(moved, "row", [(partner(a, step, count), a) for a in range(count)]))
    others = []
    for shift in range(1, layers):
        pairs = [((l + shift) % layers, l) for l in range(layers)]
        others += [lax.ppermute(piece, "layer", pairs) for piece in plane]
    return update_trailing(line, plane + others, share, half, layers, tile, col_tiles)


def solution(mesh):
    assert mesh.shape["row"] == mesh.shape["col"]
    return jax.shard_map(
        per_device,
        mesh=mesh,
        in_specs=(P(None, "row", None, None, "col", None), P(None, "row", "col", None), P()),
        out_specs=P("layer", "row", None, None, "col", None),
        check_vma=False,
    )
```

```python
import jax
import jax.numpy as jnp
from jax import lax
from jax.experimental import pallas as pl
from jax.experimental.pallas import tpu as pltpu
from jax.sharding import PartitionSpec as P

LANES = 128
CHUNK_ROWS = 256
VMEM_BYTES = 24 * 1024 * 1024
LOAD_VMEM_BYTES = 52000 * 1024
FACTOR_VMEM_BYTES = 55040 * 1024
AXES = ("row", "col", "layer")


def split(x):
    parts = []
    for _ in range(3):
        parts.append(x.astype(jnp.bfloat16))
        x = x - parts[-1].astype(jnp.float32)
    return parts


def factor_kernel(panel_ref, inverse_ref, factor_ref, panel_buf, inverse_buf, sems):
    half = factor_ref.shape[0]
    tile_rows = factor_ref.shape[1]
    width = factor_ref.shape[2]
    layer = lax.axis_index("layer")
    copies = [
        pltpu.make_async_copy(panel_ref.at[pl.ds(layer * half, half), 0], panel_buf, sems.at[0]),
        pltpu.make_async_copy(inverse_ref, inverse_buf, sems.at[1]),
    ]
    for copy in copies:
        copy.start()
    for copy in copies:
        copy.wait()
    rows = half * tile_rows
    panel = split(panel_buf[...].reshape(rows, width))
    inverse = split(inverse_buf[...])

    def times(parts, part):
        return lax.dot_general(
            jnp.concatenate(parts, axis=0), part, (((1,), (1,)), ((), ())), preferred_element_type=jnp.float32
        )

    high = times(panel, inverse[0])
    middle = times(panel[:2], inverse[1])
    low = times(panel[:1], inverse[2])
    product = (low + middle[rows:]) + high[2 * rows :]
    product = (product + (middle[:rows] + high[rows : 2 * rows])) + high[:rows]
    factor_ref[...] = product.astype(jnp.bfloat16).reshape(factor_ref.shape)


def make_factor(panel, inverse_factor, half):
    _, _, tile_rows, width = panel.shape
    return pl.pallas_call(
        factor_kernel,
        out_shape=jax.ShapeDtypeStruct((half, tile_rows, width), jnp.bfloat16),
        in_specs=[pl.BlockSpec(memory_space=pltpu.HBM)] * 2,
        out_specs=pl.BlockSpec(memory_space=pltpu.VMEM),
        scratch_shapes=[
            pltpu.VMEM((half, tile_rows, width), jnp.float32),
            pltpu.VMEM((width, width), jnp.float32),
            pltpu.SemaphoreType.DMA((2,)),
        ],
        compiler_params=pltpu.CompilerParams(vmem_limit_bytes=FACTOR_VMEM_BYTES),
        name="factor",
    )(panel, inverse_factor)


def partner(index, step, count):
    return index ^ step if count & (count - 1) == 0 else (index + step) % count


def plane_slots(count):
    if count == 4:
        return ((3, 0, 1, 2), (3, 2, 1, 0), (0, 2, 1, 3), (3, 2, 1, 0))
    return tuple(tuple(count - 1 - b for b in range(count)) for _ in range(count))


def plane_mates(count, plane):
    if count == 4:
        return (0, 1, 2, 3) if plane == 0 else (0, 2, 1, 3)
    return tuple(range(count))


def slab_of(slots, plane, place):
    if len(slots) == 4:
        packed = sum(row.index(p) << 2 * (4 * at + p) for at, row in enumerate(slots) for p in range(4))
        packed -= (packed >> 31) << 32
        return (jnp.int32(packed) >> (2 * (4 * plane + place))) & 3
    slab = jnp.int32(0)
    for at, row in enumerate(slots):
        for b, slot in enumerate(row):
            slab = jnp.where((plane == at) & (place == slot), b, slab)
    return slab


def gather_line(factor, late_factor, count):
    if count != 4:
        line = [factor]
        for step in range(1, count):
            line.append(lax.ppermute(factor, "col", [(partner(b, step, count), b) for b in range(count)]))
        return line
    sources = {(r, c): (r ^ 1, c) if r == c else (r, c ^ 1) for r in range(count) for c in range(count)}
    near = lax.ppermute(
        factor, ("row", "col"), [(a * count + b, r * count + c) for (r, c), (a, b) in sources.items()]
    )
    far = lax.ppermute(late_factor, "col", [(b ^ 2, b) for b in range(count)])
    both = lax.ppermute(far, "col", [(b ^ 1, b) for b in range(count)])
    return [factor, near, far, both]


def load_kernel(after_ref, lines_ref, share_ref, sem):
    rows = share_ref.shape[0]
    layer = lax.axis_index("layer")
    load = pltpu.make_async_copy(lines_ref.at[pl.ds(layer * rows, rows)], share_ref, sem)
    load.start()
    load.wait()


def load_share(after, lines, layers):
    rows = lines.shape[0] // layers
    return pl.pallas_call(
        load_kernel,
        out_shape=jax.ShapeDtypeStruct((rows, LANES), jnp.float32),
        in_specs=[pl.BlockSpec(memory_space=pl.ANY), pl.BlockSpec(memory_space=pltpu.HBM)],
        out_specs=pl.BlockSpec(memory_space=pltpu.VMEM),
        scratch_shapes=[pltpu.SemaphoreType.DMA],
        compiler_params=pltpu.CompilerParams(vmem_limit_bytes=LOAD_VMEM_BYTES),
        cost_estimate=pl.CostEstimate(flops=0, bytes_accessed=rows * LANES * 8, transcendentals=0),
        name="load_share",
    )(after, lines)


def update_kernel(pieces, layers, half, tile, tile_rows, col_tiles, *refs):
    row_refs = refs[:pieces]
    col_refs = refs[pieces : pieces * (1 + layers)]
    share_ref, out_ref, row_buf, col_buf, out_buf, out_sems = refs[pieces * (1 + layers) :]
    r, c, layer = (lax.axis_index(axis) for axis in AXES)
    slots = plane_slots(pieces)
    per_row = col_tiles * tile // LANES
    for step in range(pieces):
        mate = jnp.where(c == 0, plane_mates(pieces, 0)[step], plane_mates(pieces, 1)[step])
        row_at = pl.multiple_of(partner(c, step, pieces) * tile_rows, tile_rows)
        slab = slab_of(slots, c, partner(r, mate, pieces))
        col_at = pl.multiple_of(slab * tile_rows, tile_rows)
        for k in range(half):
            row_buf[k, pl.ds(row_at, tile_rows), :] = row_refs[step][k]
        for shift in range(layers):
            owner = lax.rem(layer + shift, layers)
            for k in range(half):
                col_buf[owner * half + k, pl.ds(col_at, tile_rows), :] = col_refs[shift * pieces + step][k]
    if pieces == 4:

        @pl.when(r == c)
        def _():
            row_buf[...] = col_buf[pl.ds(layer * half, half)]

    chunks = half * (tile // CHUNK_ROWS)
    chunk_lines = CHUNK_ROWS * per_row
    stores = []
    for chunk in range(chunks):
        k, first_row = divmod(chunk * CHUNK_ROWS, tile)
        update = lax.dot_general(
            row_buf[k, first_row : first_row + CHUNK_ROWS, :],
            col_buf[...].reshape(col_tiles * tile, -1),
            (((1,), (1,)), ((), ())),
            preferred_element_type=jnp.float32,
        )
        written = pl.ds(chunk * chunk_lines, chunk_lines)
        out_buf[written, :] = share_ref[written, :] - update.reshape(chunk_lines, LANES)
        store = pltpu.make_async_copy(out_buf.at[written], out_ref.at[written], out_sems.at[chunk])
        store.start()
        stores.append(store)
    for store in stores:
        store.wait()


def update_trailing(row_pieces, col_pieces, share, half, layers, tile, col_tiles):
    pieces = len(row_pieces)
    tile_rows = row_pieces[0].shape[1]
    width = row_pieces[0].shape[2]

    def body(*refs):
        update_kernel(pieces, layers, half, tile, tile_rows, col_tiles, *refs)

    result = pl.pallas_call(
        body,
        out_shape=jax.ShapeDtypeStruct(share.shape, jnp.float32),
        in_specs=[pl.BlockSpec(memory_space=pltpu.VMEM)] * (pieces * (1 + layers) + 1),
        out_specs=pl.BlockSpec(memory_space=pltpu.HBM),
        scratch_shapes=[
            pltpu.VMEM((half, tile, width), jnp.bfloat16),
            pltpu.VMEM((half * layers, tile, width), jnp.bfloat16),
            pltpu.VMEM(share.shape, jnp.float32),
            pltpu.SemaphoreType.DMA((half * (tile // CHUNK_ROWS),)),
        ],
        compiler_params=pltpu.CompilerParams(vmem_limit_bytes=VMEM_BYTES),
        name="update",
    )(*row_pieces, *col_pieces, share)
    return result.reshape(half, 1, tile, col_tiles, 1, tile)


def per_device(trailing, panel, inverse_factor):
    layers = lax.axis_size("layer")
    count = lax.axis_size("row")
    row_tiles, _, tile, col_tiles, _, _ = trailing.shape
    half = row_tiles // layers
    slots = plane_slots(count)
    factor = make_factor(panel, inverse_factor, half)
    moved = lax.ppermute(
        factor, ("row", "col"), [(a * count + b, slots[a][b] * count + a) for a in range(count) for b in range(count)]
    )
    share = load_share(factor, trailing.reshape(-1, LANES), layers)
    loaded_factor, share = lax.optimization_barrier((factor, share))
    line = gather_line(factor, loaded_factor, count)
    plane = [moved]
    for step in range(1, count):
        pairs = [
            (partner(a, plane_mates(count, b)[step], count) * count + b, a * count + b)
            for a in range(count)
            for b in range(count)
        ]
        plane.append(lax.ppermute(moved, ("row", "col"), pairs))
    others = []
    for shift in range(1, layers):
        pairs = [((l + shift) % layers, l) for l in range(layers)]
        others += [lax.ppermute(piece, "layer", pairs) for piece in plane]
    return update_trailing(line, plane + others, share, half, layers, tile, col_tiles)


def solution(mesh):
    assert mesh.shape["row"] == mesh.shape["col"]
    return jax.shard_map(
        per_device,
        mesh=mesh,
        in_specs=(P(None, "row", None, None, "col", None), P(None, "row", "col", None), P()),
        out_specs=P("layer", "row", None, None, "col", None),
        check_vma=False,
    )
```

```python
import jax
import jax.numpy as jnp
from jax import lax
from jax.experimental import pallas as pl
from jax.experimental.pallas import tpu as pltpu
from jax.sharding import PartitionSpec as P

LANES = 128
VMEM_BYTES = 24 * 1024 * 1024
LOAD_VMEM_BYTES = 52000 * 1024
FACTOR_VMEM_BYTES = 55040 * 1024
AXES = ("row", "col", "layer")


def split(x):
    parts = []
    for _ in range(3):
        parts.append(x.astype(jnp.bfloat16))
        x = x - parts[-1].astype(jnp.float32)
    return parts


def factor_kernel(panel_ref, inverse_ref, factor_ref, panel_buf, inverse_buf, sems):
    half = factor_ref.shape[0]
    tile_rows = factor_ref.shape[1]
    width = factor_ref.shape[2]
    layer = lax.axis_index("layer")
    copies = [
        pltpu.make_async_copy(panel_ref.at[pl.ds(layer * half, half), 0], panel_buf, sems.at[0]),
        pltpu.make_async_copy(inverse_ref, inverse_buf, sems.at[1]),
    ]
    for copy in copies:
        copy.start()
    for copy in copies:
        copy.wait()
    rows = half * tile_rows
    panel = split(panel_buf[...].reshape(rows, width))
    inverse = split(inverse_buf[...])

    def times(parts, part):
        return lax.dot_general(
            jnp.concatenate(parts, axis=0), part, (((1,), (1,)), ((), ())), preferred_element_type=jnp.float32
        )

    high = times(panel, inverse[0])
    middle = times(panel[:2], inverse[1])
    low = times(panel[:1], inverse[2])
    product = (low + middle[rows:]) + high[2 * rows :]
    product = (product + (middle[:rows] + high[rows : 2 * rows])) + high[:rows]
    factor_ref[...] = product.astype(jnp.bfloat16).reshape(factor_ref.shape)


def make_factor(panel, inverse_factor, half):
    _, _, tile_rows, width = panel.shape
    return pl.pallas_call(
        factor_kernel,
        out_shape=jax.ShapeDtypeStruct((half, tile_rows, width), jnp.bfloat16),
        in_specs=[pl.BlockSpec(memory_space=pltpu.HBM)] * 2,
        out_specs=pl.BlockSpec(memory_space=pltpu.VMEM),
        scratch_shapes=[
            pltpu.VMEM((half, tile_rows, width), jnp.float32),
            pltpu.VMEM((width, width), jnp.float32),
            pltpu.SemaphoreType.DMA((2,)),
        ],
        compiler_params=pltpu.CompilerParams(vmem_limit_bytes=FACTOR_VMEM_BYTES),
        name="factor",
    )(panel, inverse_factor)


def partner(index, step, count):
    return index ^ step if count & (count - 1) == 0 else (index + step) % count


def plane_slots(count):
    if count == 4:
        return ((3, 0, 1, 2), (3, 2, 1, 0), (0, 2, 1, 3), (3, 2, 1, 0))
    return tuple(tuple(count - 1 - b for b in range(count)) for _ in range(count))


def plane_mates(count, plane):
    if count == 4:
        return (0, 1, 2, 3) if plane == 0 else (0, 2, 1, 3)
    return tuple(range(count))


def slab_of(slots, plane, place):
    if len(slots) == 4:
        packed = sum(row.index(p) << 2 * (4 * at + p) for at, row in enumerate(slots) for p in range(4))
        packed -= (packed >> 31) << 32
        return (jnp.int32(packed) >> (2 * (4 * plane + place))) & 3
    slab = jnp.int32(0)
    for at, row in enumerate(slots):
        for b, slot in enumerate(row):
            slab = jnp.where((plane == at) & (place == slot), b, slab)
    return slab


def gather_line(factor, late_factor, count):
    if count != 4:
        line = [factor]
        for step in range(1, count):
            line.append(lax.ppermute(factor, "col", [(partner(b, step, count), b) for b in range(count)]))
        return line
    sources = {(r, c): (r ^ 1, c) if r == c else (r, c ^ 1) for r in range(count) for c in range(count)}
    near = lax.ppermute(
        factor, ("row", "col"), [(a * count + b, r * count + c) for (r, c), (a, b) in sources.items()]
    )
    far = lax.ppermute(late_factor, "col", [(b ^ 2, b) for b in range(count)])
    both = lax.ppermute(far, "col", [(b ^ 1, b) for b in range(count)])
    return [factor, near, far, both]


def load_kernel(after_ref, lines_ref, share_ref, sem):
    rows = share_ref.shape[0]
    layer = lax.axis_index("layer")
    load = pltpu.make_async_copy(lines_ref.at[pl.ds(layer * rows, rows)], share_ref, sem)
    load.start()
    load.wait()


def load_share(after, lines, layers):
    rows = lines.shape[0] // layers
    return pl.pallas_call(
        load_kernel,
        out_shape=jax.ShapeDtypeStruct((rows, LANES), jnp.float32),
        in_specs=[pl.BlockSpec(memory_space=pl.ANY), pl.BlockSpec(memory_space=pltpu.HBM)],
        out_specs=pl.BlockSpec(memory_space=pltpu.VMEM),
        scratch_shapes=[pltpu.SemaphoreType.DMA],
        compiler_params=pltpu.CompilerParams(vmem_limit_bytes=LOAD_VMEM_BYTES),
        cost_estimate=pl.CostEstimate(flops=0, bytes_accessed=rows * LANES * 8, transcendentals=0),
        name="load_share",
    )(after, lines)


def fill_columns(columns_ref, pieces, slots, r, c, owner):
    half, tile_rows, _ = pieces[0].shape
    tile = tile_rows * len(pieces)
    for step, piece in enumerate(pieces):
        mate = jnp.where(c == 0, plane_mates(len(pieces), 0)[step], plane_mates(len(pieces), 1)[step])
        slab = slab_of(slots, c, partner(r, mate, len(pieces)))
        for k in range(half):
            at = pl.multiple_of(k * tile + slab * tile_rows, tile_rows)
            columns_ref[pl.ds(at, tile_rows), :] = piece[k]


def subtract_product(share_ref, rows, columns, tile, first_row, first_line, per_row):
    half, tile_rows, width = rows.shape
    product = lax.dot_general(
        rows.reshape(half * tile_rows, width),
        columns,
        (((1,), (1,)), ((), ())),
        preferred_element_type=jnp.float32,
    )
    for k in range(half):
        for part in range(product.shape[1] // LANES):
            start = (k * tile + first_row) * per_row + first_line + part
            at = pl.ds(start, tile_rows, stride=per_row)
            share_ref[at, :] -= product[k * tile_rows : (k + 1) * tile_rows, part * LANES : (part + 1) * LANES]


def begin_kernel(pieces, layers, tile, *refs):
    column_refs, row_refs, rest = refs[:pieces], refs[pieces : 2 * pieces - 1], refs[2 * pieces - 1 :]
    _, share_ref, columns_ref, near_ref = rest
    r, c, layer = (lax.axis_index(axis) for axis in AXES)
    half, tile_rows, _ = row_refs[0].shape
    own_lines = half * tile // LANES
    fill_columns(columns_ref, column_refs, plane_slots(pieces), r, c, layer)
    near_ref[...] = row_refs[1][...]
    near_at = pl.multiple_of(partner(c, 1, pieces) * tile_rows, tile_rows)
    if pieces == 4:

        @pl.when(r == c)
        def _():
            for k in range(half):
                near_ref[k] = columns_ref[pl.ds(k * tile + near_at, tile_rows), :]

    for step, row_ref in enumerate((row_refs[0], near_ref, *row_refs[2:])):
        first_row = partner(c, step, pieces) * tile_rows
        subtract_product(
            share_ref, row_ref[...], columns_ref[...], tile, first_row, layer * own_lines, layers * own_lines
        )


def begin_update(column_pieces, row_pieces, share, layers, tile):
    pieces = len(column_pieces)
    half, _, width = row_pieces[0].shape

    def body(*refs):
        begin_kernel(pieces, layers, tile, *refs)

    return pl.pallas_call(
        body,
        out_shape=[
            jax.ShapeDtypeStruct(share.shape, jnp.float32),
            jax.ShapeDtypeStruct((half * tile, width), jnp.bfloat16),
            jax.ShapeDtypeStruct(row_pieces[0].shape, jnp.bfloat16),
        ],
        in_specs=[pl.BlockSpec(memory_space=pltpu.VMEM)] * (2 * pieces),
        out_specs=[pl.BlockSpec(memory_space=pltpu.VMEM)] * 3,
        input_output_aliases={2 * pieces - 1: 0},
        compiler_params=pltpu.CompilerParams(vmem_limit_bytes=VMEM_BYTES),
        name="begin_update",
    )(*column_pieces, *row_pieces, share)


def end_kernel(pieces, layers, tile, *refs):
    others = pieces * (layers - 1)
    column_refs, row_refs, rest = refs[:others], refs[others : others + pieces], refs[others + pieces :]
    own_ref, _, out_ref, share_ref, columns_buf, sems = rest
    r, c, layer = (lax.axis_index(axis) for axis in AXES)
    half, tile_rows, _ = row_refs[0].shape
    own_lines = half * tile // LANES
    per_row = layers * own_lines
    owners = [lax.rem(layer + shift, layers) for shift in range(1, layers)]
    for at, owner in enumerate(owners):
        fill_columns(
            columns_buf.at[at], column_refs[at * pieces : (at + 1) * pieces], plane_slots(pieces), r, c, owner
        )
    stores = []
    for step, row_ref in enumerate(row_refs):
        first_row = partner(c, step, pieces) * tile_rows
        rows = row_ref[...]
        for at, owner in enumerate(owners):
            subtract_product(share_ref, rows, columns_buf[at], tile, first_row, owner * own_lines, per_row)
        if step == pieces - 1:
            subtract_product(share_ref, rows, own_ref[...], tile, first_row, layer * own_lines, per_row)
        for k in range(half):
            lines = tile_rows * per_row
            start = pl.multiple_of((k * tile + first_row) * per_row, lines)
            store = pltpu.make_async_copy(
                share_ref.at[pl.ds(start, lines)], out_ref.at[pl.ds(start, lines)], sems.at[step * half + k]
            )
            store.start()
            stores.append(store)
    for store in stores:
        store.wait()


def end_update(column_pieces, row_pieces, own_columns, share, layers, tile):
    pieces = len(row_pieces)
    half = row_pieces[0].shape[0]
    operands = (*column_pieces, *row_pieces, own_columns, share)

    def body(*refs):
        end_kernel(pieces, layers, tile, *refs)

    result, _ = pl.pallas_call(
        body,
        out_shape=[jax.ShapeDtypeStruct(share.shape, jnp.float32)] * 2,
        in_specs=[pl.BlockSpec(memory_space=pltpu.VMEM)] * len(operands),
        out_specs=[pl.BlockSpec(memory_space=pltpu.HBM), pl.BlockSpec(memory_space=pltpu.VMEM)],
        scratch_shapes=[
            pltpu.VMEM((layers - 1, *own_columns.shape), jnp.bfloat16),
            pltpu.SemaphoreType.DMA((half * pieces,)),
        ],
        input_output_aliases={len(operands) - 1: 1},
        compiler_params=pltpu.CompilerParams(vmem_limit_bytes=VMEM_BYTES),
        name="end_update",
    )(*operands)
    return result


def per_device(trailing, panel, inverse_factor):
    layers = lax.axis_size("layer")
    count = lax.axis_size("row")
    row_tiles, _, tile, col_tiles, _, _ = trailing.shape
    half = row_tiles // layers
    slots = plane_slots(count)
    factor = make_factor(panel, inverse_factor, half)
    moved = lax.ppermute(
        factor, ("row", "col"), [(a * count + b, slots[a][b] * count + a) for a in range(count) for b in range(count)]
    )
    share = load_share(factor, trailing.reshape(-1, LANES), layers)
    loaded_factor, share = lax.optimization_barrier((factor, share))
    line = gather_line(factor, loaded_factor, count)
    plane = [moved]
    for step in range(1, count):
        pairs = [
            (partner(a, plane_mates(count, b)[step], count) * count + b, a * count + b)
            for a in range(count)
            for b in range(count)
        ]
        plane.append(lax.ppermute(moved, ("row", "col"), pairs))
    others = []
    for shift in range(1, layers):
        pairs = [((l + shift) % layers, l) for l in range(layers)]
        others += [lax.ppermute(piece, "layer", pairs) for piece in plane]
    share, own_columns, near = begin_update(plane, line[:-1], share, layers, tile)
    rows = [line[0], near, *line[2:]]
    result = end_update(others, rows, own_columns, share, layers, tile)
    return result.reshape(half, 1, tile, col_tiles, 1, tile)


def solution(mesh):
    assert mesh.shape["row"] == mesh.shape["col"]
    return jax.shard_map(
        per_device,
        mesh=mesh,
        in_specs=(P(None, "row", None, None, "col", None), P(None, "row", "col", None), P()),
        out_specs=P("layer", "row", None, None, "col", None),
        check_vma=False,
    )
```

```python
import jax
import jax.numpy as jnp
from jax import lax
from jax.experimental import pallas as pl
from jax.experimental.pallas import tpu as pltpu
from jax.sharding import PartitionSpec as P

LANES = 128
VMEM_BYTES = 24 * 1024 * 1024
LOAD_VMEM_BYTES = 52000 * 1024
FACTOR_VMEM_BYTES = 55040 * 1024
AXES = ("row", "col", "layer")


def split(x):
    parts = []
    for _ in range(3):
        parts.append(x.astype(jnp.bfloat16))
        x = x - parts[-1].astype(jnp.float32)
    return parts


def factor_kernel(panel_ref, inverse_ref, factor_ref, panel_buf, inverse_buf, sems):
    half = factor_ref.shape[0]
    tile_rows = factor_ref.shape[1]
    width = factor_ref.shape[2]
    layer = lax.axis_index("layer")
    copies = [
        pltpu.make_async_copy(panel_ref.at[pl.ds(layer * half, half), 0], panel_buf, sems.at[0]),
        pltpu.make_async_copy(inverse_ref, inverse_buf, sems.at[1]),
    ]
    for copy in copies:
        copy.start()
    for copy in copies:
        copy.wait()
    rows = half * tile_rows
    panel = split(panel_buf[...].reshape(rows, width))
    inverse = split(inverse_buf[...])

    def times(parts, part):
        return lax.dot_general(
            jnp.concatenate(parts, axis=0), part, (((1,), (1,)), ((), ())), preferred_element_type=jnp.float32
        )

    high = times(panel, inverse[0])
    middle = times(panel[:2], inverse[1])
    low = times(panel[:1], inverse[2])
    product = (low + middle[rows:]) + high[2 * rows :]
    product = (product + (middle[:rows] + high[rows : 2 * rows])) + high[:rows]
    factor_ref[...] = product.astype(jnp.bfloat16).reshape(factor_ref.shape)


def make_factor(panel, inverse_factor, half):
    _, _, tile_rows, width = panel.shape
    return pl.pallas_call(
        factor_kernel,
        out_shape=jax.ShapeDtypeStruct((half, tile_rows, width), jnp.bfloat16),
        in_specs=[pl.BlockSpec(memory_space=pltpu.HBM)] * 2,
        out_specs=pl.BlockSpec(memory_space=pltpu.VMEM),
        scratch_shapes=[
            pltpu.VMEM((half, tile_rows, width), jnp.float32),
            pltpu.VMEM((width, width), jnp.float32),
            pltpu.SemaphoreType.DMA((2,)),
        ],
        compiler_params=pltpu.CompilerParams(vmem_limit_bytes=FACTOR_VMEM_BYTES),
        name="factor",
    )(panel, inverse_factor)


def partner(index, step, count):
    return index ^ step if count & (count - 1) == 0 else (index + step) % count


def plane_slots(count):
    if count == 4:
        return ((3, 0, 1, 2), (3, 2, 0, 1), (0, 2, 1, 3), (2, 3, 1, 0))
    return tuple(tuple(count - 1 - b for b in range(count)) for _ in range(count))


def plane_mates(count, plane):
    if count == 4:
        return (0, 1, 2, 3) if plane == 0 else (0, 2, 1, 3)
    return tuple(range(count))


def slab_of(slots, plane, place):
    if len(slots) == 4:
        packed = sum(row.index(p) << 2 * (4 * at + p) for at, row in enumerate(slots) for p in range(4))
        packed -= (packed >> 31) << 32
        return (jnp.int32(packed) >> (2 * (4 * plane + place))) & 3
    slab = jnp.int32(0)
    for at, row in enumerate(slots):
        for b, slot in enumerate(row):
            slab = jnp.where((plane == at) & (place == slot), b, slab)
    return slab


def line_steps(count):
    return (0, 2, 1, 3) if count == 4 else tuple(range(count))


def move(x, sources, count):
    return lax.ppermute(x, ("row", "col"), [(a * count + b, r * count + c) for (r, c), (a, b) in sources.items()])


def gather_line(factor, late_factor, moved, count):
    if count != 4:
        line = [factor]
        for step in range(1, count):
            line.append(lax.ppermute(factor, "col", [(partner(b, step, count), b) for b in range(count)]))
        return line
    places = [(r, c) for r in range(count) for c in range(count)]
    near = move(late_factor, {(r, c): (r ^ 1, c) if r == c else (r, c ^ 1) for r, c in places}, count)
    far = move(late_factor, {(r, c): (r ^ 2, c) if r == c else (r, c ^ 2) for r, c in places}, count)
    r, c = lax.axis_index("row"), lax.axis_index("col")
    odd = r % 2 == 1
    sent = jnp.where(~odd & (c == r ^ 3), near, far)
    sent = jnp.where(odd & (c == r), moved, sent)
    sent = jnp.where(~odd & (c == r ^ 1), late_factor, sent)
    cycle = {0: 0, 2: 1, 3: 2, 1: 3}
    last = move(sent, {(r, c): (r, c ^ 1) if r % 2 == 1 else (r, r ^ cycle[c ^ r]) for r, c in places}, count)
    return [factor, far, near, last]


def load_kernel(after_ref, lines_ref, share_ref, sem):
    rows = share_ref.shape[0]
    layer = lax.axis_index("layer")
    load = pltpu.make_async_copy(lines_ref.at[pl.ds(layer * rows, rows)], share_ref, sem)
    load.start()
    load.wait()


def load_share(after, lines, layers):
    rows = lines.shape[0] // layers
    return pl.pallas_call(
        load_kernel,
        out_shape=jax.ShapeDtypeStruct((rows, LANES), jnp.float32),
        in_specs=[pl.BlockSpec(memory_space=pl.ANY), pl.BlockSpec(memory_space=pltpu.HBM)],
        out_specs=pl.BlockSpec(memory_space=pltpu.VMEM),
        scratch_shapes=[pltpu.SemaphoreType.DMA],
        compiler_params=pltpu.CompilerParams(vmem_limit_bytes=LOAD_VMEM_BYTES),
        cost_estimate=pl.CostEstimate(flops=0, bytes_accessed=rows * LANES * 8, transcendentals=0),
        name="load_share",
    )(after, lines)


def fill_columns(columns_ref, pieces, slots, r, c, owner):
    half, tile_rows, _ = pieces[0].shape
    tile = tile_rows * len(pieces)
    for step, piece in enumerate(pieces):
        mate = jnp.where(c == 0, plane_mates(len(pieces), 0)[step], plane_mates(len(pieces), 1)[step])
        slab = slab_of(slots, c, partner(r, mate, len(pieces)))
        for k in range(half):
            at = pl.multiple_of(k * tile + slab * tile_rows, tile_rows)
            columns_ref[pl.ds(at, tile_rows), :] = piece[k]


def subtract_product(share_ref, rows, columns, tile, first_row, first_line, per_row):
    half, tile_rows, width = rows.shape
    product = lax.dot_general(
        rows.reshape(half * tile_rows, width),
        columns,
        (((1,), (1,)), ((), ())),
        preferred_element_type=jnp.float32,
    )
    for k in range(half):
        for part in range(product.shape[1] // LANES):
            start = (k * tile + first_row) * per_row + first_line + part
            at = pl.ds(start, tile_rows, stride=per_row)
            share_ref[at, :] -= product[k * tile_rows : (k + 1) * tile_rows, part * LANES : (part + 1) * LANES]


def take_rows(rows_ref, columns_ref, c, step, pieces):
    half, tile_rows, _ = rows_ref.shape
    for k in range(half):
        at = pl.multiple_of((k * pieces + partner(c, step, pieces)) * tile_rows, tile_rows)
        rows_ref[k] = columns_ref[pl.ds(at, tile_rows), :]


def begin_kernel(pieces, layers, tile, *refs):
    column_refs, row_refs, rest = refs[:pieces], refs[pieces : 2 * pieces - 1], refs[2 * pieces - 1 :]
    _, share_ref, columns_ref, *line_refs = rest
    r, c, layer = (lax.axis_index(axis) for axis in AXES)
    half, tile_rows, _ = row_refs[0].shape
    own_lines = half * tile // LANES
    fill_columns(columns_ref, column_refs, plane_slots(pieces), r, c, layer)
    for line_ref, row_ref in zip(line_refs, row_refs[1:]):
        line_ref[...] = row_ref[...]
    if pieces == 4:

        @pl.when(r == c)
        def _():
            for step, line_ref in zip(line_steps(pieces)[1:], line_refs):
                take_rows(line_ref, columns_ref, c, step, pieces)

    for step, row_ref in zip(line_steps(pieces), (row_refs[0], *line_refs)):
        first_row = partner(c, step, pieces) * tile_rows
        subtract_product(
            share_ref, row_ref[...], columns_ref[...], tile, first_row, layer * own_lines, layers * own_lines
        )


def begin_update(column_pieces, row_pieces, share, layers, tile):
    pieces = len(column_pieces)
    half, _, width = row_pieces[0].shape

    def body(*refs):
        begin_kernel(pieces, layers, tile, *refs)

    return pl.pallas_call(
        body,
        out_shape=[
            jax.ShapeDtypeStruct(share.shape, jnp.float32),
            jax.ShapeDtypeStruct((half * tile, width), jnp.bfloat16),
            *[jax.ShapeDtypeStruct(row_pieces[0].shape, jnp.bfloat16)] * (pieces - 2),
        ],
        in_specs=[pl.BlockSpec(memory_space=pltpu.VMEM)] * (2 * pieces),
        out_specs=[pl.BlockSpec(memory_space=pltpu.VMEM)] * pieces,
        input_output_aliases={2 * pieces - 1: 0},
        compiler_params=pltpu.CompilerParams(vmem_limit_bytes=VMEM_BYTES),
        name="begin_update",
    )(*column_pieces, *row_pieces, share)


def end_kernel(pieces, layers, tile, *refs):
    others = pieces * (layers - 1)
    column_refs, row_refs, rest = refs[:others], refs[others : others + pieces], refs[others + pieces :]
    own_ref, _, out_ref, share_ref, columns_buf, last_buf, sems = rest
    r, c, layer = (lax.axis_index(axis) for axis in AXES)
    half, tile_rows, _ = row_refs[0].shape
    own_lines = half * tile // LANES
    per_row = layers * own_lines
    owners = [lax.rem(layer + shift, layers) for shift in range(1, layers)]
    for at, owner in enumerate(owners):
        fill_columns(
            columns_buf.at[at], column_refs[at * pieces : (at + 1) * pieces], plane_slots(pieces), r, c, owner
        )
    last_buf[...] = row_refs[-1][...]
    if pieces == 4:

        @pl.when(r == c)
        def _():
            take_rows(last_buf, own_ref, c, line_steps(pieces)[-1], pieces)

    stores = []
    for at_row, row_ref in enumerate((*row_refs[:-1], last_buf)):
        first_row = partner(c, line_steps(pieces)[at_row], pieces) * tile_rows
        rows = row_ref[...]
        for at, owner in enumerate(owners):
            subtract_product(share_ref, rows, columns_buf[at], tile, first_row, owner * own_lines, per_row)
        if at_row == pieces - 1:
            subtract_product(share_ref, rows, own_ref[...], tile, first_row, layer * own_lines, per_row)
        for k in range(half):
            lines = tile_rows * per_row
            start = pl.multiple_of((k * tile + first_row) * per_row, lines)
            store = pltpu.make_async_copy(
                share_ref.at[pl.ds(start, lines)], out_ref.at[pl.ds(start, lines)], sems.at[at_row * half + k]
            )
            store.start()
            stores.append(store)
    for store in stores:
        store.wait()


def end_update(column_pieces, row_pieces, own_columns, share, layers, tile):
    pieces = len(row_pieces)
    half = row_pieces[0].shape[0]
    operands = (*column_pieces, *row_pieces, own_columns, share)

    def body(*refs):
        end_kernel(pieces, layers, tile, *refs)

    result, _ = pl.pallas_call(
        body,
        out_shape=[jax.ShapeDtypeStruct(share.shape, jnp.float32)] * 2,
        in_specs=[pl.BlockSpec(memory_space=pltpu.VMEM)] * len(operands),
        out_specs=[pl.BlockSpec(memory_space=pltpu.HBM), pl.BlockSpec(memory_space=pltpu.VMEM)],
        scratch_shapes=[
            pltpu.VMEM((layers - 1, *own_columns.shape), jnp.bfloat16),
            pltpu.VMEM(row_pieces[0].shape, jnp.bfloat16),
            pltpu.SemaphoreType.DMA((half * pieces,)),
        ],
        input_output_aliases={len(operands) - 1: 1},
        compiler_params=pltpu.CompilerParams(vmem_limit_bytes=VMEM_BYTES),
        name="end_update",
    )(*operands)
    return result


def per_device(trailing, panel, inverse_factor):
    layers = lax.axis_size("layer")
    count = lax.axis_size("row")
    row_tiles, _, tile, col_tiles, _, _ = trailing.shape
    half = row_tiles // layers
    slots = plane_slots(count)
    factor = make_factor(panel, inverse_factor, half)
    moved = lax.ppermute(
        factor, ("row", "col"), [(a * count + b, slots[a][b] * count + a) for a in range(count) for b in range(count)]
    )
    share = load_share(factor, trailing.reshape(-1, LANES), layers)
    loaded_factor, share = lax.optimization_barrier((factor, share))
    line = gather_line(factor, loaded_factor, moved, count)
    plane = [moved]
    for step in range(1, count):
        pairs = [
            (partner(a, plane_mates(count, b)[step], count) * count + b, a * count + b)
            for a in range(count)
            for b in range(count)
        ]
        plane.append(lax.ppermute(moved, ("row", "col"), pairs))
    others = []
    for shift in range(1, layers):
        pairs = [((l + shift) % layers, l) for l in range(layers)]
        others += [lax.ppermute(piece, "layer", pairs) for piece in plane]
    share, own_columns, *rows = begin_update(plane, line[:-1], share, layers, tile)
    rows = [line[0], *rows, line[-1]]
    result = end_update(others, rows, own_columns, share, layers, tile)
    return result.reshape(half, 1, tile, col_tiles, 1, tile)


def solution(mesh):
    assert mesh.shape["row"] == mesh.shape["col"]
    return jax.shard_map(
        per_device,
        mesh=mesh,
        in_specs=(P(None, "row", None, None, "col", None), P(None, "row", "col", None), P()),
        out_specs=P("layer", "row", None, None, "col", None),
        check_vma=False,
    )
```

```python
import jax
import jax.numpy as jnp
from jax import lax
from jax.experimental import pallas as pl
from jax.experimental.pallas import tpu as pltpu
from jax.sharding import PartitionSpec as P

LANES = 128
VMEM_BYTES = 24 * 1024 * 1024
LOAD_VMEM_BYTES = 52000 * 1024
FACTOR_VMEM_BYTES = 55040 * 1024
AXES = ("row", "col", "layer")


def split(x):
    parts = []
    for _ in range(3):
        parts.append(x.astype(jnp.bfloat16))
        x = x - parts[-1].astype(jnp.float32)
    return parts


def factor_kernel(panel_ref, inverse_ref, factor_ref, panel_buf, inverse_buf, sems):
    half = factor_ref.shape[0]
    tile_rows = factor_ref.shape[1]
    width = factor_ref.shape[2]
    layer = lax.axis_index("layer")
    copies = [
        pltpu.make_async_copy(panel_ref.at[pl.ds(layer * half, half), 0], panel_buf, sems.at[0]),
        pltpu.make_async_copy(inverse_ref, inverse_buf, sems.at[1]),
    ]
    for copy in copies:
        copy.start()
    for copy in copies:
        copy.wait()
    rows = half * tile_rows
    panel = split(panel_buf[...].reshape(rows, width))
    inverse = split(inverse_buf[...])

    def times(parts, part):
        return lax.dot_general(
            jnp.concatenate(parts, axis=0), part, (((1,), (1,)), ((), ())), preferred_element_type=jnp.float32
        )

    high = times(panel, inverse[0])
    middle = times(panel[:2], inverse[1])
    low = times(panel[:1], inverse[2])
    product = (low + middle[rows:]) + high[2 * rows :]
    product = (product + (middle[:rows] + high[rows : 2 * rows])) + high[:rows]
    factor_ref[...] = product.astype(jnp.bfloat16).reshape(factor_ref.shape)


def make_factor(panel, inverse_factor, half):
    _, _, tile_rows, width = panel.shape
    return pl.pallas_call(
        factor_kernel,
        out_shape=jax.ShapeDtypeStruct((half, tile_rows, width), jnp.bfloat16),
        in_specs=[pl.BlockSpec(memory_space=pltpu.HBM)] * 2,
        out_specs=pl.BlockSpec(memory_space=pltpu.VMEM),
        scratch_shapes=[
            pltpu.VMEM((half, tile_rows, width), jnp.float32),
            pltpu.VMEM((width, width), jnp.float32),
            pltpu.SemaphoreType.DMA((2,)),
        ],
        compiler_params=pltpu.CompilerParams(vmem_limit_bytes=FACTOR_VMEM_BYTES),
        name="factor",
    )(panel, inverse_factor)


def partner(index, step, count):
    return index ^ step if count & (count - 1) == 0 else (index + step) % count


def plane_slots(count):
    if count == 4:
        return ((3, 0, 1, 2), (3, 2, 0, 1), (0, 2, 1, 3), (2, 3, 1, 0))
    return tuple(tuple(count - 1 - b for b in range(count)) for _ in range(count))


def plane_mates(count, plane):
    if count == 4:
        return (0, 1, 2, 3) if plane == 0 else (0, 2, 1, 3)
    return tuple(range(count))


def slab_of(slots, plane, place):
    if len(slots) == 4:
        packed = sum(row.index(p) << 2 * (4 * at + p) for at, row in enumerate(slots) for p in range(4))
        packed -= (packed >> 31) << 32
        return (jnp.int32(packed) >> (2 * (4 * plane + place))) & 3
    slab = jnp.int32(0)
    for at, row in enumerate(slots):
        for b, slot in enumerate(row):
            slab = jnp.where((plane == at) & (place == slot), b, slab)
    return slab


def line_steps(count):
    return (0, 2, 1, 3) if count == 4 else tuple(range(count))


def move(x, sources, count):
    return lax.ppermute(x, ("row", "col"), [(a * count + b, r * count + c) for (r, c), (a, b) in sources.items()])


def gather_line(factor, late_factor, moved, count):
    if count != 4:
        line = [factor]
        for step in range(1, count):
            line.append(lax.ppermute(factor, "col", [(partner(b, step, count), b) for b in range(count)]))
        return line
    places = [(r, c) for r in range(count) for c in range(count)]
    near = move(late_factor, {(r, c): (r ^ 1, c) if r == c else (r, c ^ 1) for r, c in places}, count)
    far = move(late_factor, {(r, c): (r ^ 2, c) if r == c and r % 2 == 1 else (r, c ^ 2) for r, c in places}, count)
    r, c = lax.axis_index("row"), lax.axis_index("col")
    relayed = jnp.where((r == c) & (r % 2 == 1), moved, far)
    relayed = jnp.where(r == c ^ 1, near, relayed)
    last = move(relayed, {(r, c): (r, c ^ 1) for r, c in places}, count)
    return [factor, far, near, last]


def load_kernel(after_ref, lines_ref, share_ref, sem):
    rows = share_ref.shape[0]
    layer = lax.axis_index("layer")
    load = pltpu.make_async_copy(lines_ref.at[pl.ds(layer * rows, rows)], share_ref, sem)
    load.start()
    load.wait()


def load_share(after, lines, layers):
    rows = lines.shape[0] // layers
    return pl.pallas_call(
        load_kernel,
        out_shape=jax.ShapeDtypeStruct((rows, LANES), jnp.float32),
        in_specs=[pl.BlockSpec(memory_space=pl.ANY), pl.BlockSpec(memory_space=pltpu.HBM)],
        out_specs=pl.BlockSpec(memory_space=pltpu.VMEM),
        scratch_shapes=[pltpu.SemaphoreType.DMA],
        compiler_params=pltpu.CompilerParams(vmem_limit_bytes=LOAD_VMEM_BYTES),
        cost_estimate=pl.CostEstimate(flops=0, bytes_accessed=rows * LANES * 8, transcendentals=0),
        name="load_share",
    )(after, lines)


def fill_columns(columns_ref, pieces, slots, r, c, owner):
    half, tile_rows, _ = pieces[0].shape
    tile = tile_rows * len(pieces)
    for step, piece in enumerate(pieces):
        mate = jnp.where(c == 0, plane_mates(len(pieces), 0)[step], plane_mates(len(pieces), 1)[step])
        slab = slab_of(slots, c, partner(r, mate, len(pieces)))
        for k in range(half):
            at = pl.multiple_of(k * tile + slab * tile_rows, tile_rows)
            columns_ref[pl.ds(at, tile_rows), :] = piece[k]


def subtract_product(share_ref, rows, columns, tile, first_row, first_line, per_row):
    half, tile_rows, width = rows.shape
    product = lax.dot_general(
        rows.reshape(half * tile_rows, width),
        columns,
        (((1,), (1,)), ((), ())),
        preferred_element_type=jnp.float32,
    )
    for k in range(half):
        for part in range(product.shape[1] // LANES):
            start = (k * tile + first_row) * per_row + first_line + part
            at = pl.ds(start, tile_rows, stride=per_row)
            share_ref[at, :] -= product[k * tile_rows : (k + 1) * tile_rows, part * LANES : (part + 1) * LANES]


def take_rows(rows_ref, columns_ref, c, step, pieces):
    half, tile_rows, _ = rows_ref.shape
    for k in range(half):
        at = pl.multiple_of((k * pieces + partner(c, step, pieces)) * tile_rows, tile_rows)
        rows_ref[k] = columns_ref[pl.ds(at, tile_rows), :]


def begin_kernel(pieces, layers, tile, *refs):
    column_refs, row_refs, rest = refs[:pieces], refs[pieces : 2 * pieces - 1], refs[2 * pieces - 1 :]
    _, share_ref, columns_ref, *line_refs = rest
    r, c, layer = (lax.axis_index(axis) for axis in AXES)
    half, tile_rows, _ = row_refs[0].shape
    own_lines = half * tile // LANES
    fill_columns(columns_ref, column_refs, plane_slots(pieces), r, c, layer)
    for line_ref, row_ref in zip(line_refs, row_refs[1:]):
        line_ref[...] = row_ref[...]
    if pieces == 4:

        @pl.when(r == c)
        def _():
            for step, line_ref in zip(line_steps(pieces)[1:], line_refs):
                take_rows(line_ref, columns_ref, c, step, pieces)

    for step, row_ref in zip(line_steps(pieces), (row_refs[0], *line_refs)):
        first_row = partner(c, step, pieces) * tile_rows
        subtract_product(
            share_ref, row_ref[...], columns_ref[...], tile, first_row, layer * own_lines, layers * own_lines
        )


def begin_update(column_pieces, row_pieces, share, layers, tile):
    pieces = len(column_pieces)
    half, _, width = row_pieces[0].shape

    def body(*refs):
        begin_kernel(pieces, layers, tile, *refs)

    return pl.pallas_call(
        body,
        out_shape=[
            jax.ShapeDtypeStruct(share.shape, jnp.float32),
            jax.ShapeDtypeStruct((half * tile, width), jnp.bfloat16),
            *[jax.ShapeDtypeStruct(row_pieces[0].shape, jnp.bfloat16)] * (pieces - 2),
        ],
        in_specs=[pl.BlockSpec(memory_space=pltpu.VMEM)] * (2 * pieces),
        out_specs=[pl.BlockSpec(memory_space=pltpu.VMEM)] * pieces,
        input_output_aliases={2 * pieces - 1: 0},
        compiler_params=pltpu.CompilerParams(vmem_limit_bytes=VMEM_BYTES),
        name="begin_update",
    )(*column_pieces, *row_pieces, share)


def end_kernel(pieces, layers, tile, *refs):
    others = pieces * (layers - 1)
    column_refs, row_refs, rest = refs[:others], refs[others : others + pieces], refs[others + pieces :]
    own_ref, _, out_ref, share_ref, columns_buf, last_buf, sems = rest
    r, c, layer = (lax.axis_index(axis) for axis in AXES)
    half, tile_rows, _ = row_refs[0].shape
    own_lines = half * tile // LANES
    per_row = layers * own_lines
    owners = [lax.rem(layer + shift, layers) for shift in range(1, layers)]
    for at, owner in enumerate(owners):
        fill_columns(
            columns_buf.at[at], column_refs[at * pieces : (at + 1) * pieces], plane_slots(pieces), r, c, owner
        )
    last_buf[...] = row_refs[-1][...]
    if pieces == 4:

        @pl.when(r == c)
        def _():
            take_rows(last_buf, own_ref, c, line_steps(pieces)[-1], pieces)

    stores = []
    for at_row, row_ref in enumerate((*row_refs[:-1], last_buf)):
        first_row = partner(c, line_steps(pieces)[at_row], pieces) * tile_rows
        rows = row_ref[...]
        for at, owner in enumerate(owners):
            subtract_product(share_ref, rows, columns_buf[at], tile, first_row, owner * own_lines, per_row)
        if at_row == pieces - 1:
            subtract_product(share_ref, rows, own_ref[...], tile, first_row, layer * own_lines, per_row)
        for k in range(half):
            lines = tile_rows * per_row
            start = pl.multiple_of((k * tile + first_row) * per_row, lines)
            store = pltpu.make_async_copy(
                share_ref.at[pl.ds(start, lines)], out_ref.at[pl.ds(start, lines)], sems.at[at_row * half + k]
            )
            store.start()
            stores.append(store)
    for store in stores:
        store.wait()


def end_update(column_pieces, row_pieces, own_columns, share, layers, tile):
    pieces = len(row_pieces)
    half = row_pieces[0].shape[0]
    operands = (*column_pieces, *row_pieces, own_columns, share)

    def body(*refs):
        end_kernel(pieces, layers, tile, *refs)

    result, _ = pl.pallas_call(
        body,
        out_shape=[jax.ShapeDtypeStruct(share.shape, jnp.float32)] * 2,
        in_specs=[pl.BlockSpec(memory_space=pltpu.VMEM)] * len(operands),
        out_specs=[pl.BlockSpec(memory_space=pltpu.HBM), pl.BlockSpec(memory_space=pltpu.VMEM)],
        scratch_shapes=[
            pltpu.VMEM((layers - 1, *own_columns.shape), jnp.bfloat16),
            pltpu.VMEM(row_pieces[0].shape, jnp.bfloat16),
            pltpu.SemaphoreType.DMA((half * pieces,)),
        ],
        input_output_aliases={len(operands) - 1: 1},
        compiler_params=pltpu.CompilerParams(vmem_limit_bytes=VMEM_BYTES),
        name="end_update",
    )(*operands)
    return result


def per_device(trailing, panel, inverse_factor):
    layers = lax.axis_size("layer")
    count = lax.axis_size("row")
    row_tiles, _, tile, col_tiles, _, _ = trailing.shape
    half = row_tiles // layers
    slots = plane_slots(count)
    factor = make_factor(panel, inverse_factor, half)
    moved = lax.ppermute(
        factor, ("row", "col"), [(a * count + b, slots[a][b] * count + a) for a in range(count) for b in range(count)]
    )
    share = load_share(factor, trailing.reshape(-1, LANES), layers)
    loaded_factor, share = lax.optimization_barrier((factor, share))
    line = gather_line(factor, loaded_factor, moved, count)
    plane = [moved]
    for step in range(1, count):
        pairs = [
            (partner(a, plane_mates(count, b)[step], count) * count + b, a * count + b)
            for a in range(count)
            for b in range(count)
        ]
        plane.append(lax.ppermute(moved, ("row", "col"), pairs))
    others = []
    for shift in range(1, layers):
        pairs = [((l + shift) % layers, l) for l in range(layers)]
        others += [lax.ppermute(piece, "layer", pairs) for piece in plane]
    share, own_columns, *rows = begin_update(plane, line[:-1], share, layers, tile)
    rows = [line[0], *rows, line[-1]]
    result = end_update(others, rows, own_columns, share, layers, tile)
    return result.reshape(half, 1, tile, col_tiles, 1, tile)


def solution(mesh):
    assert mesh.shape["row"] == mesh.shape["col"]
    return jax.shard_map(
        per_device,
        mesh=mesh,
        in_specs=(P(None, "row", None, None, "col", None), P(None, "row", "col", None), P()),
        out_specs=P("layer", "row", None, None, "col", None),
        check_vma=False,
    )
```

```python
import jax
import jax.numpy as jnp
from jax import lax
from jax.experimental import pallas as pl
from jax.experimental.pallas import tpu as pltpu
from jax.sharding import PartitionSpec as P

LANES = 128
VMEM_BYTES = 24 * 1024 * 1024
LOAD_VMEM_BYTES = 52000 * 1024
FACTOR_VMEM_BYTES = 55040 * 1024
AXES = ("row", "col", "layer")


def split(x):
    parts = []
    for _ in range(3):
        parts.append(x.astype(jnp.bfloat16))
        x = x - parts[-1].astype(jnp.float32)
    return parts


def factor_kernel(panel_ref, inverse_ref, factor_ref, panel_buf, inverse_buf, sems):
    half = factor_ref.shape[0]
    tile_rows = factor_ref.shape[1]
    width = factor_ref.shape[2]
    layer = lax.axis_index("layer")
    copies = [
        pltpu.make_async_copy(panel_ref.at[pl.ds(layer * half, half), 0], panel_buf, sems.at[0]),
        pltpu.make_async_copy(inverse_ref, inverse_buf, sems.at[1]),
    ]
    for copy in copies:
        copy.start()
    for copy in copies:
        copy.wait()
    rows = half * tile_rows
    panel = split(panel_buf[...].reshape(rows, width))
    inverse = split(inverse_buf[...])

    def times(parts, part):
        return lax.dot_general(
            jnp.concatenate(parts, axis=0), part, (((1,), (1,)), ((), ())), preferred_element_type=jnp.float32
        )

    high = times(panel, inverse[0])
    middle = times(panel[:2], inverse[1])
    low = times(panel[:1], inverse[2])
    product = (low + middle[rows:]) + high[2 * rows :]
    product = (product + (middle[:rows] + high[rows : 2 * rows])) + high[:rows]
    factor_ref[...] = product.astype(jnp.bfloat16).reshape(factor_ref.shape)


def make_factor(panel, inverse_factor, half):
    _, _, tile_rows, width = panel.shape
    return pl.pallas_call(
        factor_kernel,
        out_shape=jax.ShapeDtypeStruct((half, tile_rows, width), jnp.bfloat16),
        in_specs=[pl.BlockSpec(memory_space=pltpu.HBM)] * 2,
        out_specs=pl.BlockSpec(memory_space=pltpu.VMEM),
        scratch_shapes=[
            pltpu.VMEM((half, tile_rows, width), jnp.float32),
            pltpu.VMEM((width, width), jnp.float32),
            pltpu.SemaphoreType.DMA((2,)),
        ],
        compiler_params=pltpu.CompilerParams(vmem_limit_bytes=FACTOR_VMEM_BYTES),
        name="factor",
    )(panel, inverse_factor)


def partner(index, step, count):
    return index ^ step if count & (count - 1) == 0 else (index + step) % count


def plane_slots(count):
    if count == 4:
        return ((3, 0, 1, 2), (3, 0, 2, 1), (0, 2, 1, 3), (2, 3, 1, 0))
    return tuple(tuple(count - 1 - b for b in range(count)) for _ in range(count))


def plane_mates(count, plane):
    if count == 4:
        return ((0, 3, 1, 2), (0, 1, 2, 3), (0, 2, 1, 3), (0, 2, 1, 3))[plane]
    return tuple(range(count))


def slab_of(slots, plane, place):
    if len(slots) == 4:
        packed = sum(row.index(p) << 2 * (4 * at + p) for at, row in enumerate(slots) for p in range(4))
        packed -= (packed >> 31) << 32
        return (jnp.int32(packed) >> (2 * (4 * plane + place))) & 3
    slab = jnp.int32(0)
    for at, row in enumerate(slots):
        for b, slot in enumerate(row):
            slab = jnp.where((plane == at) & (place == slot), b, slab)
    return slab


def line_steps(count):
    return (0, 2, 1, 3) if count == 4 else tuple(range(count))


def move(x, sources, count):
    return lax.ppermute(x, ("row", "col"), [(a * count + b, r * count + c) for (r, c), (a, b) in sources.items()])


def gather_line(factor, late_factor, moved, count):
    if count != 4:
        line = [factor]
        for step in range(1, count):
            line.append(lax.ppermute(factor, "col", [(partner(b, step, count), b) for b in range(count)]))
        return line
    places = [(r, c) for r in range(count) for c in range(count)]
    near = move(late_factor, {(r, c): (r ^ 1, c) if r == c else (r, c ^ 1) for r, c in places}, count)
    far = move(late_factor, {(r, c): (r ^ 2, c) if r == c and r % 2 == 1 else (r, c ^ 2) for r, c in places}, count)
    r, c = lax.axis_index("row"), lax.axis_index("col")
    relayed = jnp.where((r == c) & (r % 2 == 1), moved, far)
    relayed = jnp.where(r == c ^ 1, near, relayed)
    last = move(relayed, {(r, c): (r, c ^ 1) for r, c in places}, count)
    return [factor, far, near, last]


def load_kernel(after_ref, lines_ref, share_ref, sem):
    rows = share_ref.shape[0]
    layer = lax.axis_index("layer")
    load = pltpu.make_async_copy(lines_ref.at[pl.ds(layer * rows, rows)], share_ref, sem)
    load.start()
    load.wait()


def load_share(after, lines, layers):
    rows = lines.shape[0] // layers
    return pl.pallas_call(
        load_kernel,
        out_shape=jax.ShapeDtypeStruct((rows, LANES), jnp.float32),
        in_specs=[pl.BlockSpec(memory_space=pl.ANY), pl.BlockSpec(memory_space=pltpu.HBM)],
        out_specs=pl.BlockSpec(memory_space=pltpu.VMEM),
        scratch_shapes=[pltpu.SemaphoreType.DMA],
        compiler_params=pltpu.CompilerParams(vmem_limit_bytes=LOAD_VMEM_BYTES),
        cost_estimate=pl.CostEstimate(flops=0, bytes_accessed=rows * LANES * 8, transcendentals=0),
        name="load_share",
    )(after, lines)


def fill_columns(columns_ref, pieces, slots, r, c, owner):
    half, tile_rows, _ = pieces[0].shape
    tile = tile_rows * len(pieces)
    for step, piece in enumerate(pieces):
        mate = jnp.int32(plane_mates(len(pieces), 0)[step])
        for plane in range(1, len(pieces) if len(pieces) == 4 else 1):
            mate = jnp.where(c == plane, plane_mates(len(pieces), plane)[step], mate)
        slab = slab_of(slots, c, partner(r, mate, len(pieces)))
        for k in range(half):
            at = pl.multiple_of(k * tile + slab * tile_rows, tile_rows)
            columns_ref[pl.ds(at, tile_rows), :] = piece[k]


def subtract_product(share_ref, rows, columns, tile, first_row, first_line, per_row):
    half, tile_rows, width = rows.shape
    product = lax.dot_general(
        rows.reshape(half * tile_rows, width),
        columns,
        (((1,), (1,)), ((), ())),
        preferred_element_type=jnp.float32,
    )
    for k in range(half):
        for part in range(product.shape[1] // LANES):
            start = (k * tile + first_row) * per_row + first_line + part
            at = pl.ds(start, tile_rows, stride=per_row)
            share_ref[at, :] -= product[k * tile_rows : (k + 1) * tile_rows, part * LANES : (part + 1) * LANES]


def take_rows(rows_ref, columns_ref, c, step, pieces):
    half, tile_rows, _ = rows_ref.shape
    for k in range(half):
        at = pl.multiple_of((k * pieces + partner(c, step, pieces)) * tile_rows, tile_rows)
        rows_ref[k] = columns_ref[pl.ds(at, tile_rows), :]


def begin_kernel(pieces, layers, tile, *refs):
    column_refs, row_refs, rest = refs[:pieces], refs[pieces : 2 * pieces - 1], refs[2 * pieces - 1 :]
    _, share_ref, columns_ref, *line_refs = rest
    r, c, layer = (lax.axis_index(axis) for axis in AXES)
    half, tile_rows, _ = row_refs[0].shape
    own_lines = half * tile // LANES
    fill_columns(columns_ref, column_refs, plane_slots(pieces), r, c, layer)
    for line_ref, row_ref in zip(line_refs, row_refs[1:]):
        line_ref[...] = row_ref[...]
    if pieces == 4:

        @pl.when(r == c)
        def _():
            for step, line_ref in zip(line_steps(pieces)[1:], line_refs):
                take_rows(line_ref, columns_ref, c, step, pieces)

    for step, row_ref in zip(line_steps(pieces), (row_refs[0], *line_refs)):
        first_row = partner(c, step, pieces) * tile_rows
        subtract_product(
            share_ref, row_ref[...], columns_ref[...], tile, first_row, layer * own_lines, layers * own_lines
        )


def begin_update(column_pieces, row_pieces, share, layers, tile):
    pieces = len(column_pieces)
    half, _, width = row_pieces[0].shape

    def body(*refs):
        begin_kernel(pieces, layers, tile, *refs)

    return pl.pallas_call(
        body,
        out_shape=[
            jax.ShapeDtypeStruct(share.shape, jnp.float32),
            jax.ShapeDtypeStruct((half * tile, width), jnp.bfloat16),
            *[jax.ShapeDtypeStruct(row_pieces[0].shape, jnp.bfloat16)] * (pieces - 2),
        ],
        in_specs=[pl.BlockSpec(memory_space=pltpu.VMEM)] * (2 * pieces),
        out_specs=[pl.BlockSpec(memory_space=pltpu.VMEM)] * pieces,
        input_output_aliases={2 * pieces - 1: 0},
        compiler_params=pltpu.CompilerParams(vmem_limit_bytes=VMEM_BYTES),
        name="begin_update",
    )(*column_pieces, *row_pieces, share)


def end_kernel(pieces, layers, tile, *refs):
    others = pieces * (layers - 1)
    column_refs, row_refs, rest = refs[:others], refs[others : others + pieces], refs[others + pieces :]
    own_ref, _, out_ref, share_ref, columns_buf, last_buf, sems = rest
    r, c, layer = (lax.axis_index(axis) for axis in AXES)
    half, tile_rows, _ = row_refs[0].shape
    own_lines = half * tile // LANES
    per_row = layers * own_lines
    owners = [lax.rem(layer + shift, layers) for shift in range(1, layers)]
    for at, owner in enumerate(owners):
        fill_columns(
            columns_buf.at[at], column_refs[at * pieces : (at + 1) * pieces], plane_slots(pieces), r, c, owner
        )
    last_buf[...] = row_refs[-1][...]
    if pieces == 4:

        @pl.when(r == c)
        def _():
            take_rows(last_buf, own_ref, c, line_steps(pieces)[-1], pieces)

    stores = []
    for at_row, row_ref in enumerate((*row_refs[:-1], last_buf)):
        first_row = partner(c, line_steps(pieces)[at_row], pieces) * tile_rows
        rows = row_ref[...]
        for at, owner in enumerate(owners):
            subtract_product(share_ref, rows, columns_buf[at], tile, first_row, owner * own_lines, per_row)
        if at_row == pieces - 1:
            subtract_product(share_ref, rows, own_ref[...], tile, first_row, layer * own_lines, per_row)
        for k in range(half):
            lines = tile_rows * per_row
            start = pl.multiple_of((k * tile + first_row) * per_row, lines)
            store = pltpu.make_async_copy(
                share_ref.at[pl.ds(start, lines)], out_ref.at[pl.ds(start, lines)], sems.at[at_row * half + k]
            )
            store.start()
            stores.append(store)
    for store in stores:
        store.wait()


def end_update(column_pieces, row_pieces, own_columns, share, layers, tile):
    pieces = len(row_pieces)
    half = row_pieces[0].shape[0]
    operands = (*column_pieces, *row_pieces, own_columns, share)

    def body(*refs):
        end_kernel(pieces, layers, tile, *refs)

    result, _ = pl.pallas_call(
        body,
        out_shape=[jax.ShapeDtypeStruct(share.shape, jnp.float32)] * 2,
        in_specs=[pl.BlockSpec(memory_space=pltpu.VMEM)] * len(operands),
        out_specs=[pl.BlockSpec(memory_space=pltpu.HBM), pl.BlockSpec(memory_space=pltpu.VMEM)],
        scratch_shapes=[
            pltpu.VMEM((layers - 1, *own_columns.shape), jnp.bfloat16),
            pltpu.VMEM(row_pieces[0].shape, jnp.bfloat16),
            pltpu.SemaphoreType.DMA((half * pieces,)),
        ],
        input_output_aliases={len(operands) - 1: 1},
        compiler_params=pltpu.CompilerParams(vmem_limit_bytes=VMEM_BYTES),
        name="end_update",
    )(*operands)
    return result


def per_device(trailing, panel, inverse_factor):
    layers = lax.axis_size("layer")
    count = lax.axis_size("row")
    row_tiles, _, tile, col_tiles, _, _ = trailing.shape
    half = row_tiles // layers
    slots = plane_slots(count)
    factor = make_factor(panel, inverse_factor, half)
    moved = lax.ppermute(
        factor, ("row", "col"), [(a * count + b, slots[a][b] * count + a) for a in range(count) for b in range(count)]
    )
    share = load_share(factor, trailing.reshape(-1, LANES), layers)
    loaded_factor, share = lax.optimization_barrier((factor, share))
    line = gather_line(factor, loaded_factor, moved, count)
    plane = [moved]
    for step in range(1, count):
        sources = {
            (r, c): (partner(r, plane_mates(count, c)[step], count), c) for r in range(count) for c in range(count)
        }
        if count == 4 and step == 1:
            sources[0, 0], sources[1, 1] = (0, 1), (3, 0)
        plane.append(move(moved, sources, count))
    if count == 4:
        r, c = lax.axis_index("row"), lax.axis_index("col")
        plane[1] = jnp.where((r == c) & (r < 2), factor, plane[1])
    others = []
    for shift in range(1, layers):
        pairs = [((l + shift) % layers, l) for l in range(layers)]
        others += [lax.ppermute(piece, "layer", pairs) for piece in plane]
    share, own_columns, *rows = begin_update(plane, line[:-1], share, layers, tile)
    rows = [line[0], *rows, line[-1]]
    result = end_update(others, rows, own_columns, share, layers, tile)
    return result.reshape(half, 1, tile, col_tiles, 1, tile)


def solution(mesh):
    assert mesh.shape["row"] == mesh.shape["col"]
    return jax.shard_map(
        per_device,
        mesh=mesh,
        in_specs=(P(None, "row", None, None, "col", None), P(None, "row", "col", None), P()),
        out_specs=P("layer", "row", None, None, "col", None),
        check_vma=False,
    )
```

```python
import jax
import jax.numpy as jnp
from jax import lax
from jax.experimental import pallas as pl
from jax.experimental.pallas import tpu as pltpu
from jax.sharding import PartitionSpec as P

LANES = 128
VMEM_BYTES = 24 * 1024 * 1024
LOAD_VMEM_BYTES = 52000 * 1024
FACTOR_VMEM_BYTES = 55040 * 1024
AXES = ("row", "col", "layer")


def split(x):
    parts = []
    for _ in range(3):
        parts.append(x.astype(jnp.bfloat16))
        x = x - parts[-1].astype(jnp.float32)
    return parts


def factor_kernel(panel_ref, inverse_ref, factor_ref, panel_buf, inverse_buf, sems):
    half = factor_ref.shape[0]
    tile_rows = factor_ref.shape[1]
    width = factor_ref.shape[2]
    layer = lax.axis_index("layer")
    copies = [
        pltpu.make_async_copy(panel_ref.at[pl.ds(layer * half, half), 0], panel_buf, sems.at[0]),
        pltpu.make_async_copy(inverse_ref, inverse_buf, sems.at[1]),
    ]
    for copy in copies:
        copy.start()
    for copy in copies:
        copy.wait()
    rows = half * tile_rows
    panel = split(panel_buf[...].reshape(rows, width))
    inverse = split(inverse_buf[...])

    def times(parts, part):
        return lax.dot_general(
            jnp.concatenate(parts, axis=0), part, (((1,), (1,)), ((), ())), preferred_element_type=jnp.float32
        )

    high = times(panel, inverse[0])
    middle = times(panel[:2], inverse[1])
    low = times(panel[:1], inverse[2])
    product = (low + middle[rows:]) + high[2 * rows :]
    product = (product + (middle[:rows] + high[rows : 2 * rows])) + high[:rows]
    factor_ref[...] = product.astype(jnp.bfloat16).reshape(factor_ref.shape)


def make_factor(panel, inverse_factor, half):
    _, _, tile_rows, width = panel.shape
    return pl.pallas_call(
        factor_kernel,
        out_shape=jax.ShapeDtypeStruct((half, tile_rows, width), jnp.bfloat16),
        in_specs=[pl.BlockSpec(memory_space=pltpu.HBM)] * 2,
        out_specs=pl.BlockSpec(memory_space=pltpu.VMEM),
        scratch_shapes=[
            pltpu.VMEM((half, tile_rows, width), jnp.float32),
            pltpu.VMEM((width, width), jnp.float32),
            pltpu.SemaphoreType.DMA((2,)),
        ],
        compiler_params=pltpu.CompilerParams(vmem_limit_bytes=FACTOR_VMEM_BYTES),
        name="factor",
    )(panel, inverse_factor)


def partner(index, step, count):
    return index ^ step if count & (count - 1) == 0 else (index + step) % count


def plane_slots(count):
    if count == 4:
        return ((3, 0, 1, 2), (3, 0, 2, 1), (0, 2, 1, 3), (2, 3, 1, 0))
    return tuple(tuple(count - 1 - b for b in range(count)) for _ in range(count))


def plane_mates(count, plane):
    if count == 4:
        return ((0, 3, 1, 2), (0, 1, 2, 3), (0, 2, 1, 3), (0, 2, 1, 3))[plane]
    return tuple(range(count))


def slab_of(slots, plane, place):
    if len(slots) == 4:
        packed = sum(row.index(p) << 2 * (4 * at + p) for at, row in enumerate(slots) for p in range(4))
        packed -= (packed >> 31) << 32
        return (jnp.int32(packed) >> (2 * (4 * plane + place))) & 3
    slab = jnp.int32(0)
    for at, row in enumerate(slots):
        for b, slot in enumerate(row):
            slab = jnp.where((plane == at) & (place == slot), b, slab)
    return slab


def line_steps(count):
    return (0, 2, 1, 3) if count == 4 else tuple(range(count))


def move(x, sources, count):
    return lax.ppermute(x, ("row", "col"), [(a * count + b, r * count + c) for (r, c), (a, b) in sources.items()])


def gather_line(factor, late_factor, moved, count):
    if count != 4:
        line = [factor]
        for step in range(1, count):
            line.append(lax.ppermute(factor, "col", [(partner(b, step, count), b) for b in range(count)]))
        return line
    places = [(r, c) for r in range(count) for c in range(count)]
    near = move(late_factor, {(r, c): (r ^ 1, c) if r == c else (r, c ^ 1) for r, c in places}, count)
    far = move(late_factor, {(r, c): (r ^ 2, c) if r == c and r % 2 == 1 else (r, c ^ 2) for r, c in places}, count)
    r, c = lax.axis_index("row"), lax.axis_index("col")
    relayed = jnp.where((r == c) & (r % 2 == 1), moved, far)
    relayed = jnp.where(r == c ^ 1, near, relayed)
    last = move(relayed, {(r, c): (r, c ^ 1) for r, c in places}, count)
    return [factor, far, near, last]


def load_kernel(rows, after_ref, lines_ref, share_ref, sem):
    layer = lax.axis_index("layer")
    load = pltpu.make_async_copy(lines_ref.at[pl.ds(layer * rows, rows)], share_ref.at[pl.ds(0, rows)], sem)
    load.start()
    load.wait()


def load_share(after, lines, layers, per_row):
    rows = lines.shape[0] // layers

    def body(*refs):
        load_kernel(rows, *refs)

    return pl.pallas_call(
        body,
        out_shape=jax.ShapeDtypeStruct((rows + per_row, LANES), jnp.float32),
        in_specs=[pl.BlockSpec(memory_space=pl.ANY), pl.BlockSpec(memory_space=pltpu.HBM)],
        out_specs=pl.BlockSpec(memory_space=pltpu.VMEM),
        scratch_shapes=[pltpu.SemaphoreType.DMA],
        compiler_params=pltpu.CompilerParams(vmem_limit_bytes=LOAD_VMEM_BYTES),
        cost_estimate=pl.CostEstimate(flops=0, bytes_accessed=rows * LANES * 8, transcendentals=0),
        name="load_share",
    )(after, lines)


def fill_columns(columns_ref, pieces, slots, r, c, owner):
    half, tile_rows, _ = pieces[0].shape
    tile = tile_rows * len(pieces)
    for step, piece in enumerate(pieces):
        mate = jnp.int32(plane_mates(len(pieces), 0)[step])
        for plane in range(1, len(pieces) if len(pieces) == 4 else 1):
            mate = jnp.where(c == plane, plane_mates(len(pieces), plane)[step], mate)
        slab = slab_of(slots, c, partner(r, mate, len(pieces)))
        for k in range(half):
            at = pl.multiple_of(k * tile + slab * tile_rows, tile_rows)
            columns_ref[pl.ds(at, tile_rows), :] = piece[k]


def subtract_product(share_ref, rows, columns, tile, first_row, first_line, per_row):
    half, tile_rows, width = rows.shape
    product = lax.dot_general(
        rows.reshape(half * tile_rows, width),
        columns,
        (((1,), (1,)), ((), ())),
        preferred_element_type=jnp.float32,
    )
    for k in range(half):
        for part in range(product.shape[1] // LANES):
            start = (k * tile + first_row) * per_row + first_line + part
            at = pl.ds(start, tile_rows, stride=per_row)
            share_ref[at, :] -= product[k * tile_rows : (k + 1) * tile_rows, part * LANES : (part + 1) * LANES]


def take_rows(rows_ref, columns_ref, c, step, pieces):
    half, tile_rows, _ = rows_ref.shape
    for k in range(half):
        at = pl.multiple_of((k * pieces + partner(c, step, pieces)) * tile_rows, tile_rows)
        rows_ref[k] = columns_ref[pl.ds(at, tile_rows), :]


def begin_kernel(pieces, layers, tile, *refs):
    column_refs, row_refs, rest = refs[:pieces], refs[pieces : 2 * pieces - 1], refs[2 * pieces - 1 :]
    _, share_ref, columns_ref, *line_refs = rest
    r, c, layer = (lax.axis_index(axis) for axis in AXES)
    half, tile_rows, _ = row_refs[0].shape
    own_lines = half * tile // LANES
    fill_columns(columns_ref, column_refs, plane_slots(pieces), r, c, layer)
    for line_ref, row_ref in zip(line_refs, row_refs[1:]):
        line_ref[...] = row_ref[...]
    if pieces == 4:

        @pl.when(r == c)
        def _():
            for step, line_ref in zip(line_steps(pieces)[1:], line_refs):
                take_rows(line_ref, columns_ref, c, step, pieces)

    for step, row_ref in zip(line_steps(pieces), (row_refs[0], *line_refs)):
        first_row = partner(c, step, pieces) * tile_rows
        subtract_product(
            share_ref, row_ref[...], columns_ref[...], tile, first_row, layer * own_lines, layers * own_lines
        )


def begin_update(column_pieces, row_pieces, share, layers, tile):
    pieces = len(column_pieces)
    half, _, width = row_pieces[0].shape

    def body(*refs):
        begin_kernel(pieces, layers, tile, *refs)

    return pl.pallas_call(
        body,
        out_shape=[
            jax.ShapeDtypeStruct(share.shape, jnp.float32),
            jax.ShapeDtypeStruct((half * tile, width), jnp.bfloat16),
            *[jax.ShapeDtypeStruct(row_pieces[0].shape, jnp.bfloat16)] * (pieces - 2),
        ],
        in_specs=[pl.BlockSpec(memory_space=pltpu.VMEM)] * (2 * pieces),
        out_specs=[pl.BlockSpec(memory_space=pltpu.VMEM)] * pieces,
        input_output_aliases={2 * pieces - 1: 0},
        compiler_params=pltpu.CompilerParams(vmem_limit_bytes=VMEM_BYTES),
        name="begin_update",
    )(*column_pieces, *row_pieces, share)


def end_kernel(pieces, layers, tile, *refs):
    others = pieces * (layers - 1)
    column_refs, row_refs, rest = refs[:others], refs[others : others + pieces], refs[others + pieces :]
    own_ref, _, out_ref, share_ref, columns_buf, last_buf, sems = rest
    r, c, layer = (lax.axis_index(axis) for axis in AXES)
    half, tile_rows, _ = row_refs[0].shape
    own_lines = half * tile // LANES
    per_row = layers * own_lines
    owners = [lax.rem(layer + shift, layers) for shift in range(1, layers)]
    for at, owner in enumerate(owners):
        fill_columns(
            columns_buf.at[at], column_refs[at * pieces : (at + 1) * pieces], plane_slots(pieces), r, c, owner
        )
    last_buf[...] = row_refs[-1][...]
    if pieces == 4:

        @pl.when(r == c)
        def _():
            take_rows(last_buf, own_ref, c, line_steps(pieces)[-1], pieces)

    stores = []
    for at_row, row_ref in enumerate((*row_refs[:-1], last_buf)):
        first_row = partner(c, line_steps(pieces)[at_row], pieces) * tile_rows
        rows = row_ref[...]
        for at, owner in enumerate(owners):
            subtract_product(share_ref, rows, columns_buf[at], tile, first_row, owner * own_lines, per_row)
        if at_row == pieces - 1:
            subtract_product(share_ref, rows, own_ref[...], tile, first_row, layer * own_lines, per_row)
        for k in range(half):
            lines = tile_rows * per_row
            start = pl.multiple_of((k * tile + first_row) * per_row, lines)
            store = pltpu.make_async_copy(
                share_ref.at[pl.ds(start, lines)], out_ref.at[pl.ds(start, lines)], sems.at[at_row * half + k]
            )
            store.start()
            stores.append(store)
    for store in stores:
        store.wait()


def end_update(column_pieces, row_pieces, own_columns, share, layers, tile):
    pieces = len(row_pieces)
    half = row_pieces[0].shape[0]
    per_row = layers * own_columns.shape[0] // LANES
    operands = (*column_pieces, *row_pieces, own_columns, share)

    def body(*refs):
        end_kernel(pieces, layers, tile, *refs)

    result, _ = pl.pallas_call(
        body,
        out_shape=[
            jax.ShapeDtypeStruct((half * pieces * row_pieces[0].shape[1] * per_row, LANES), jnp.float32),
            jax.ShapeDtypeStruct(share.shape, jnp.float32),
        ],
        in_specs=[pl.BlockSpec(memory_space=pltpu.VMEM)] * len(operands),
        out_specs=[pl.BlockSpec(memory_space=pltpu.HBM), pl.BlockSpec(memory_space=pltpu.VMEM)],
        scratch_shapes=[
            pltpu.VMEM((layers - 1, *own_columns.shape), jnp.bfloat16),
            pltpu.VMEM(row_pieces[0].shape, jnp.bfloat16),
            pltpu.SemaphoreType.DMA((half * pieces,)),
        ],
        input_output_aliases={len(operands) - 1: 1},
        compiler_params=pltpu.CompilerParams(vmem_limit_bytes=VMEM_BYTES),
        name="end_update",
    )(*operands)
    return result


def per_device(trailing, panel, inverse_factor):
    layers = lax.axis_size("layer")
    count = lax.axis_size("row")
    row_tiles, _, tile, col_tiles, _, _ = trailing.shape
    half = row_tiles // layers
    slots = plane_slots(count)
    factor = make_factor(panel, inverse_factor, half)
    moved = lax.ppermute(
        factor, ("row", "col"), [(a * count + b, slots[a][b] * count + a) for a in range(count) for b in range(count)]
    )
    share = load_share(factor, trailing.reshape(-1, LANES), layers, col_tiles * tile // LANES)
    loaded_factor, share = lax.optimization_barrier((factor, share))
    line = gather_line(factor, loaded_factor, moved, count)
    plane = [moved]
    for step in range(1, count):
        sources = {
            (r, c): (partner(r, plane_mates(count, c)[step], count), c) for r in range(count) for c in range(count)
        }
        if count == 4 and step == 1:
            sources[0, 0], sources[1, 1] = (0, 1), (3, 0)
        plane.append(move(moved, sources, count))
    if count == 4:
        r, c = lax.axis_index("row"), lax.axis_index("col")
        plane[1] = jnp.where((r == c) & (r < 2), factor, plane[1])
    others = []
    for shift in range(1, layers):
        pairs = [((l + shift) % layers, l) for l in range(layers)]
        others += [lax.ppermute(piece, "layer", pairs) for piece in plane]
    share, own_columns, *rows = begin_update(plane, line[:-1], share, layers, tile)
    rows = [line[0], *rows, line[-1]]
    result = end_update(others, rows, own_columns, share, layers, tile)
    return result.reshape(half, 1, tile, col_tiles, 1, tile)


def solution(mesh):
    assert mesh.shape["row"] == mesh.shape["col"]
    return jax.shard_map(
        per_device,
        mesh=mesh,
        in_specs=(P(None, "row", None, None, "col", None), P(None, "row", "col", None), P()),
        out_specs=P("layer", "row", None, None, "col", None),
        check_vma=False,
    )
```

```python
import jax
import jax.numpy as jnp
from jax import lax
from jax.experimental import pallas as pl
from jax.experimental.pallas import tpu as pltpu
from jax.sharding import PartitionSpec as P

LANES = 128
VMEM_BYTES = 24 * 1024 * 1024
LOAD_VMEM_BYTES = 52000 * 1024
FACTOR_VMEM_BYTES = 55040 * 1024
AXES = ("row", "col", "layer")


def split(x):
    parts = []
    for _ in range(3):
        parts.append(x.astype(jnp.bfloat16))
        x = x - parts[-1].astype(jnp.float32)
    return parts


def factor_kernel(panel_ref, inverse_ref, factor_ref, panel_buf, inverse_buf, sems):
    half = factor_ref.shape[0]
    tile_rows = factor_ref.shape[1]
    width = factor_ref.shape[2]
    layer = lax.axis_index("layer")
    copies = [
        pltpu.make_async_copy(panel_ref.at[pl.ds(layer * half, half), 0], panel_buf, sems.at[0]),
        pltpu.make_async_copy(inverse_ref, inverse_buf, sems.at[1]),
    ]
    for copy in copies:
        copy.start()
    for copy in copies:
        copy.wait()
    rows = half * tile_rows
    panel = split(panel_buf[...].reshape(rows, width))
    inverse = split(inverse_buf[...])

    def times(parts, part):
        return lax.dot_general(
            jnp.concatenate(parts, axis=0), part, (((1,), (1,)), ((), ())), preferred_element_type=jnp.float32
        )

    high = times(panel, inverse[0])
    middle = times(panel[:2], inverse[1])
    low = times(panel[:1], inverse[2])
    product = (low + middle[rows:]) + high[2 * rows :]
    product = (product + (middle[:rows] + high[rows : 2 * rows])) + high[:rows]
    factor_ref[...] = product.astype(jnp.bfloat16).reshape(factor_ref.shape)


def make_factor(panel, inverse_factor, half):
    _, _, tile_rows, width = panel.shape
    return pl.pallas_call(
        factor_kernel,
        out_shape=jax.ShapeDtypeStruct((half, tile_rows, width), jnp.bfloat16),
        in_specs=[pl.BlockSpec(memory_space=pltpu.HBM)] * 2,
        out_specs=pl.BlockSpec(memory_space=pltpu.VMEM),
        scratch_shapes=[
            pltpu.VMEM((half, tile_rows, width), jnp.float32),
            pltpu.VMEM((width, width), jnp.float32),
            pltpu.SemaphoreType.DMA((2,)),
        ],
        compiler_params=pltpu.CompilerParams(vmem_limit_bytes=FACTOR_VMEM_BYTES),
        name="factor",
    )(panel, inverse_factor)


def partner(index, step, count):
    return index ^ step if count & (count - 1) == 0 else (index + step) % count


def plane_slots(count):
    if count == 4:
        return ((3, 0, 1, 2), (3, 0, 2, 1), (0, 2, 1, 3), (2, 3, 1, 0))
    return tuple(tuple(count - 1 - b for b in range(count)) for _ in range(count))


def plane_mates(count, plane):
    if count == 4:
        return ((0, 3, 1, 2), (0, 1, 2, 3), (0, 2, 1, 3), (0, 2, 1, 3))[plane]
    return tuple(range(count))


def slab_of(slots, plane, place):
    if len(slots) == 4:
        packed = sum(row.index(p) << 2 * (4 * at + p) for at, row in enumerate(slots) for p in range(4))
        packed -= (packed >> 31) << 32
        return (jnp.int32(packed) >> (2 * (4 * plane + place))) & 3
    slab = jnp.int32(0)
    for at, row in enumerate(slots):
        for b, slot in enumerate(row):
            slab = jnp.where((plane == at) & (place == slot), b, slab)
    return slab


def early_late(count):
    return ((0, 2), (1, 3)) if count == 4 else (tuple(range(count - 1)), (count - 1,))


def move(x, sources, count):
    return lax.ppermute(x, ("row", "col"), [(a * count + b, r * count + c) for (r, c), (a, b) in sources.items()])


def line_sources(step, count, kept):
    return {
        (r, c): (partner(r, step, count), c) if kept and r == c and r in kept else (r, partner(c, step, count))
        for r in range(count)
        for c in range(count)
    }


def load_kernel(rows, after_ref, lines_ref, share_ref, sem):
    layer = lax.axis_index("layer")
    load = pltpu.make_async_copy(lines_ref.at[pl.ds(layer * rows, rows)], share_ref.at[pl.ds(0, rows)], sem)
    load.start()
    load.wait()


def load_share(after, lines, layers, per_row):
    rows = lines.shape[0] // layers

    def body(*refs):
        load_kernel(rows, *refs)

    return pl.pallas_call(
        body,
        out_shape=jax.ShapeDtypeStruct((rows + per_row, LANES), jnp.float32),
        in_specs=[pl.BlockSpec(memory_space=pl.ANY), pl.BlockSpec(memory_space=pltpu.HBM)],
        out_specs=pl.BlockSpec(memory_space=pltpu.VMEM),
        scratch_shapes=[pltpu.SemaphoreType.DMA],
        compiler_params=pltpu.CompilerParams(vmem_limit_bytes=LOAD_VMEM_BYTES),
        cost_estimate=pl.CostEstimate(flops=0, bytes_accessed=rows * LANES * 8, transcendentals=0),
        name="load_share",
    )(after, lines)


def fill_columns(columns_ref, pieces, slots, r, c, owner):
    half, tile_rows, _ = pieces[0].shape
    tile = tile_rows * len(pieces)
    for step, piece in enumerate(pieces):
        mate = jnp.int32(plane_mates(len(pieces), 0)[step])
        for plane in range(1, len(pieces) if len(pieces) == 4 else 1):
            mate = jnp.where(c == plane, plane_mates(len(pieces), plane)[step], mate)
        slab = slab_of(slots, c, partner(r, mate, len(pieces)))
        for k in range(half):
            at = pl.multiple_of(k * tile + slab * tile_rows, tile_rows)
            columns_ref[pl.ds(at, tile_rows), :] = piece[k]


def subtract_product(share_ref, rows, columns, tile, first_row, first_line, per_row):
    half, tile_rows, width = rows.shape
    product = lax.dot_general(
        rows.reshape(half * tile_rows, width),
        columns,
        (((1,), (1,)), ((), ())),
        preferred_element_type=jnp.float32,
    )
    for k in range(half):
        for part in range(product.shape[1] // LANES):
            start = (k * tile + first_row) * per_row + first_line + part
            at = pl.ds(start, tile_rows, stride=per_row)
            share_ref[at, :] -= product[k * tile_rows : (k + 1) * tile_rows, part * LANES : (part + 1) * LANES]


def take_rows(rows_ref, piece_ref, columns_ref, r, c, step, pieces):
    rows_ref[...] = piece_ref[...]
    if pieces == 4:

        @pl.when(r == c)
        def _():
            half, tile_rows, _ = rows_ref.shape
            for k in range(half):
                at = pl.multiple_of((k * pieces + partner(c, step, pieces)) * tile_rows, tile_rows)
                rows_ref[k] = columns_ref[pl.ds(at, tile_rows), :]


def begin_kernel(pieces, layers, tile, *refs):
    early, _ = early_late(pieces)
    column_refs, row_refs, rest = refs[:pieces], refs[pieces : pieces + len(early)], refs[pieces + len(early) :]
    _, share_ref, columns_ref, *line_refs = rest
    r, c, layer = (lax.axis_index(axis) for axis in AXES)
    half, tile_rows, _ = row_refs[0].shape
    own_lines = half * tile // LANES
    fill_columns(columns_ref, column_refs, plane_slots(pieces), r, c, layer)
    for step, line_ref, row_ref in zip(early[1:], line_refs, row_refs[1:]):
        take_rows(line_ref, row_ref, columns_ref, r, c, step, pieces)
    for step, row_ref in zip(early, (row_refs[0], *line_refs)):
        first_row = partner(c, step, pieces) * tile_rows
        subtract_product(
            share_ref, row_ref[...], columns_ref[...], tile, first_row, layer * own_lines, layers * own_lines
        )


def begin_update(column_pieces, row_pieces, share, layers, tile):
    pieces = len(column_pieces)
    half, _, width = row_pieces[0].shape
    operands = (*column_pieces, *row_pieces, share)

    def body(*refs):
        begin_kernel(pieces, layers, tile, *refs)

    return pl.pallas_call(
        body,
        out_shape=[
            jax.ShapeDtypeStruct(share.shape, jnp.float32),
            jax.ShapeDtypeStruct((half * tile, width), jnp.bfloat16),
            *[jax.ShapeDtypeStruct(row_pieces[0].shape, jnp.bfloat16)] * (len(row_pieces) - 1),
        ],
        in_specs=[pl.BlockSpec(memory_space=pltpu.VMEM)] * len(operands),
        out_specs=[pl.BlockSpec(memory_space=pltpu.VMEM)] * (len(row_pieces) + 1),
        input_output_aliases={len(operands) - 1: 0},
        compiler_params=pltpu.CompilerParams(vmem_limit_bytes=VMEM_BYTES),
        name="begin_update",
    )(*operands)


def end_kernel(pieces, layers, tile, *refs):
    others = pieces * (layers - 1)
    column_refs, row_refs, rest = refs[:others], refs[others : others + pieces], refs[others + pieces :]
    own_ref, _, out_ref, share_ref, columns_buf, late_buf, sems = rest
    r, c, layer = (lax.axis_index(axis) for axis in AXES)
    half, tile_rows, _ = row_refs[0].shape
    own_lines = half * tile // LANES
    per_row = layers * own_lines
    owners = [lax.rem(layer + shift, layers) for shift in range(1, layers)]
    for at, owner in enumerate(owners):
        fill_columns(
            columns_buf.at[at], column_refs[at * pieces : (at + 1) * pieces], plane_slots(pieces), r, c, owner
        )
    early, late = early_late(pieces)
    for at, step in enumerate(late):
        take_rows(late_buf.at[at], row_refs[len(early) + at], own_ref, r, c, step, pieces)
    stores = []
    for at_row, step in enumerate(early + late):
        first_row = partner(c, step, pieces) * tile_rows
        is_late = at_row >= len(early)
        rows = late_buf[at_row - len(early)] if is_late else row_refs[at_row][...]
        for at, owner in enumerate(owners):
            subtract_product(share_ref, rows, columns_buf[at], tile, first_row, owner * own_lines, per_row)
        if is_late:
            subtract_product(share_ref, rows, own_ref[...], tile, first_row, layer * own_lines, per_row)
        for k in range(half):
            lines = tile_rows * per_row
            start = pl.multiple_of((k * tile + first_row) * per_row, lines)
            store = pltpu.make_async_copy(
                share_ref.at[pl.ds(start, lines)], out_ref.at[pl.ds(start, lines)], sems.at[at_row * half + k]
            )
            store.start()
            stores.append(store)
    for store in stores:
        store.wait()


def end_update(column_pieces, row_pieces, own_columns, share, layers, tile):
    pieces = len(row_pieces)
    half = row_pieces[0].shape[0]
    per_row = layers * own_columns.shape[0] // LANES
    operands = (*column_pieces, *row_pieces, own_columns, share)

    def body(*refs):
        end_kernel(pieces, layers, tile, *refs)

    result, _ = pl.pallas_call(
        body,
        out_shape=[
            jax.ShapeDtypeStruct((half * pieces * row_pieces[0].shape[1] * per_row, LANES), jnp.float32),
            jax.ShapeDtypeStruct(share.shape, jnp.float32),
        ],
        in_specs=[pl.BlockSpec(memory_space=pltpu.VMEM)] * len(operands),
        out_specs=[pl.BlockSpec(memory_space=pltpu.HBM), pl.BlockSpec(memory_space=pltpu.VMEM)],
        scratch_shapes=[
            pltpu.VMEM((layers - 1, *own_columns.shape), jnp.bfloat16),
            pltpu.VMEM((len(early_late(pieces)[1]), *row_pieces[0].shape), jnp.bfloat16),
            pltpu.SemaphoreType.DMA((half * pieces,)),
        ],
        input_output_aliases={len(operands) - 1: 1},
        compiler_params=pltpu.CompilerParams(vmem_limit_bytes=VMEM_BYTES),
        name="end_update",
    )(*operands)
    return result


def per_device(trailing, panel, inverse_factor):
    layers = lax.axis_size("layer")
    count = lax.axis_size("row")
    row_tiles, _, tile, col_tiles, _, _ = trailing.shape
    half = row_tiles // layers
    slots = plane_slots(count)
    factor = make_factor(panel, inverse_factor, half)
    moved = lax.ppermute(
        factor, ("row", "col"), [(a * count + b, slots[a][b] * count + a) for a in range(count) for b in range(count)]
    )
    share = load_share(factor, trailing.reshape(-1, LANES), layers, col_tiles * tile // LANES)
    loaded_factor, share = lax.optimization_barrier((factor, share))
    if count == 4:
        early = [factor, move(loaded_factor, line_sources(2, count, (1, 3)), count)]
    else:
        line = [move(loaded_factor, line_sources(step, count, ()), count) for step in range(1, count)]
        early, late = [factor, *line[:-1]], line[-1:]
    plane = [moved]
    for step in range(1, count):
        sources = {
            (r, c): (partner(r, plane_mates(count, c)[step], count), c) for r in range(count) for c in range(count)
        }
        if count == 4 and step == 1:
            sources[0, 0], sources[1, 1] = (0, 1), (3, 0)
        plane.append(move(moved, sources, count))
    if count == 4:
        r, c = lax.axis_index("row"), lax.axis_index("col")
        plane[1] = jnp.where((r == c) & (r < 2), factor, plane[1])
        relayed = jnp.where((r == c) & (r % 2 == 1), moved, early[1])
        last = move(relayed, line_sources(1, count, ()), count)
        late_factor, plane[-1] = lax.optimization_barrier((factor, plane[-1]))
        late = [move(late_factor, line_sources(1, count, range(count)), count), last]
    others = []
    for shift in range(1, layers):
        pairs = [((l + shift) % layers, l) for l in range(layers)]
        others += [lax.ppermute(piece, "layer", pairs) for piece in plane]
    share, own_columns, *rows = begin_update(plane, early, share, layers, tile)
    result = end_update(others, [factor, *rows, *late], own_columns, share, layers, tile)
    return result.reshape(half, 1, tile, col_tiles, 1, tile)


def solution(mesh):
    assert mesh.shape["row"] == mesh.shape["col"]
    return jax.shard_map(
        per_device,
        mesh=mesh,
        in_specs=(P(None, "row", None, None, "col", None), P(None, "row", "col", None), P()),
        out_specs=P("layer", "row", None, None, "col", None),
        check_vma=False,
    )
```

```python
import jax
import jax.numpy as jnp
from jax import lax
from jax.experimental import pallas as pl
from jax.experimental.pallas import tpu as pltpu
from jax.sharding import PartitionSpec as P

LANES = 128
VMEM_BYTES = 24 * 1024 * 1024
LOAD_VMEM_BYTES = 52000 * 1024
FACTOR_VMEM_BYTES = 55040 * 1024
AXES = ("row", "col", "layer")


def split(x):
    parts = []
    for _ in range(3):
        parts.append(x.astype(jnp.bfloat16))
        x = x - parts[-1].astype(jnp.float32)
    return parts


def factor_kernel(panel_ref, inverse_ref, factor_ref, panel_buf, inverse_buf, sems):
    half = factor_ref.shape[0]
    tile_rows = factor_ref.shape[1]
    width = factor_ref.shape[2]
    layer = lax.axis_index("layer")
    copies = [
        pltpu.make_async_copy(panel_ref.at[pl.ds(layer * half, half), 0], panel_buf, sems.at[0]),
        pltpu.make_async_copy(inverse_ref, inverse_buf, sems.at[1]),
    ]
    for copy in copies:
        copy.start()
    for copy in copies:
        copy.wait()
    rows = half * tile_rows
    panel = split(panel_buf[...].reshape(rows, width))
    inverse = split(inverse_buf[...])

    def times(parts, part):
        return lax.dot_general(
            jnp.concatenate(parts, axis=0), part, (((1,), (1,)), ((), ())), preferred_element_type=jnp.float32
        )

    high = times(panel, inverse[0])
    middle = times(panel[:2], inverse[1])
    low = times(panel[:1], inverse[2])
    product = (low + middle[rows:]) + high[2 * rows :]
    product = (product + (middle[:rows] + high[rows : 2 * rows])) + high[:rows]
    factor_ref[...] = product.astype(jnp.bfloat16).reshape(factor_ref.shape)


def make_factor(panel, inverse_factor, half):
    _, _, tile_rows, width = panel.shape
    return pl.pallas_call(
        factor_kernel,
        out_shape=jax.ShapeDtypeStruct((half, tile_rows, width), jnp.bfloat16),
        in_specs=[pl.BlockSpec(memory_space=pltpu.HBM)] * 2,
        out_specs=pl.BlockSpec(memory_space=pltpu.VMEM),
        scratch_shapes=[
            pltpu.VMEM((half, tile_rows, width), jnp.float32),
            pltpu.VMEM((width, width), jnp.float32),
            pltpu.SemaphoreType.DMA((2,)),
        ],
        compiler_params=pltpu.CompilerParams(vmem_limit_bytes=FACTOR_VMEM_BYTES),
        name="factor",
    )(panel, inverse_factor)


def partner(index, step, count):
    return index ^ step if count & (count - 1) == 0 else (index + step) % count


def plane_slots(count):
    if count == 4:
        return ((3, 0, 1, 2), (3, 0, 2, 1), (0, 2, 1, 3), (2, 3, 1, 0))
    return tuple(tuple(count - 1 - b for b in range(count)) for _ in range(count))


def plane_mates(count, plane):
    if count == 4:
        return ((0, 3, 1, 2), (0, 1, 2, 3), (0, 2, 1, 3), (0, 2, 1, 3))[plane]
    return tuple(range(count))


def slab_of(slots, plane, place):
    if len(slots) == 4:
        packed = sum(row.index(p) << 2 * (4 * at + p) for at, row in enumerate(slots) for p in range(4))
        packed -= (packed >> 31) << 32
        return (jnp.int32(packed) >> (2 * (4 * plane + place))) & 3
    slab = jnp.int32(0)
    for at, row in enumerate(slots):
        for b, slot in enumerate(row):
            slab = jnp.where((plane == at) & (place == slot), b, slab)
    return slab


def line_steps(count):
    return (0, 2, 1, 3) if count == 4 else tuple(range(count))


def move(x, sources, count):
    return lax.ppermute(x, ("row", "col"), [(a * count + b, r * count + c) for (r, c), (a, b) in sources.items()])


def gather_line(factor, late_factor, moved, count):
    if count != 4:
        line = [factor]
        for step in range(1, count):
            line.append(lax.ppermute(factor, "col", [(partner(b, step, count), b) for b in range(count)]))
        return line
    places = [(r, c) for r in range(count) for c in range(count)]
    near = move(late_factor, {(r, c): (r ^ 1, c) if r == c else (r, c ^ 1) for r, c in places}, count)
    far = move(late_factor, {(r, c): (r ^ 2, c) if r == c and r % 2 == 1 else (r, c ^ 2) for r, c in places}, count)
    r, c = lax.axis_index("row"), lax.axis_index("col")
    relayed = jnp.where((r == c) & (r % 2 == 1), moved, far)
    relayed = jnp.where(r == c ^ 1, near, relayed)
    last = move(relayed, {(r, c): (r, c ^ 1) for r, c in places}, count)
    return [factor, far, near, last]


def load_kernel(rows, after_ref, lines_ref, share_ref, sem):
    layer = lax.axis_index("layer")
    load = pltpu.make_async_copy(lines_ref.at[pl.ds(layer * rows, rows)], share_ref.at[pl.ds(0, rows)], sem)
    load.start()
    load.wait()


def load_share(after, lines, layers, per_row):
    rows = lines.shape[0] // layers

    def body(*refs):
        load_kernel(rows, *refs)

    return pl.pallas_call(
        body,
        out_shape=jax.ShapeDtypeStruct((rows + per_row, LANES), jnp.float32),
        in_specs=[pl.BlockSpec(memory_space=pl.ANY), pl.BlockSpec(memory_space=pltpu.HBM)],
        out_specs=pl.BlockSpec(memory_space=pltpu.VMEM),
        scratch_shapes=[pltpu.SemaphoreType.DMA],
        compiler_params=pltpu.CompilerParams(vmem_limit_bytes=LOAD_VMEM_BYTES),
        cost_estimate=pl.CostEstimate(flops=0, bytes_accessed=rows * LANES * 8, transcendentals=0),
        name="load_share",
    )(after, lines)


def fill_columns(columns_ref, pieces, slots, r, c, owner):
    half, tile_rows, _ = pieces[0].shape
    tile = tile_rows * len(pieces)
    for step, piece in enumerate(pieces):
        mate = jnp.int32(plane_mates(len(pieces), 0)[step])
        for plane in range(1, len(pieces) if len(pieces) == 4 else 1):
            mate = jnp.where(c == plane, plane_mates(len(pieces), plane)[step], mate)
        slab = slab_of(slots, c, partner(r, mate, len(pieces)))
        for k in range(half):
            at = pl.multiple_of(k * tile + slab * tile_rows, tile_rows)
            columns_ref[pl.ds(at, tile_rows), :] = piece[k]


def subtract_product(share_ref, rows, columns, tile, first_row, first_line, per_row):
    half, tile_rows, width = rows.shape
    product = lax.dot_general(
        rows.reshape(half * tile_rows, width),
        columns,
        (((1,), (1,)), ((), ())),
        preferred_element_type=jnp.float32,
    )
    for k in range(half):
        for part in range(product.shape[1] // LANES):
            start = (k * tile + first_row) * per_row + first_line + part
            at = pl.ds(start, tile_rows, stride=per_row)
            share_ref[at, :] -= product[k * tile_rows : (k + 1) * tile_rows, part * LANES : (part + 1) * LANES]


def take_rows(rows_ref, columns_ref, c, step, pieces):
    half, tile_rows, _ = rows_ref.shape
    for k in range(half):
        at = pl.multiple_of((k * pieces + partner(c, step, pieces)) * tile_rows, tile_rows)
        rows_ref[k] = columns_ref[pl.ds(at, tile_rows), :]


def begin_kernel(pieces, layers, tile, *refs):
    column_refs, row_refs, rest = refs[:pieces], refs[pieces : 2 * pieces - 1], refs[2 * pieces - 1 :]
    loaded_ref, share_ref, columns_ref, *line_refs = rest
    r, c, layer = (lax.axis_index(axis) for axis in AXES)
    half, tile_rows, _ = row_refs[0].shape
    own_lines = half * tile // LANES
    share_ref[...] = loaded_ref[...]
    fill_columns(columns_ref, column_refs, plane_slots(pieces), r, c, layer)
    for line_ref, row_ref in zip(line_refs, row_refs[1:]):
        line_ref[...] = row_ref[...]
    if pieces == 4:

        @pl.when(r == c)
        def _():
            for step, line_ref in zip(line_steps(pieces)[1:], line_refs):
                take_rows(line_ref, columns_ref, c, step, pieces)

    for step, row_ref in zip(line_steps(pieces), (row_refs[0], *line_refs)):
        first_row = partner(c, step, pieces) * tile_rows
        subtract_product(
            share_ref, row_ref[...], columns_ref[...], tile, first_row, layer * own_lines, layers * own_lines
        )


def begin_update(column_pieces, row_pieces, share, layers, tile):
    pieces = len(column_pieces)
    half, _, width = row_pieces[0].shape

    def body(*refs):
        begin_kernel(pieces, layers, tile, *refs)

    return pl.pallas_call(
        body,
        out_shape=[
            jax.ShapeDtypeStruct(share.shape, jnp.float32),
            jax.ShapeDtypeStruct((half * tile, width), jnp.bfloat16),
            *[jax.ShapeDtypeStruct(row_pieces[0].shape, jnp.bfloat16)] * (pieces - 2),
        ],
        in_specs=[pl.BlockSpec(memory_space=pltpu.VMEM)] * (2 * pieces),
        out_specs=[pl.BlockSpec(memory_space=pltpu.VMEM)] * pieces,
        input_output_aliases={2 * pieces - 1: 0},
        compiler_params=pltpu.CompilerParams(vmem_limit_bytes=VMEM_BYTES),
        name="begin_update",
    )(*column_pieces, *row_pieces, share)


def end_kernel(pieces, layers, tile, *refs):
    others = pieces * (layers - 1)
    column_refs, row_refs, rest = refs[:others], refs[others : others + pieces], refs[others + pieces :]
    own_ref, share_ref, out_ref, _, columns_buf, last_buf, sems = rest
    r, c, layer = (lax.axis_index(axis) for axis in AXES)
    half, tile_rows, _ = row_refs[0].shape
    own_lines = half * tile // LANES
    per_row = layers * own_lines
    owners = [lax.rem(layer + shift, layers) for shift in range(1, layers)]
    for at, owner in enumerate(owners):
        fill_columns(
            columns_buf.at[at], column_refs[at * pieces : (at + 1) * pieces], plane_slots(pieces), r, c, owner
        )
    last_buf[...] = row_refs[-1][...]
    if pieces == 4:

        @pl.when(r == c)
        def _():
            take_rows(last_buf, own_ref, c, line_steps(pieces)[-1], pieces)

    stores = []
    for at_row, row_ref in enumerate((*row_refs[:-1], last_buf)):
        first_row = partner(c, line_steps(pieces)[at_row], pieces) * tile_rows
        rows = row_ref[...]
        for at, owner in enumerate(owners):
            subtract_product(share_ref, rows, columns_buf[at], tile, first_row, owner * own_lines, per_row)
        if at_row == pieces - 1:
            subtract_product(share_ref, rows, own_ref[...], tile, first_row, layer * own_lines, per_row)
        for k in range(half):
            lines = tile_rows * per_row
            start = pl.multiple_of((k * tile + first_row) * per_row, lines)
            store = pltpu.make_async_copy(
                share_ref.at[pl.ds(start, lines)], out_ref.at[pl.ds(start, lines)], sems.at[at_row * half + k]
            )
            store.start()
            stores.append(store)
    for store in stores:
        store.wait()


def end_update(column_pieces, row_pieces, own_columns, share, layers, tile):
    pieces = len(row_pieces)
    half = row_pieces[0].shape[0]
    per_row = layers * own_columns.shape[0] // LANES
    operands = (*column_pieces, *row_pieces, own_columns, share)

    def body(*refs):
        end_kernel(pieces, layers, tile, *refs)

    result, _ = pl.pallas_call(
        body,
        out_shape=[
            jax.ShapeDtypeStruct((half * pieces * row_pieces[0].shape[1] * per_row, LANES), jnp.float32),
            jax.ShapeDtypeStruct(share.shape, jnp.float32),
        ],
        in_specs=[pl.BlockSpec(memory_space=pltpu.VMEM)] * len(operands),
        out_specs=[pl.BlockSpec(memory_space=pltpu.HBM), pl.BlockSpec(memory_space=pltpu.VMEM)],
        scratch_shapes=[
            pltpu.VMEM((layers - 1, *own_columns.shape), jnp.bfloat16),
            pltpu.VMEM(row_pieces[0].shape, jnp.bfloat16),
            pltpu.SemaphoreType.DMA((half * pieces,)),
        ],
        input_output_aliases={len(operands) - 1: 1},
        compiler_params=pltpu.CompilerParams(vmem_limit_bytes=VMEM_BYTES),
        name="end_update",
    )(*operands)
    return result


def per_device(trailing, panel, inverse_factor):
    layers = lax.axis_size("layer")
    count = lax.axis_size("row")
    row_tiles, _, tile, col_tiles, _, _ = trailing.shape
    half = row_tiles // layers
    slots = plane_slots(count)
    factor = make_factor(panel, inverse_factor, half)
    moved = lax.ppermute(
        factor, ("row", "col"), [(a * count + b, slots[a][b] * count + a) for a in range(count) for b in range(count)]
    )
    share = load_share(factor, trailing.reshape(-1, LANES), layers, col_tiles * tile // LANES)
    loaded_factor, share = lax.optimization_barrier((factor, share))
    line = gather_line(factor, loaded_factor, moved, count)
    plane = [moved]
    for step in range(1, count):
        sources = {
            (r, c): (partner(r, plane_mates(count, c)[step], count), c) for r in range(count) for c in range(count)
        }
        if count == 4 and step == 1:
            sources[0, 0], sources[1, 1] = (0, 1), (3, 0)
        plane.append(move(moved, sources, count))
    if count == 4:
        r, c = lax.axis_index("row"), lax.axis_index("col")
        plane[1] = jnp.where((r == c) & (r < 2), factor, plane[1])
    others = []
    for shift in range(1, layers):
        pairs = [((l + shift) % layers, l) for l in range(layers)]
        others += [lax.ppermute(piece, "layer", pairs) for piece in plane]
    share, own_columns, *rows = begin_update(plane, line[:-1], share, layers, tile)
    rows = [line[0], *rows, line[-1]]
    result = end_update(others, rows, own_columns, share, layers, tile)
    return result.reshape(half, 1, tile, col_tiles, 1, tile)


def solution(mesh):
    assert mesh.shape["row"] == mesh.shape["col"]
    return jax.shard_map(
        per_device,
        mesh=mesh,
        in_specs=(P(None, "row", None, None, "col", None), P(None, "row", "col", None), P()),
        out_specs=P("layer", "row", None, None, "col", None),
        check_vma=False,
    )
```

```python
import jax
import jax.numpy as jnp
from jax import lax
from jax.experimental import pallas as pl
from jax.experimental.pallas import tpu as pltpu
from jax.sharding import PartitionSpec as P

LANES = 128
VMEM_BYTES = 24 * 1024 * 1024
LOAD_VMEM_BYTES = 52000 * 1024
FACTOR_VMEM_BYTES = 55040 * 1024
AXES = ("row", "col", "layer")


def split(x):
    parts = []
    for _ in range(3):
        parts.append(x.astype(jnp.bfloat16))
        x = x - parts[-1].astype(jnp.float32)
    return parts


def factor_kernel(panel_ref, inverse_ref, factor_ref, panel_buf, inverse_buf, sems):
    half = factor_ref.shape[0]
    tile_rows = factor_ref.shape[1]
    width = factor_ref.shape[2]
    layer = lax.axis_index("layer")
    copies = [
        pltpu.make_async_copy(panel_ref.at[pl.ds(layer * half, half), 0], panel_buf, sems.at[0]),
        pltpu.make_async_copy(inverse_ref, inverse_buf, sems.at[1]),
    ]
    for copy in copies:
        copy.start()
    for copy in copies:
        copy.wait()
    rows = half * tile_rows
    panel = split(panel_buf[...].reshape(rows, width))
    inverse = split(inverse_buf[...])

    def times(parts, part):
        return lax.dot_general(
            jnp.concatenate(parts, axis=0), part, (((1,), (1,)), ((), ())), preferred_element_type=jnp.float32
        )

    high = times(panel, inverse[0])
    middle = times(panel[:2], inverse[1])
    low = times(panel[:1], inverse[2])
    product = (low + middle[rows:]) + high[2 * rows :]
    product = (product + (middle[:rows] + high[rows : 2 * rows])) + high[:rows]
    factor_ref[...] = product.astype(jnp.bfloat16).reshape(factor_ref.shape)


def make_factor(panel, inverse_factor, half):
    _, _, tile_rows, width = panel.shape
    return pl.pallas_call(
        factor_kernel,
        out_shape=jax.ShapeDtypeStruct((half, tile_rows, width), jnp.bfloat16),
        in_specs=[pl.BlockSpec(memory_space=pltpu.HBM)] * 2,
        out_specs=pl.BlockSpec(memory_space=pltpu.VMEM),
        scratch_shapes=[
            pltpu.VMEM((half, tile_rows, width), jnp.float32),
            pltpu.VMEM((width, width), jnp.float32),
            pltpu.SemaphoreType.DMA((2,)),
        ],
        compiler_params=pltpu.CompilerParams(vmem_limit_bytes=FACTOR_VMEM_BYTES),
        name="factor",
    )(panel, inverse_factor)


def partner(index, step, count):
    return index ^ step if count & (count - 1) == 0 else (index + step) % count


def plane_slots(count):
    if count == 4:
        return ((3, 0, 1, 2), (3, 0, 2, 1), (3, 2, 1, 0), (2, 3, 1, 0))
    return tuple(tuple(count - 1 - b for b in range(count)) for _ in range(count))


def plane_mates(count, plane):
    if count == 4:
        return ((0, 3, 1, 2), (0, 1, 2, 3), (0, 2, 1, 3), (0, 2, 1, 3))[plane]
    return tuple(range(count))


def slab_of(slots, plane, place):
    if len(slots) == 4:
        packed = sum(row.index(p) << 2 * (4 * at + p) for at, row in enumerate(slots) for p in range(4))
        packed -= (packed >> 31) << 32
        return (jnp.int32(packed) >> (2 * (4 * plane + place))) & 3
    slab = jnp.int32(0)
    for at, row in enumerate(slots):
        for b, slot in enumerate(row):
            slab = jnp.where((plane == at) & (place == slot), b, slab)
    return slab


def line_steps(count):
    return (0, 2, 1, 3) if count == 4 else tuple(range(count))


def move(x, sources, count):
    return lax.ppermute(x, ("row", "col"), [(a * count + b, r * count + c) for (r, c), (a, b) in sources.items()])


def gather_line(factor, late_factor, moved, count):
    if count != 4:
        line = [factor]
        for step in range(1, count):
            line.append(lax.ppermute(factor, "col", [(partner(b, step, count), b) for b in range(count)]))
        return line
    places = [(r, c) for r in range(count) for c in range(count)]
    near = move(late_factor, {(r, c): (r ^ 1, c) if r == c else (r, c ^ 1) for r, c in places}, count)
    far = move(late_factor, {(r, c): (r ^ 2, c) if r == c and r % 2 == 1 else (r, c ^ 2) for r, c in places}, count)
    r, c = lax.axis_index("row"), lax.axis_index("col")
    relayed = jnp.where((r == c) & (r % 2 == 1), moved, far)
    relayed = jnp.where(r == c ^ 1, near, relayed)
    last = move(relayed, {(r, c): (r, c ^ 1) for r, c in places}, count)
    return [factor, far, near, last]


def load_kernel(rows, after_ref, lines_ref, share_ref, sem):
    layer = lax.axis_index("layer")
    load = pltpu.make_async_copy(lines_ref.at[pl.ds(layer * rows, rows)], share_ref.at[pl.ds(0, rows)], sem)
    load.start()
    load.wait()


def load_share(after, lines, layers, per_row):
    rows = lines.shape[0] // layers

    def body(*refs):
        load_kernel(rows, *refs)

    return pl.pallas_call(
        body,
        out_shape=jax.ShapeDtypeStruct((rows + per_row, LANES), jnp.float32),
        in_specs=[pl.BlockSpec(memory_space=pl.ANY), pl.BlockSpec(memory_space=pltpu.HBM)],
        out_specs=pl.BlockSpec(memory_space=pltpu.VMEM),
        scratch_shapes=[pltpu.SemaphoreType.DMA],
        compiler_params=pltpu.CompilerParams(vmem_limit_bytes=LOAD_VMEM_BYTES),
        cost_estimate=pl.CostEstimate(flops=0, bytes_accessed=rows * LANES * 8, transcendentals=0),
        name="load_share",
    )(after, lines)


def fill_columns(columns_ref, pieces, slots, r, c, owner):
    half, tile_rows, _ = pieces[0].shape
    tile = tile_rows * len(pieces)
    for step, piece in enumerate(pieces):
        mate = jnp.int32(plane_mates(len(pieces), 0)[step])
        for plane in range(1, len(pieces) if len(pieces) == 4 else 1):
            mate = jnp.where(c == plane, plane_mates(len(pieces), plane)[step], mate)
        slab = slab_of(slots, c, partner(r, mate, len(pieces)))
        for k in range(half):
            at = pl.multiple_of(k * tile + slab * tile_rows, tile_rows)
            columns_ref[pl.ds(at, tile_rows), :] = piece[k]


def subtract_product(share_ref, rows, columns, tile, first_row, first_line, per_row):
    half, tile_rows, width = rows.shape
    product = lax.dot_general(
        rows.reshape(half * tile_rows, width),
        columns,
        (((1,), (1,)), ((), ())),
        preferred_element_type=jnp.float32,
    )
    for k in range(half):
        for part in range(product.shape[1] // LANES):
            start = (k * tile + first_row) * per_row + first_line + part
            at = pl.ds(start, tile_rows, stride=per_row)
            share_ref[at, :] -= product[k * tile_rows : (k + 1) * tile_rows, part * LANES : (part + 1) * LANES]


def take_rows(rows_ref, columns_ref, c, step, pieces):
    half, tile_rows, _ = rows_ref.shape
    for k in range(half):
        at = pl.multiple_of((k * pieces + partner(c, step, pieces)) * tile_rows, tile_rows)
        rows_ref[k] = columns_ref[pl.ds(at, tile_rows), :]


def begin_kernel(pieces, layers, tile, *refs):
    column_refs, row_refs, rest = refs[:pieces], refs[pieces : 2 * pieces - 1], refs[2 * pieces - 1 :]
    loaded_ref, share_ref, columns_ref, *line_refs = rest
    r, c, layer = (lax.axis_index(axis) for axis in AXES)
    half, tile_rows, _ = row_refs[0].shape
    own_lines = half * tile // LANES
    share_ref[...] = loaded_ref[...]
    fill_columns(columns_ref, column_refs, plane_slots(pieces), r, c, layer)
    for line_ref, row_ref in zip(line_refs, row_refs[1:]):
        line_ref[...] = row_ref[...]
    if pieces == 4:

        @pl.when(r == c)
        def _():
            for step, line_ref in zip(line_steps(pieces)[1:], line_refs):
                take_rows(line_ref, columns_ref, c, step, pieces)

    for step, row_ref in zip(line_steps(pieces), (row_refs[0], *line_refs)):
        first_row = partner(c, step, pieces) * tile_rows
        subtract_product(
            share_ref, row_ref[...], columns_ref[...], tile, first_row, layer * own_lines, layers * own_lines
        )


def begin_update(column_pieces, row_pieces, share, layers, tile):
    pieces = len(column_pieces)
    half, _, width = row_pieces[0].shape

    def body(*refs):
        begin_kernel(pieces, layers, tile, *refs)

    return pl.pallas_call(
        body,
        out_shape=[
            jax.ShapeDtypeStruct(share.shape, jnp.float32),
            jax.ShapeDtypeStruct((half * tile, width), jnp.bfloat16),
            *[jax.ShapeDtypeStruct(row_pieces[0].shape, jnp.bfloat16)] * (pieces - 2),
        ],
        in_specs=[pl.BlockSpec(memory_space=pltpu.VMEM)] * (2 * pieces),
        out_specs=[pl.BlockSpec(memory_space=pltpu.VMEM)] * pieces,
        input_output_aliases={2 * pieces - 1: 0},
        compiler_params=pltpu.CompilerParams(vmem_limit_bytes=VMEM_BYTES),
        name="begin_update",
    )(*column_pieces, *row_pieces, share)


def end_kernel(pieces, layers, tile, *refs):
    others = pieces * (layers - 1)
    column_refs, row_refs, rest = refs[:others], refs[others : others + pieces], refs[others + pieces :]
    own_ref, share_ref, out_ref, _, columns_buf, last_buf, sems = rest
    r, c, layer = (lax.axis_index(axis) for axis in AXES)
    half, tile_rows, _ = row_refs[0].shape
    own_lines = half * tile // LANES
    per_row = layers * own_lines
    owners = [lax.rem(layer + shift, layers) for shift in range(1, layers)]
    for at, owner in enumerate(owners):
        fill_columns(
            columns_buf.at[at], column_refs[at * pieces : (at + 1) * pieces], plane_slots(pieces), r, c, owner
        )
    last_buf[...] = row_refs[-1][...]
    if pieces == 4:

        @pl.when(r == c)
        def _():
            take_rows(last_buf, own_ref, c, line_steps(pieces)[-1], pieces)

    stores = []
    for at_row, row_ref in enumerate((*row_refs[:-1], last_buf)):
        first_row = partner(c, line_steps(pieces)[at_row], pieces) * tile_rows
        rows = row_ref[...]
        for at, owner in enumerate(owners):
            subtract_product(share_ref, rows, columns_buf[at], tile, first_row, owner * own_lines, per_row)
        if at_row == pieces - 1:
            subtract_product(share_ref, rows, own_ref[...], tile, first_row, layer * own_lines, per_row)
        for k in range(half):
            lines = tile_rows * per_row
            start = pl.multiple_of((k * tile + first_row) * per_row, lines)
            store = pltpu.make_async_copy(
                share_ref.at[pl.ds(start, lines)], out_ref.at[pl.ds(start, lines)], sems.at[at_row * half + k]
            )
            store.start()
            stores.append(store)
    for store in stores:
        store.wait()


def end_update(column_pieces, row_pieces, own_columns, share, layers, tile):
    pieces = len(row_pieces)
    half = row_pieces[0].shape[0]
    per_row = layers * own_columns.shape[0] // LANES
    operands = (*column_pieces, *row_pieces, own_columns, share)

    def body(*refs):
        end_kernel(pieces, layers, tile, *refs)

    result, _ = pl.pallas_call(
        body,
        out_shape=[
            jax.ShapeDtypeStruct((half * pieces * row_pieces[0].shape[1] * per_row, LANES), jnp.float32),
            jax.ShapeDtypeStruct(share.shape, jnp.float32),
        ],
        in_specs=[pl.BlockSpec(memory_space=pltpu.VMEM)] * len(operands),
        out_specs=[pl.BlockSpec(memory_space=pltpu.HBM), pl.BlockSpec(memory_space=pltpu.VMEM)],
        scratch_shapes=[
            pltpu.VMEM((layers - 1, *own_columns.shape), jnp.bfloat16),
            pltpu.VMEM(row_pieces[0].shape, jnp.bfloat16),
            pltpu.SemaphoreType.DMA((half * pieces,)),
        ],
        input_output_aliases={len(operands) - 1: 1},
        compiler_params=pltpu.CompilerParams(vmem_limit_bytes=VMEM_BYTES),
        name="end_update",
    )(*operands)
    return result


def per_device(trailing, panel, inverse_factor):
    layers = lax.axis_size("layer")
    count = lax.axis_size("row")
    row_tiles, _, tile, col_tiles, _, _ = trailing.shape
    half = row_tiles // layers
    slots = plane_slots(count)
    factor = make_factor(panel, inverse_factor, half)
    moved = lax.ppermute(
        factor, ("row", "col"), [(a * count + b, slots[a][b] * count + a) for a in range(count) for b in range(count)]
    )
    share = load_share(factor, trailing.reshape(-1, LANES), layers, col_tiles * tile // LANES)
    loaded_factor, share = lax.optimization_barrier((factor, share))
    line = gather_line(factor, loaded_factor, moved, count)
    plane = [moved]
    for step in range(1, count):
        sources = {
            (r, c): (partner(r, plane_mates(count, c)[step], count), c) for r in range(count) for c in range(count)
        }
        if count == 4 and step == 1:
            sources[0, 0], sources[1, 1] = (0, 1), (3, 0)
        plane.append(move(moved, sources, count))
    if count == 4:
        r, c = lax.axis_index("row"), lax.axis_index("col")
        plane[1] = jnp.where((r == c) & (r < 2), factor, plane[1])
    others = []
    for shift in range(1, layers):
        pairs = [((l + shift) % layers, l) for l in range(layers)]
        others += [lax.ppermute(piece, "layer", pairs) for piece in plane]
    share, own_columns, *rows = begin_update(plane, line[:-1], share, layers, tile)
    rows = [line[0], *rows, line[-1]]
    result = end_update(others, rows, own_columns, share, layers, tile)
    return result.reshape(half, 1, tile, col_tiles, 1, tile)


def solution(mesh):
    assert mesh.shape["row"] == mesh.shape["col"]
    return jax.shard_map(
        per_device,
        mesh=mesh,
        in_specs=(P(None, "row", None, None, "col", None), P(None, "row", "col", None), P()),
        out_specs=P("layer", "row", None, None, "col", None),
        check_vma=False,
    )
```

```python
import jax
import jax.numpy as jnp
from jax import lax
from jax.experimental import pallas as pl
from jax.experimental.pallas import tpu as pltpu
from jax.sharding import PartitionSpec as P

LANES = 128
VMEM_BYTES = 24 * 1024 * 1024
LOAD_VMEM_BYTES = 52000 * 1024
FACTOR_VMEM_BYTES = 55040 * 1024
AXES = ("row", "col", "layer")


def split(x):
    parts = []
    for _ in range(3):
        parts.append(x.astype(jnp.bfloat16))
        x = x - parts[-1].astype(jnp.float32)
    return parts


def factor_kernel(panel_ref, inverse_ref, factor_ref, panel_buf, inverse_buf, sems):
    half = factor_ref.shape[0]
    tile_rows = factor_ref.shape[1]
    width = factor_ref.shape[2]
    layer = lax.axis_index("layer")
    copies = [
        pltpu.make_async_copy(panel_ref.at[pl.ds(layer * half, half), 0], panel_buf, sems.at[0]),
        pltpu.make_async_copy(inverse_ref, inverse_buf, sems.at[1]),
    ]
    for copy in copies:
        copy.start()
    for copy in copies:
        copy.wait()
    rows = half * tile_rows
    panel = split(panel_buf[...].reshape(rows, width))
    inverse = split(inverse_buf[...])

    def times(parts, part):
        return lax.dot_general(
            jnp.concatenate(parts, axis=0), part, (((1,), (1,)), ((), ())), preferred_element_type=jnp.float32
        )

    high = times(panel, inverse[0])
    middle = times(panel[:2], inverse[1])
    low = times(panel[:1], inverse[2])
    product = (low + middle[rows:]) + high[2 * rows :]
    product = (product + (middle[:rows] + high[rows : 2 * rows])) + high[:rows]
    factor_ref[...] = product.astype(jnp.bfloat16).reshape(factor_ref.shape)


def make_factor(panel, inverse_factor, half):
    _, _, tile_rows, width = panel.shape
    return pl.pallas_call(
        factor_kernel,
        out_shape=jax.ShapeDtypeStruct((half, tile_rows, width), jnp.bfloat16),
        in_specs=[pl.BlockSpec(memory_space=pltpu.HBM)] * 2,
        out_specs=pl.BlockSpec(memory_space=pltpu.VMEM),
        scratch_shapes=[
            pltpu.VMEM((half, tile_rows, width), jnp.float32),
            pltpu.VMEM((width, width), jnp.float32),
            pltpu.SemaphoreType.DMA((2,)),
        ],
        compiler_params=pltpu.CompilerParams(vmem_limit_bytes=FACTOR_VMEM_BYTES),
        name="factor",
    )(panel, inverse_factor)


def partner(index, step, count):
    return index ^ step if count & (count - 1) == 0 else (index + step) % count


def plane_slots(count):
    if count == 4:
        return ((3, 0, 1, 2), (3, 0, 2, 1), (3, 2, 1, 0), (2, 3, 1, 0))
    return tuple(tuple(count - 1 - b for b in range(count)) for _ in range(count))


def plane_mates(count, plane):
    if count == 4:
        return ((0, 3, 1, 2), (0, 1, 2, 3), (0, 2, 1, 3), (0, 2, 1, 3))[plane]
    return tuple(range(count))


def slab_of(slots, plane, place):
    if len(slots) == 4:
        packed = sum(row.index(p) << 2 * (4 * at + p) for at, row in enumerate(slots) for p in range(4))
        packed -= (packed >> 31) << 32
        return (jnp.int32(packed) >> (2 * (4 * plane + place))) & 3
    slab = jnp.int32(0)
    for at, row in enumerate(slots):
        for b, slot in enumerate(row):
            slab = jnp.where((plane == at) & (place == slot), b, slab)
    return slab


def line_steps(count, line):
    if count == 4:
        return (0, 3, 1, 2) if line == 0 else (0, 2, 1, 3)
    return tuple(range(count))


def steps_of(count, r):
    pairs = zip(line_steps(count, 0), line_steps(count, 1))
    return [first if first == other else jnp.where(r == 0, first, other) for first, other in pairs]


def move(x, sources, count):
    return lax.ppermute(x, ("row", "col"), [(a * count + b, r * count + c) for (r, c), (a, b) in sources.items()])


def gather_line(factor, late_factor, moved, count):
    if count != 4:
        line = [factor]
        for step in range(1, count):
            line.append(lax.ppermute(factor, "col", [(partner(b, step, count), b) for b in range(count)]))
        return line
    places = [(r, c) for r in range(count) for c in range(count)]
    near = move(late_factor, {(r, c): (r ^ 1, c) if r == c else (r, c ^ 1) for r, c in places}, count)
    sources = {
        (r, c): (r ^ 2, c) if r == c and r % 2 == 1 else (r, c ^ line_steps(count, r)[1]) for r, c in places
    }
    far = move(late_factor, sources, count)
    r, c = lax.axis_index("row"), lax.axis_index("col")
    relayed = jnp.where((r == c) & (r % 2 == 1), moved, far)
    relayed = jnp.where(r == c ^ 1, near, relayed)
    last = move(relayed, {(r, c): (r, c ^ 1) for r, c in places}, count)
    return [factor, far, near, last]


def load_kernel(rows, after_ref, lines_ref, share_ref, sem):
    layer = lax.axis_index("layer")
    load = pltpu.make_async_copy(lines_ref.at[pl.ds(layer * rows, rows)], share_ref.at[pl.ds(0, rows)], sem)
    load.start()
    load.wait()


def load_share(after, lines, layers, per_row):
    rows = lines.shape[0] // layers

    def body(*refs):
        load_kernel(rows, *refs)

    return pl.pallas_call(
        body,
        out_shape=jax.ShapeDtypeStruct((rows + per_row, LANES), jnp.float32),
        in_specs=[pl.BlockSpec(memory_space=pl.ANY), pl.BlockSpec(memory_space=pltpu.HBM)],
        out_specs=pl.BlockSpec(memory_space=pltpu.VMEM),
        scratch_shapes=[pltpu.SemaphoreType.DMA],
        compiler_params=pltpu.CompilerParams(vmem_limit_bytes=LOAD_VMEM_BYTES),
        cost_estimate=pl.CostEstimate(flops=0, bytes_accessed=rows * LANES * 8, transcendentals=0),
        name="load_share",
    )(after, lines)


def fill_columns(columns_ref, pieces, slots, r, c, owner):
    half, tile_rows, _ = pieces[0].shape
    tile = tile_rows * len(pieces)
    for step, piece in enumerate(pieces):
        mate = jnp.int32(plane_mates(len(pieces), 0)[step])
        for plane in range(1, len(pieces) if len(pieces) == 4 else 1):
            mate = jnp.where(c == plane, plane_mates(len(pieces), plane)[step], mate)
        slab = slab_of(slots, c, partner(r, mate, len(pieces)))
        for k in range(half):
            at = pl.multiple_of(k * tile + slab * tile_rows, tile_rows)
            columns_ref[pl.ds(at, tile_rows), :] = piece[k]


def subtract_product(share_ref, rows, columns, tile, first_row, first_line, per_row):
    half, tile_rows, width = rows.shape
    product = lax.dot_general(
        rows.reshape(half * tile_rows, width),
        columns,
        (((1,), (1,)), ((), ())),
        preferred_element_type=jnp.float32,
    )
    for k in range(half):
        for part in range(product.shape[1] // LANES):
            start = (k * tile + first_row) * per_row + first_line + part
            at = pl.ds(start, tile_rows, stride=per_row)
            share_ref[at, :] -= product[k * tile_rows : (k + 1) * tile_rows, part * LANES : (part + 1) * LANES]


def take_rows(rows_ref, columns_ref, c, step, pieces):
    half, tile_rows, _ = rows_ref.shape
    for k in range(half):
        at = pl.multiple_of((k * pieces + partner(c, step, pieces)) * tile_rows, tile_rows)
        rows_ref[k] = columns_ref[pl.ds(at, tile_rows), :]


def begin_kernel(pieces, layers, tile, *refs):
    column_refs, row_refs, rest = refs[:pieces], refs[pieces : 2 * pieces - 1], refs[2 * pieces - 1 :]
    loaded_ref, share_ref, columns_ref, *line_refs = rest
    r, c, layer = (lax.axis_index(axis) for axis in AXES)
    half, tile_rows, _ = row_refs[0].shape
    own_lines = half * tile // LANES
    share_ref[...] = loaded_ref[...]
    fill_columns(columns_ref, column_refs, plane_slots(pieces), r, c, layer)
    for line_ref, row_ref in zip(line_refs, row_refs[1:]):
        line_ref[...] = row_ref[...]
    if pieces == 4:

        @pl.when(r == c)
        def _():
            for step, line_ref in zip(steps_of(pieces, r)[1:], line_refs):
                take_rows(line_ref, columns_ref, c, step, pieces)

    for step, row_ref in zip(steps_of(pieces, r), (row_refs[0], *line_refs)):
        first_row = partner(c, step, pieces) * tile_rows
        subtract_product(
            share_ref, row_ref[...], columns_ref[...], tile, first_row, layer * own_lines, layers * own_lines
        )


def begin_update(column_pieces, row_pieces, share, layers, tile):
    pieces = len(column_pieces)
    half, _, width = row_pieces[0].shape

    def body(*refs):
        begin_kernel(pieces, layers, tile, *refs)

    return pl.pallas_call(
        body,
        out_shape=[
            jax.ShapeDtypeStruct(share.shape, jnp.float32),
            jax.ShapeDtypeStruct((half * tile, width), jnp.bfloat16),
            *[jax.ShapeDtypeStruct(row_pieces[0].shape, jnp.bfloat16)] * (pieces - 2),
        ],
        in_specs=[pl.BlockSpec(memory_space=pltpu.VMEM)] * (2 * pieces),
        out_specs=[pl.BlockSpec(memory_space=pltpu.VMEM)] * pieces,
        input_output_aliases={2 * pieces - 1: 0},
        compiler_params=pltpu.CompilerParams(vmem_limit_bytes=VMEM_BYTES),
        name="begin_update",
    )(*column_pieces, *row_pieces, share)


def end_kernel(pieces, layers, tile, *refs):
    others = pieces * (layers - 1)
    column_refs, row_refs, rest = refs[:others], refs[others : others + pieces], refs[others + pieces :]
    own_ref, share_ref, out_ref, _, columns_buf, last_buf, sems = rest
    r, c, layer = (lax.axis_index(axis) for axis in AXES)
    half, tile_rows, _ = row_refs[0].shape
    own_lines = half * tile // LANES
    per_row = layers * own_lines
    owners = [lax.rem(layer + shift, layers) for shift in range(1, layers)]
    for at, owner in enumerate(owners):
        fill_columns(
            columns_buf.at[at], column_refs[at * pieces : (at + 1) * pieces], plane_slots(pieces), r, c, owner
        )
    last_buf[...] = row_refs[-1][...]
    if pieces == 4:

        @pl.when(r == c)
        def _():
            take_rows(last_buf, own_ref, c, steps_of(pieces, r)[-1], pieces)

    stores = []
    for at_row, row_ref in enumerate((*row_refs[:-1], last_buf)):
        first_row = partner(c, steps_of(pieces, r)[at_row], pieces) * tile_rows
        rows = row_ref[...]
        for at, owner in enumerate(owners):
            subtract_product(share_ref, rows, columns_buf[at], tile, first_row, owner * own_lines, per_row)
        if at_row == pieces - 1:
            subtract_product(share_ref, rows, own_ref[...], tile, first_row, layer * own_lines, per_row)
        for k in range(half):
            lines = tile_rows * per_row
            start = pl.multiple_of((k * tile + first_row) * per_row, lines)
            store = pltpu.make_async_copy(
                share_ref.at[pl.ds(start, lines)], out_ref.at[pl.ds(start, lines)], sems.at[at_row * half + k]
            )
            store.start()
            stores.append(store)
    for store in stores:
        store.wait()


def end_update(column_pieces, row_pieces, own_columns, share, layers, tile):
    pieces = len(row_pieces)
    half = row_pieces[0].shape[0]
    per_row = layers * own_columns.shape[0] // LANES
    operands = (*column_pieces, *row_pieces, own_columns, share)

    def body(*refs):
        end_kernel(pieces, layers, tile, *refs)

    result, _ = pl.pallas_call(
        body,
        out_shape=[
            jax.ShapeDtypeStruct((half * pieces * row_pieces[0].shape[1] * per_row, LANES), jnp.float32),
            jax.ShapeDtypeStruct(share.shape, jnp.float32),
        ],
        in_specs=[pl.BlockSpec(memory_space=pltpu.VMEM)] * len(operands),
        out_specs=[pl.BlockSpec(memory_space=pltpu.HBM), pl.BlockSpec(memory_space=pltpu.VMEM)],
        scratch_shapes=[
            pltpu.VMEM((layers - 1, *own_columns.shape), jnp.bfloat16),
            pltpu.VMEM(row_pieces[0].shape, jnp.bfloat16),
            pltpu.SemaphoreType.DMA((half * pieces,)),
        ],
        input_output_aliases={len(operands) - 1: 1},
        compiler_params=pltpu.CompilerParams(vmem_limit_bytes=VMEM_BYTES),
        name="end_update",
    )(*operands)
    return result


def per_device(trailing, panel, inverse_factor):
    layers = lax.axis_size("layer")
    count = lax.axis_size("row")
    row_tiles, _, tile, col_tiles, _, _ = trailing.shape
    half = row_tiles // layers
    slots = plane_slots(count)
    factor = make_factor(panel, inverse_factor, half)
    moved = lax.ppermute(
        factor, ("row", "col"), [(a * count + b, slots[a][b] * count + a) for a in range(count) for b in range(count)]
    )
    share = load_share(factor, trailing.reshape(-1, LANES), layers, col_tiles * tile // LANES)
    loaded_factor, share = lax.optimization_barrier((factor, share))
    line = gather_line(factor, loaded_factor, moved, count)
    plane = [moved]
    for step in range(1, count):
        sources = {
            (r, c): (partner(r, plane_mates(count, c)[step], count), c) for r in range(count) for c in range(count)
        }
        if count == 4 and step == 1:
            sources[0, 0], sources[1, 1] = (0, 1), (3, 0)
        plane.append(move(moved, sources, count))
    if count == 4:
        r, c = lax.axis_index("row"), lax.axis_index("col")
        plane[1] = jnp.where((r == c) & (r < 2), factor, plane[1])
    others = []
    for shift in range(1, layers):
        pairs = [((l + shift) % layers, l) for l in range(layers)]
        others += [lax.ppermute(piece, "layer", pairs) for piece in plane]
    share, own_columns, *rows = begin_update(plane, line[:-1], share, layers, tile)
    rows = [line[0], *rows, line[-1]]
    result = end_update(others, rows, own_columns, share, layers, tile)
    return result.reshape(half, 1, tile, col_tiles, 1, tile)


def solution(mesh):
    assert mesh.shape["row"] == mesh.shape["col"]
    return jax.shard_map(
        per_device,
        mesh=mesh,
        in_specs=(P(None, "row", None, None, "col", None), P(None, "row", "col", None), P()),
        out_specs=P("layer", "row", None, None, "col", None),
        check_vma=False,
    )
```

```python
import jax
import jax.numpy as jnp
from jax import lax
from jax.experimental import pallas as pl
from jax.experimental.pallas import tpu as pltpu
from jax.sharding import PartitionSpec as P

LANES = 128
VMEM_BYTES = 24 * 1024 * 1024
LOAD_VMEM_BYTES = 52000 * 1024
FACTOR_VMEM_BYTES = 55040 * 1024
AXES = ("row", "col", "layer")


def split(x):
    parts = []
    for _ in range(3):
        parts.append(x.astype(jnp.bfloat16))
        x = x - parts[-1].astype(jnp.float32)
    return parts


def factor_kernel(panel_ref, inverse_ref, factor_ref, panel_buf, inverse_buf, sems):
    half = factor_ref.shape[0]
    tile_rows = factor_ref.shape[1]
    width = factor_ref.shape[2]
    layer = lax.axis_index("layer")
    copies = [
        pltpu.make_async_copy(panel_ref.at[pl.ds(layer * half, half), 0], panel_buf, sems.at[0]),
        pltpu.make_async_copy(inverse_ref, inverse_buf, sems.at[1]),
    ]
    for copy in copies:
        copy.start()
    for copy in copies:
        copy.wait()
    rows = half * tile_rows
    panel = split(panel_buf[...].reshape(rows, width))
    inverse = split(inverse_buf[...])

    def times(parts, part):
        return lax.dot_general(
            jnp.concatenate(parts, axis=0), part, (((1,), (1,)), ((), ())), preferred_element_type=jnp.float32
        )

    high = times(panel, inverse[0])
    middle = times(panel[:2], inverse[1])
    low = times(panel[:1], inverse[2])
    product = (low + middle[rows:]) + high[2 * rows :]
    product = (product + (middle[:rows] + high[rows : 2 * rows])) + high[:rows]
    factor_ref[...] = product.astype(jnp.bfloat16).reshape(factor_ref.shape)


def make_factor(panel, inverse_factor, half):
    _, _, tile_rows, width = panel.shape
    return pl.pallas_call(
        factor_kernel,
        out_shape=jax.ShapeDtypeStruct((half, tile_rows, width), jnp.bfloat16),
        in_specs=[pl.BlockSpec(memory_space=pltpu.HBM)] * 2,
        out_specs=pl.BlockSpec(memory_space=pltpu.VMEM),
        scratch_shapes=[
            pltpu.VMEM((half, tile_rows, width), jnp.float32),
            pltpu.VMEM((width, width), jnp.float32),
            pltpu.SemaphoreType.DMA((2,)),
        ],
        compiler_params=pltpu.CompilerParams(vmem_limit_bytes=FACTOR_VMEM_BYTES),
        name="factor",
    )(panel, inverse_factor)


def partner(index, step, count):
    return index ^ step if count & (count - 1) == 0 else (index + step) % count


def plane_slots(count):
    if count == 4:
        return ((3, 0, 1, 2), (3, 0, 2, 1), (3, 2, 1, 0), (2, 3, 1, 0))
    return tuple(tuple(count - 1 - b for b in range(count)) for _ in range(count))


def plane_mates(count, plane):
    if count == 4:
        return ((0, 3, 1, 2), (0, 1, 2, 3), (0, 2, 1, 3), (0, 2, 1, 3))[plane]
    return tuple(range(count))


def slab_of(slots, plane, place):
    if len(slots) == 4:
        packed = sum(row.index(p) << 2 * (4 * at + p) for at, row in enumerate(slots) for p in range(4))
        packed -= (packed >> 31) << 32
        return (jnp.int32(packed) >> (2 * (4 * plane + place))) & 3
    slab = jnp.int32(0)
    for at, row in enumerate(slots):
        for b, slot in enumerate(row):
            slab = jnp.where((plane == at) & (place == slot), b, slab)
    return slab


def line_steps(count):
    return (0, 2, 1, 3) if count == 4 else tuple(range(count))


def move(x, sources, count):
    return lax.ppermute(x, ("row", "col"), [(a * count + b, r * count + c) for (r, c), (a, b) in sources.items()])


def gather_line(factor, late_factor, moved, count):
    if count != 4:
        line = [factor]
        for step in range(1, count):
            line.append(lax.ppermute(factor, "col", [(partner(b, step, count), b) for b in range(count)]))
        return line
    places = [(r, c) for r in range(count) for c in range(count)]
    near = move(late_factor, {(r, c): (r ^ 1, c) if r == c else (r, c ^ 1) for r, c in places}, count)
    far = move(late_factor, {(r, c): (r ^ 2, c) if r == c and r % 2 == 1 else (r, c ^ 2) for r, c in places}, count)
    r, c = lax.axis_index("row"), lax.axis_index("col")
    relayed = jnp.where((r == c) & (r % 2 == 1), moved, far)
    relayed = jnp.where(r == c ^ 1, near, relayed)
    last = move(relayed, {(r, c): (r, c ^ 1) for r, c in places}, count)
    return [factor, far, near, last]


def load_kernel(rows, after_ref, lines_ref, share_ref, sem):
    layer = lax.axis_index("layer")
    load = pltpu.make_async_copy(lines_ref.at[pl.ds(layer * rows, rows)], share_ref.at[pl.ds(0, rows)], sem)
    load.start()
    load.wait()


def load_share(after, lines, layers, per_row):
    rows = lines.shape[0] // layers

    def body(*refs):
        load_kernel(rows, *refs)

    return pl.pallas_call(
        body,
        out_shape=jax.ShapeDtypeStruct((rows + per_row, LANES), jnp.float32),
        in_specs=[pl.BlockSpec(memory_space=pl.ANY), pl.BlockSpec(memory_space=pltpu.HBM)],
        out_specs=pl.BlockSpec(memory_space=pltpu.VMEM),
        scratch_shapes=[pltpu.SemaphoreType.DMA],
        compiler_params=pltpu.CompilerParams(vmem_limit_bytes=LOAD_VMEM_BYTES),
        cost_estimate=pl.CostEstimate(flops=0, bytes_accessed=rows * LANES * 8, transcendentals=0),
        name="load_share",
    )(after, lines)


def fill_columns(columns_ref, pieces, slots, r, c, owner):
    half, tile_rows, _ = pieces[0].shape
    tile = tile_rows * len(pieces)
    for step, piece in enumerate(pieces):
        mate = jnp.int32(plane_mates(len(pieces), 0)[step])
        for plane in range(1, len(pieces) if len(pieces) == 4 else 1):
            mate = jnp.where(c == plane, plane_mates(len(pieces), plane)[step], mate)
        slab = slab_of(slots, c, partner(r, mate, len(pieces)))
        for k in range(half):
            at = pl.multiple_of(k * tile + slab * tile_rows, tile_rows)
            columns_ref[pl.ds(at, tile_rows), :] = piece[k]


def product_of(rows, columns):
    half, tile_rows, width = rows.shape
    return lax.dot_general(
        rows.reshape(half * tile_rows, width),
        columns,
        (((1,), (1,)), ((), ())),
        preferred_element_type=jnp.float32,
    )


def subtract(share_ref, product, k, tile, tile_rows, first_row, first_line, per_row):
    for part in range(product.shape[1] // LANES):
        start = (k * tile + first_row) * per_row + first_line + part
        at = pl.ds(start, tile_rows, stride=per_row)
        share_ref[at, :] -= product[k * tile_rows : (k + 1) * tile_rows, part * LANES : (part + 1) * LANES]


def take_rows(rows_ref, columns_ref, c, step, pieces):
    half, tile_rows, _ = rows_ref.shape
    for k in range(half):
        at = pl.multiple_of((k * pieces + partner(c, step, pieces)) * tile_rows, tile_rows)
        rows_ref[k] = columns_ref[pl.ds(at, tile_rows), :]


def begin_kernel(pieces, layers, tile, *refs):
    column_refs, row_refs, rest = refs[:pieces], refs[pieces : 2 * pieces - 1], refs[2 * pieces - 1 :]
    loaded_ref, share_ref, columns_ref, *line_refs = rest
    r, c, layer = (lax.axis_index(axis) for axis in AXES)
    half, tile_rows, _ = row_refs[0].shape
    own_lines = half * tile // LANES
    share_ref[...] = loaded_ref[...]
    fill_columns(columns_ref, column_refs, plane_slots(pieces), r, c, layer)
    for line_ref, row_ref in zip(line_refs, row_refs[1:]):
        line_ref[...] = row_ref[...]
    if pieces == 4:

        @pl.when(r == c)
        def _():
            for step, line_ref in zip(line_steps(pieces)[1:], line_refs):
                take_rows(line_ref, columns_ref, c, step, pieces)

    for step, row_ref in zip(line_steps(pieces), (row_refs[0], *line_refs)):
        first_row = partner(c, step, pieces) * tile_rows
        product = product_of(row_ref[...], columns_ref[...])
        for k in range(half):
            subtract(share_ref, product, k, tile, tile_rows, first_row, layer * own_lines, layers * own_lines)


def begin_update(column_pieces, row_pieces, share, layers, tile):
    pieces = len(column_pieces)
    half, _, width = row_pieces[0].shape

    def body(*refs):
        begin_kernel(pieces, layers, tile, *refs)

    return pl.pallas_call(
        body,
        out_shape=[
            jax.ShapeDtypeStruct(share.shape, jnp.float32),
            jax.ShapeDtypeStruct((half * tile, width), jnp.bfloat16),
            *[jax.ShapeDtypeStruct(row_pieces[0].shape, jnp.bfloat16)] * (pieces - 2),
        ],
        in_specs=[pl.BlockSpec(memory_space=pltpu.VMEM)] * (2 * pieces),
        out_specs=[pl.BlockSpec(memory_space=pltpu.VMEM)] * pieces,
        input_output_aliases={2 * pieces - 1: 0},
        compiler_params=pltpu.CompilerParams(vmem_limit_bytes=VMEM_BYTES),
        name="begin_update",
    )(*column_pieces, *row_pieces, share)


def end_kernel(pieces, layers, tile, *refs):
    others = pieces * (layers - 1)
    column_refs, row_refs, rest = refs[:others], refs[others : others + pieces], refs[others + pieces :]
    own_ref, share_ref, out_ref, _, columns_buf, last_buf, sems = rest
    r, c, layer = (lax.axis_index(axis) for axis in AXES)
    half, tile_rows, _ = row_refs[0].shape
    own_lines = half * tile // LANES
    per_row = layers * own_lines
    owners = [lax.rem(layer + shift, layers) for shift in range(1, layers)]
    for at, owner in enumerate(owners):
        fill_columns(
            columns_buf.at[at], column_refs[at * pieces : (at + 1) * pieces], plane_slots(pieces), r, c, owner
        )
    last_buf[...] = row_refs[-1][...]
    if pieces == 4:

        @pl.when(r == c)
        def _():
            take_rows(last_buf, own_ref, c, line_steps(pieces)[-1], pieces)

    stores = []
    for at_row, row_ref in enumerate((*row_refs[:-1], last_buf)):
        first_row = partner(c, line_steps(pieces)[at_row], pieces) * tile_rows
        rows = row_ref[...]
        products = [(product_of(rows, columns_buf[at]), owner) for at, owner in enumerate(owners)]
        if at_row == pieces - 1:
            products.append((product_of(rows, own_ref[...]), layer))
        for k in range(half):
            for product, owner in products:
                subtract(share_ref, product, k, tile, tile_rows, first_row, owner * own_lines, per_row)
            lines = tile_rows * per_row
            start = pl.multiple_of((k * tile + first_row) * per_row, lines)
            store = pltpu.make_async_copy(
                share_ref.at[pl.ds(start, lines)], out_ref.at[pl.ds(start, lines)], sems.at[at_row * half + k]
            )
            store.start()
            stores.append(store)
    for store in stores:
        store.wait()


def end_update(column_pieces, row_pieces, own_columns, share, layers, tile):
    pieces = len(row_pieces)
    half = row_pieces[0].shape[0]
    per_row = layers * own_columns.shape[0] // LANES
    operands = (*column_pieces, *row_pieces, own_columns, share)

    def body(*refs):
        end_kernel(pieces, layers, tile, *refs)

    result, _ = pl.pallas_call(
        body,
        out_shape=[
            jax.ShapeDtypeStruct((half * pieces * row_pieces[0].shape[1] * per_row, LANES), jnp.float32),
            jax.ShapeDtypeStruct(share.shape, jnp.float32),
        ],
        in_specs=[pl.BlockSpec(memory_space=pltpu.VMEM)] * len(operands),
        out_specs=[pl.BlockSpec(memory_space=pltpu.HBM), pl.BlockSpec(memory_space=pltpu.VMEM)],
        scratch_shapes=[
            pltpu.VMEM((layers - 1, *own_columns.shape), jnp.bfloat16),
            pltpu.VMEM(row_pieces[0].shape, jnp.bfloat16),
            pltpu.SemaphoreType.DMA((half * pieces,)),
        ],
        input_output_aliases={len(operands) - 1: 1},
        compiler_params=pltpu.CompilerParams(vmem_limit_bytes=VMEM_BYTES),
        name="end_update",
    )(*operands)
    return result


def per_device(trailing, panel, inverse_factor):
    layers = lax.axis_size("layer")
    count = lax.axis_size("row")
    row_tiles, _, tile, col_tiles, _, _ = trailing.shape
    half = row_tiles // layers
    slots = plane_slots(count)
    factor = make_factor(panel, inverse_factor, half)
    moved = lax.ppermute(
        factor, ("row", "col"), [(a * count + b, slots[a][b] * count + a) for a in range(count) for b in range(count)]
    )
    share = load_share(factor, trailing.reshape(-1, LANES), layers, col_tiles * tile // LANES)
    loaded_factor, share = lax.optimization_barrier((factor, share))
    line = gather_line(factor, loaded_factor, moved, count)
    plane = [moved]
    for step in range(1, count):
        sources = {
            (r, c): (partner(r, plane_mates(count, c)[step], count), c) for r in range(count) for c in range(count)
        }
        if count == 4 and step == 1:
            sources[0, 0], sources[1, 1] = (0, 1), (3, 0)
        plane.append(move(moved, sources, count))
    if count == 4:
        r, c = lax.axis_index("row"), lax.axis_index("col")
        plane[1] = jnp.where((r == c) & (r < 2), factor, plane[1])
    others = []
    for shift in range(1, layers):
        pairs = [((l + shift) % layers, l) for l in range(layers)]
        others += [lax.ppermute(piece, "layer", pairs) for piece in plane]
    share, own_columns, *rows = begin_update(plane, line[:-1], share, layers, tile)
    rows = [line[0], *rows, line[-1]]
    result = end_update(others, rows, own_columns, share, layers, tile)
    return result.reshape(half, 1, tile, col_tiles, 1, tile)


def solution(mesh):
    assert mesh.shape["row"] == mesh.shape["col"]
    return jax.shard_map(
        per_device,
        mesh=mesh,
        in_specs=(P(None, "row", None, None, "col", None), P(None, "row", "col", None), P()),
        out_specs=P("layer", "row", None, None, "col", None),
        check_vma=False,
    )
```

```python
import jax
import jax.numpy as jnp
from jax import lax
from jax.experimental import pallas as pl
from jax.experimental.pallas import tpu as pltpu
from jax.sharding import PartitionSpec as P

LANES = 128
VMEM_BYTES = 24 * 1024 * 1024
LOAD_VMEM_BYTES = 52000 * 1024
FACTOR_VMEM_BYTES = 55040 * 1024
AXES = ("row", "col", "layer")


def split(x):
    parts = []
    for _ in range(3):
        parts.append(x.astype(jnp.bfloat16))
        x = x - parts[-1].astype(jnp.float32)
    return parts


def factor_kernel(panel_ref, inverse_ref, factor_ref, panel_buf, inverse_buf, sems):
    half = factor_ref.shape[0]
    tile_rows = factor_ref.shape[1]
    width = factor_ref.shape[2]
    layer = lax.axis_index("layer")
    copies = [
        pltpu.make_async_copy(panel_ref.at[pl.ds(layer * half, half), 0], panel_buf, sems.at[0]),
        pltpu.make_async_copy(inverse_ref, inverse_buf, sems.at[1]),
    ]
    for copy in copies:
        copy.start()
    for copy in copies:
        copy.wait()
    rows = half * tile_rows
    panel = split(panel_buf[...].reshape(rows, width))
    inverse = split(inverse_buf[...])

    def times(parts, part):
        return lax.dot_general(
            jnp.concatenate(parts, axis=0), part, (((1,), (1,)), ((), ())), preferred_element_type=jnp.float32
        )

    high = times(panel, inverse[0])
    middle = times(panel[:2], inverse[1])
    low = times(panel[:1], inverse[2])
    product = (low + middle[rows:]) + high[2 * rows :]
    product = (product + (middle[:rows] + high[rows : 2 * rows])) + high[:rows]
    factor_ref[...] = product.astype(jnp.bfloat16).reshape(factor_ref.shape)


def make_factor(panel, inverse_factor, half):
    _, _, tile_rows, width = panel.shape
    return pl.pallas_call(
        factor_kernel,
        out_shape=jax.ShapeDtypeStruct((half, tile_rows, width), jnp.bfloat16),
        in_specs=[pl.BlockSpec(memory_space=pltpu.HBM)] * 2,
        out_specs=pl.BlockSpec(memory_space=pltpu.VMEM),
        scratch_shapes=[
            pltpu.VMEM((half, tile_rows, width), jnp.float32),
            pltpu.VMEM((width, width), jnp.float32),
            pltpu.SemaphoreType.DMA((2,)),
        ],
        compiler_params=pltpu.CompilerParams(vmem_limit_bytes=FACTOR_VMEM_BYTES),
        name="factor",
    )(panel, inverse_factor)


def partner(index, step, count):
    return index ^ step if count & (count - 1) == 0 else (index + step) % count


def plane_slots(count):
    if count == 4:
        return ((3, 0, 1, 2), (3, 0, 2, 1), (3, 2, 1, 0), (2, 3, 1, 0))
    return tuple(tuple(count - 1 - b for b in range(count)) for _ in range(count))


def plane_mates(count, plane):
    if count == 4:
        return ((0, 3, 1, 2), (0, 1, 2, 3), (0, 2, 1, 3), (0, 2, 1, 3))[plane]
    return tuple(range(count))


def slab_of(slots, plane, place):
    if len(slots) == 4:
        packed = sum(row.index(p) << 2 * (4 * at + p) for at, row in enumerate(slots) for p in range(4))
        packed -= (packed >> 31) << 32
        return (jnp.int32(packed) >> (2 * (4 * plane + place))) & 3
    slab = jnp.int32(0)
    for at, row in enumerate(slots):
        for b, slot in enumerate(row):
            slab = jnp.where((plane == at) & (place == slot), b, slab)
    return slab


def line_steps(count):
    return (0, 2, 1, 3) if count == 4 else tuple(range(count))


def move(x, sources, count):
    return lax.ppermute(x, ("row", "col"), [(a * count + b, r * count + c) for (r, c), (a, b) in sources.items()])


def gather_line(factor, late_factor, moved, count):
    if count != 4:
        line = [factor]
        for step in range(1, count):
            line.append(lax.ppermute(factor, "col", [(partner(b, step, count), b) for b in range(count)]))
        return line
    places = [(r, c) for r in range(count) for c in range(count)]
    near = move(late_factor, {(r, c): (r ^ 1, c) if r == c else (r, c ^ 1) for r, c in places}, count)
    far = move(late_factor, {(r, c): (r ^ 2, c) if r == c and r % 2 == 1 else (r, c ^ 2) for r, c in places}, count)
    r, c = lax.axis_index("row"), lax.axis_index("col")
    relayed = jnp.where((r == c) & (r % 2 == 1), moved, far)
    relayed = jnp.where(r == c ^ 1, near, relayed)
    last = move(relayed, {(r, c): (r, c ^ 1) for r, c in places}, count)
    return [factor, far, near, last]


def load_kernel(rows, after_ref, lines_ref, share_ref, sem):
    layer = lax.axis_index("layer")
    load = pltpu.make_async_copy(lines_ref.at[pl.ds(layer * rows, rows)], share_ref.at[pl.ds(0, rows)], sem)
    load.start()
    load.wait()


def load_share(after, lines, layers, per_row):
    rows = lines.shape[0] // layers

    def body(*refs):
        load_kernel(rows, *refs)

    return pl.pallas_call(
        body,
        out_shape=jax.ShapeDtypeStruct((rows + per_row, LANES), jnp.float32),
        in_specs=[pl.BlockSpec(memory_space=pl.ANY), pl.BlockSpec(memory_space=pltpu.HBM)],
        out_specs=pl.BlockSpec(memory_space=pltpu.VMEM),
        scratch_shapes=[pltpu.SemaphoreType.DMA],
        compiler_params=pltpu.CompilerParams(vmem_limit_bytes=LOAD_VMEM_BYTES),
        cost_estimate=pl.CostEstimate(flops=0, bytes_accessed=rows * LANES * 8, transcendentals=0),
        name="load_share",
    )(after, lines)


def fill_columns(columns_ref, pieces, slots, r, c, owner):
    half, tile_rows, _ = pieces[0].shape
    tile = tile_rows * len(pieces)
    for step, piece in enumerate(pieces):
        mate = jnp.int32(plane_mates(len(pieces), 0)[step])
        for plane in range(1, len(pieces) if len(pieces) == 4 else 1):
            mate = jnp.where(c == plane, plane_mates(len(pieces), plane)[step], mate)
        slab = slab_of(slots, c, partner(r, mate, len(pieces)))
        for k in range(half):
            at = pl.multiple_of(k * tile + slab * tile_rows, tile_rows)
            columns_ref[pl.ds(at, tile_rows), :] = piece[k]


def product_of(rows, columns):
    half, tile_rows, width = rows.shape
    return lax.dot_general(
        rows.reshape(half * tile_rows, width),
        columns,
        (((1,), (1,)), ((), ())),
        preferred_element_type=jnp.float32,
    )


def subtract(share_ref, product, k, tile, tile_rows, first_row, first_line, per_row):
    for part in range(product.shape[1] // LANES):
        start = (k * tile + first_row) * per_row + first_line + part
        at = pl.ds(start, tile_rows, stride=per_row)
        share_ref[at, :] -= product[k * tile_rows : (k + 1) * tile_rows, part * LANES : (part + 1) * LANES]


def take_rows(rows_ref, columns_ref, c, step, pieces):
    half, tile_rows, _ = rows_ref.shape
    for k in range(half):
        at = pl.multiple_of((k * pieces + partner(c, step, pieces)) * tile_rows, tile_rows)
        rows_ref[k] = columns_ref[pl.ds(at, tile_rows), :]


def begin_kernel(pieces, layers, tile, *refs):
    column_refs, row_refs, rest = refs[:pieces], refs[pieces : 2 * pieces - 1], refs[2 * pieces - 1 :]
    loaded_ref, share_ref, columns_ref, *line_refs = rest
    r, c, layer = (lax.axis_index(axis) for axis in AXES)
    half, tile_rows, _ = row_refs[0].shape
    own_lines = half * tile // LANES
    share_ref[...] = loaded_ref[...]
    fill_columns(columns_ref, column_refs, plane_slots(pieces), r, c, layer)
    for line_ref, row_ref in zip(line_refs, row_refs[1:]):
        line_ref[...] = row_ref[...]
    if pieces == 4:

        @pl.when(r == c)
        def _():
            for step, line_ref in zip(line_steps(pieces)[1:], line_refs):
                take_rows(line_ref, columns_ref, c, step, pieces)

    for step, row_ref in zip(line_steps(pieces), (row_refs[0], *line_refs)):
        first_row = partner(c, step, pieces) * tile_rows
        product = product_of(row_ref[...], columns_ref[...])
        for k in range(half):
            subtract(share_ref, product, k, tile, tile_rows, first_row, layer * own_lines, layers * own_lines)


def begin_update(column_pieces, row_pieces, share, layers, tile):
    pieces = len(column_pieces)
    half, _, width = row_pieces[0].shape

    def body(*refs):
        begin_kernel(pieces, layers, tile, *refs)

    return pl.pallas_call(
        body,
        out_shape=[
            jax.ShapeDtypeStruct(share.shape, jnp.float32),
            jax.ShapeDtypeStruct((half * tile, width), jnp.bfloat16),
            *[jax.ShapeDtypeStruct(row_pieces[0].shape, jnp.bfloat16)] * (pieces - 2),
        ],
        in_specs=[pl.BlockSpec(memory_space=pltpu.VMEM)] * (2 * pieces),
        out_specs=[pl.BlockSpec(memory_space=pltpu.VMEM)] * pieces,
        input_output_aliases={2 * pieces - 1: 0},
        compiler_params=pltpu.CompilerParams(vmem_limit_bytes=VMEM_BYTES),
        name="begin_update",
    )(*column_pieces, *row_pieces, share)


def end_kernel(pieces, layers, tile, *refs):
    others = pieces * (layers - 1)
    column_refs, row_refs, rest = refs[:others], refs[others : others + pieces], refs[others + pieces :]
    own_ref, share_ref, out_ref, _, columns_buf, last_buf, sems = rest
    r, c, layer = (lax.axis_index(axis) for axis in AXES)
    half, tile_rows, _ = row_refs[0].shape
    own_lines = half * tile // LANES
    per_row = layers * own_lines
    owners = [lax.rem(layer + shift, layers) for shift in range(1, layers)]
    for at, owner in enumerate(owners):
        fill_columns(
            columns_buf.at[at], column_refs[at * pieces : (at + 1) * pieces], plane_slots(pieces), r, c, owner
        )
    last_buf[...] = row_refs[-1][...]
    if pieces == 4:

        @pl.when(r == c)
        def _():
            take_rows(last_buf, own_ref, c, line_steps(pieces)[-1], pieces)

    stores = []
    for at_row, row_ref in enumerate((*row_refs[:-1], last_buf)):
        first_row = partner(c, line_steps(pieces)[at_row], pieces) * tile_rows
        rows = row_ref[...]
        products = [(product_of(rows, columns_buf[at]), owner) for at, owner in enumerate(owners)]
        if at_row == pieces - 1:
            products.append((product_of(rows, own_ref[...]), layer))
        for k in range(half):
            for product, owner in products:
                subtract(share_ref, product, k, tile, tile_rows, first_row, owner * own_lines, per_row)
            lines = tile_rows * per_row
            start = pl.multiple_of((k * tile + first_row) * per_row, lines)
            store = pltpu.make_async_copy(
                share_ref.at[pl.ds(start, lines)], out_ref.at[pl.ds(start, lines)], sems.at[at_row * half + k]
            )
            store.start(priority=k % 2)
            stores.append(store)
    for store in stores:
        store.wait()


def end_update(column_pieces, row_pieces, own_columns, share, layers, tile):
    pieces = len(row_pieces)
    half = row_pieces[0].shape[0]
    per_row = layers * own_columns.shape[0] // LANES
    operands = (*column_pieces, *row_pieces, own_columns, share)

    def body(*refs):
        end_kernel(pieces, layers, tile, *refs)

    result, _ = pl.pallas_call(
        body,
        out_shape=[
            jax.ShapeDtypeStruct((half * pieces * row_pieces[0].shape[1] * per_row, LANES), jnp.float32),
            jax.ShapeDtypeStruct(share.shape, jnp.float32),
        ],
        in_specs=[pl.BlockSpec(memory_space=pltpu.VMEM)] * len(operands),
        out_specs=[pl.BlockSpec(memory_space=pltpu.HBM), pl.BlockSpec(memory_space=pltpu.VMEM)],
        scratch_shapes=[
            pltpu.VMEM((layers - 1, *own_columns.shape), jnp.bfloat16),
            pltpu.VMEM(row_pieces[0].shape, jnp.bfloat16),
            pltpu.SemaphoreType.DMA((half * pieces,)),
        ],
        input_output_aliases={len(operands) - 1: 1},
        compiler_params=pltpu.CompilerParams(vmem_limit_bytes=VMEM_BYTES),
        name="end_update",
    )(*operands)
    return result


def per_device(trailing, panel, inverse_factor):
    layers = lax.axis_size("layer")
    count = lax.axis_size("row")
    row_tiles, _, tile, col_tiles, _, _ = trailing.shape
    half = row_tiles // layers
    slots = plane_slots(count)
    factor = make_factor(panel, inverse_factor, half)
    moved = lax.ppermute(
        factor, ("row", "col"), [(a * count + b, slots[a][b] * count + a) for a in range(count) for b in range(count)]
    )
    share = load_share(factor, trailing.reshape(-1, LANES), layers, col_tiles * tile // LANES)
    loaded_factor, share = lax.optimization_barrier((factor, share))
    line = gather_line(factor, loaded_factor, moved, count)
    plane = [moved]
    for step in range(1, count):
        sources = {
            (r, c): (partner(r, plane_mates(count, c)[step], count), c) for r in range(count) for c in range(count)
        }
        if count == 4 and step == 1:
            sources[0, 0], sources[1, 1] = (0, 1), (3, 0)
        plane.append(move(moved, sources, count))
    if count == 4:
        r, c = lax.axis_index("row"), lax.axis_index("col")
        plane[1] = jnp.where((r == c) & (r < 2), factor, plane[1])
    others = []
    for shift in range(1, layers):
        pairs = [((l + shift) % layers, l) for l in range(layers)]
        others += [lax.ppermute(piece, "layer", pairs) for piece in plane]
    share, own_columns, *rows = begin_update(plane, line[:-1], share, layers, tile)
    rows = [line[0], *rows, line[-1]]
    result = end_update(others, rows, own_columns, share, layers, tile)
    return result.reshape(half, 1, tile, col_tiles, 1, tile)


def solution(mesh):
    assert mesh.shape["row"] == mesh.shape["col"]
    return jax.shard_map(
        per_device,
        mesh=mesh,
        in_specs=(P(None, "row", None, None, "col", None), P(None, "row", "col", None), P()),
        out_specs=P("layer", "row", None, None, "col", None),
        check_vma=False,
    )
```

```python
import jax
import jax.numpy as jnp
from jax import lax
from jax.experimental import pallas as pl
from jax.experimental.pallas import tpu as pltpu
from jax.sharding import PartitionSpec as P

LANES = 128
VMEM_BYTES = 24 * 1024 * 1024
LOAD_VMEM_BYTES = 52000 * 1024
FACTOR_VMEM_BYTES = 55040 * 1024
AXES = ("row", "col", "layer")


def split(x):
    parts = []
    for _ in range(3):
        parts.append(x.astype(jnp.bfloat16))
        x = x - parts[-1].astype(jnp.float32)
    return parts


def factor_kernel(panel_ref, inverse_ref, factor_ref, panel_buf, inverse_buf, sems):
    half = factor_ref.shape[0]
    tile_rows = factor_ref.shape[1]
    width = factor_ref.shape[2]
    layer = lax.axis_index("layer")
    copies = [
        pltpu.make_async_copy(panel_ref.at[pl.ds(layer * half, half), 0], panel_buf, sems.at[0]),
        pltpu.make_async_copy(inverse_ref, inverse_buf, sems.at[1]),
    ]
    for copy in copies:
        copy.start()
    for copy in copies:
        copy.wait()
    rows = half * tile_rows
    panel = split(panel_buf[...].reshape(rows, width))
    inverse = split(inverse_buf[...])

    def times(parts, part):
        return lax.dot_general(
            jnp.concatenate(parts, axis=0), part, (((1,), (1,)), ((), ())), preferred_element_type=jnp.float32
        )

    high = times(panel, inverse[0])
    middle = times(panel[:2], inverse[1])
    low = times(panel[:1], inverse[2])
    product = (low + middle[rows:]) + high[2 * rows :]
    product = (product + (middle[:rows] + high[rows : 2 * rows])) + high[:rows]
    factor_ref[...] = product.astype(jnp.bfloat16).reshape(factor_ref.shape)


def make_factor(panel, inverse_factor, half):
    _, _, tile_rows, width = panel.shape
    return pl.pallas_call(
        factor_kernel,
        out_shape=jax.ShapeDtypeStruct((half, tile_rows, width), jnp.bfloat16),
        in_specs=[pl.BlockSpec(memory_space=pltpu.HBM)] * 2,
        out_specs=pl.BlockSpec(memory_space=pltpu.VMEM),
        scratch_shapes=[
            pltpu.VMEM((half, tile_rows, width), jnp.float32),
            pltpu.VMEM((width, width), jnp.float32),
            pltpu.SemaphoreType.DMA((2,)),
        ],
        compiler_params=pltpu.CompilerParams(vmem_limit_bytes=FACTOR_VMEM_BYTES),
        name="factor",
    )(panel, inverse_factor)


def partner(index, step, count):
    return index ^ step if count & (count - 1) == 0 else (index + step) % count


def plane_slots(count):
    if count == 4:
        return ((3, 0, 1, 2), (3, 0, 2, 1), (3, 2, 1, 0), (2, 3, 1, 0))
    return tuple(tuple(count - 1 - b for b in range(count)) for _ in range(count))


def plane_mates(count, plane):
    if count == 4:
        return ((0, 3, 2, 1), (0, 1, 2, 3), (0, 2, 1, 3), (0, 2, 1, 3))[plane]
    return tuple(range(count))


def slab_of(slots, plane, place):
    if len(slots) == 4:
        packed = sum(row.index(p) << 2 * (4 * at + p) for at, row in enumerate(slots) for p in range(4))
        packed -= (packed >> 31) << 32
        return (jnp.int32(packed) >> (2 * (4 * plane + place))) & 3
    slab = jnp.int32(0)
    for at, row in enumerate(slots):
        for b, slot in enumerate(row):
            slab = jnp.where((plane == at) & (place == slot), b, slab)
    return slab


def line_steps(count):
    return (0, 2, 1, 3) if count == 4 else tuple(range(count))


def move(x, sources, count):
    return lax.ppermute(x, ("row", "col"), [(a * count + b, r * count + c) for (r, c), (a, b) in sources.items()])


def gather_line(factor, late_factor, moved, count):
    if count != 4:
        line = [factor]
        for step in range(1, count):
            line.append(lax.ppermute(factor, "col", [(partner(b, step, count), b) for b in range(count)]))
        return line
    places = [(r, c) for r in range(count) for c in range(count)]
    near = move(late_factor, {(r, c): (r ^ 1, c) if r == c else (r, c ^ 1) for r, c in places}, count)
    far = move(late_factor, {(r, c): (r ^ 2, c) if r == c and r % 2 == 1 else (r, c ^ 2) for r, c in places}, count)
    r, c = lax.axis_index("row"), lax.axis_index("col")
    relayed = jnp.where((r == c) & (r % 2 == 1), moved, far)
    relayed = jnp.where(r == c ^ 1, near, relayed)
    last = move(relayed, {(r, c): (r, c ^ 1) for r, c in places}, count)
    return [factor, far, near, last]


def load_kernel(rows, after_ref, lines_ref, share_ref, sem):
    layer = lax.axis_index("layer")
    load = pltpu.make_async_copy(lines_ref.at[pl.ds(layer * rows, rows)], share_ref.at[pl.ds(0, rows)], sem)
    load.start()
    load.wait()


def load_share(after, lines, layers, per_row):
    rows = lines.shape[0] // layers

    def body(*refs):
        load_kernel(rows, *refs)

    return pl.pallas_call(
        body,
        out_shape=jax.ShapeDtypeStruct((rows + per_row, LANES), jnp.float32),
        in_specs=[pl.BlockSpec(memory_space=pl.ANY), pl.BlockSpec(memory_space=pltpu.HBM)],
        out_specs=pl.BlockSpec(memory_space=pltpu.VMEM),
        scratch_shapes=[pltpu.SemaphoreType.DMA],
        compiler_params=pltpu.CompilerParams(vmem_limit_bytes=LOAD_VMEM_BYTES),
        cost_estimate=pl.CostEstimate(flops=0, bytes_accessed=rows * LANES * 8, transcendentals=0),
        name="load_share",
    )(after, lines)


def fill_columns(columns_ref, pieces, slots, r, c, owner):
    half, tile_rows, _ = pieces[0].shape
    tile = tile_rows * len(pieces)
    for step, piece in enumerate(pieces):
        mate = jnp.int32(plane_mates(len(pieces), 0)[step])
        for plane in range(1, len(pieces) if len(pieces) == 4 else 1):
            mate = jnp.where(c == plane, plane_mates(len(pieces), plane)[step], mate)
        slab = slab_of(slots, c, partner(r, mate, len(pieces)))
        for k in range(half):
            at = pl.multiple_of(k * tile + slab * tile_rows, tile_rows)
            columns_ref[pl.ds(at, tile_rows), :] = piece[k]


def product_of(rows, columns):
    half, tile_rows, width = rows.shape
    return lax.dot_general(
        rows.reshape(half * tile_rows, width),
        columns,
        (((1,), (1,)), ((), ())),
        preferred_element_type=jnp.float32,
    )


def subtract(share_ref, product, k, tile, tile_rows, first_row, first_line, per_row):
    for part in range(product.shape[1] // LANES):
        start = (k * tile + first_row) * per_row + first_line + part
        at = pl.ds(start, tile_rows, stride=per_row)
        share_ref[at, :] -= product[k * tile_rows : (k + 1) * tile_rows, part * LANES : (part + 1) * LANES]


def take_rows(rows_ref, columns_ref, c, step, pieces):
    half, tile_rows, _ = rows_ref.shape
    for k in range(half):
        at = pl.multiple_of((k * pieces + partner(c, step, pieces)) * tile_rows, tile_rows)
        rows_ref[k] = columns_ref[pl.ds(at, tile_rows), :]


def begin_kernel(pieces, layers, tile, *refs):
    column_refs, row_refs, rest = refs[:pieces], refs[pieces : 2 * pieces - 1], refs[2 * pieces - 1 :]
    loaded_ref, share_ref, columns_ref, *line_refs = rest
    r, c, layer = (lax.axis_index(axis) for axis in AXES)
    half, tile_rows, _ = row_refs[0].shape
    own_lines = half * tile // LANES
    share_ref[...] = loaded_ref[...]
    fill_columns(columns_ref, column_refs, plane_slots(pieces), r, c, layer)
    for line_ref, row_ref in zip(line_refs, row_refs[1:]):
        line_ref[...] = row_ref[...]
    if pieces == 4:

        @pl.when(r == c)
        def _():
            for step, line_ref in zip(line_steps(pieces)[1:], line_refs):
                take_rows(line_ref, columns_ref, c, step, pieces)

    for step, row_ref in zip(line_steps(pieces), (row_refs[0], *line_refs)):
        first_row = partner(c, step, pieces) * tile_rows
        product = product_of(row_ref[...], columns_ref[...])
        for k in range(half):
            subtract(share_ref, product, k, tile, tile_rows, first_row, layer * own_lines, layers * own_lines)


def begin_update(column_pieces, row_pieces, share, layers, tile):
    pieces = len(column_pieces)
    half, _, width = row_pieces[0].shape

    def body(*refs):
        begin_kernel(pieces, layers, tile, *refs)

    return pl.pallas_call(
        body,
        out_shape=[
            jax.ShapeDtypeStruct(share.shape, jnp.float32),
            jax.ShapeDtypeStruct((half * tile, width), jnp.bfloat16),
            *[jax.ShapeDtypeStruct(row_pieces[0].shape, jnp.bfloat16)] * (pieces - 2),
        ],
        in_specs=[pl.BlockSpec(memory_space=pltpu.VMEM)] * (2 * pieces),
        out_specs=[pl.BlockSpec(memory_space=pltpu.VMEM)] * pieces,
        input_output_aliases={2 * pieces - 1: 0},
        compiler_params=pltpu.CompilerParams(vmem_limit_bytes=VMEM_BYTES),
        name="begin_update",
    )(*column_pieces, *row_pieces, share)


def end_kernel(pieces, layers, tile, *refs):
    others = pieces * (layers - 1)
    column_refs, row_refs, rest = refs[:others], refs[others : others + pieces], refs[others + pieces :]
    own_ref, share_ref, out_ref, _, columns_buf, last_buf, sems = rest
    r, c, layer = (lax.axis_index(axis) for axis in AXES)
    half, tile_rows, _ = row_refs[0].shape
    own_lines = half * tile // LANES
    per_row = layers * own_lines
    owners = [lax.rem(layer + shift, layers) for shift in range(1, layers)]
    for at, owner in enumerate(owners):
        fill_columns(
            columns_buf.at[at], column_refs[at * pieces : (at + 1) * pieces], plane_slots(pieces), r, c, owner
        )
    last_buf[...] = row_refs[-1][...]
    if pieces == 4:

        @pl.when(r == c)
        def _():
            take_rows(last_buf, own_ref, c, line_steps(pieces)[-1], pieces)

    stores = []
    for at_row, row_ref in enumerate((*row_refs[:-1], last_buf)):
        first_row = partner(c, line_steps(pieces)[at_row], pieces) * tile_rows
        rows = row_ref[...]
        products = [(product_of(rows, columns_buf[at]), owner) for at, owner in enumerate(owners)]
        if at_row == pieces - 1:
            products.append((product_of(rows, own_ref[...]), layer))
        for k in range(half):
            for product, owner in products:
                subtract(share_ref, product, k, tile, tile_rows, first_row, owner * own_lines, per_row)
            lines = tile_rows * per_row
            start = pl.multiple_of((k * tile + first_row) * per_row, lines)
            store = pltpu.make_async_copy(
                share_ref.at[pl.ds(start, lines)], out_ref.at[pl.ds(start, lines)], sems.at[at_row * half + k]
            )
            store.start()
            stores.append(store)
    for store in stores:
        store.wait()


def end_update(column_pieces, row_pieces, own_columns, share, layers, tile):
    pieces = len(row_pieces)
    half = row_pieces[0].shape[0]
    per_row = layers * own_columns.shape[0] // LANES
    operands = (*column_pieces, *row_pieces, own_columns, share)

    def body(*refs):
        end_kernel(pieces, layers, tile, *refs)

    result, _ = pl.pallas_call(
        body,
        out_shape=[
            jax.ShapeDtypeStruct((half * pieces * row_pieces[0].shape[1] * per_row, LANES), jnp.float32),
            jax.ShapeDtypeStruct(share.shape, jnp.float32),
        ],
        in_specs=[pl.BlockSpec(memory_space=pltpu.VMEM)] * len(operands),
        out_specs=[pl.BlockSpec(memory_space=pltpu.HBM), pl.BlockSpec(memory_space=pltpu.VMEM)],
        scratch_shapes=[
            pltpu.VMEM((layers - 1, *own_columns.shape), jnp.bfloat16),
            pltpu.VMEM(row_pieces[0].shape, jnp.bfloat16),
            pltpu.SemaphoreType.DMA((half * pieces,)),
        ],
        input_output_aliases={len(operands) - 1: 1},
        compiler_params=pltpu.CompilerParams(vmem_limit_bytes=VMEM_BYTES),
        name="end_update",
    )(*operands)
    return result


def per_device(trailing, panel, inverse_factor):
    layers = lax.axis_size("layer")
    count = lax.axis_size("row")
    row_tiles, _, tile, col_tiles, _, _ = trailing.shape
    half = row_tiles // layers
    slots = plane_slots(count)
    factor = make_factor(panel, inverse_factor, half)
    moved = lax.ppermute(
        factor, ("row", "col"), [(a * count + b, slots[a][b] * count + a) for a in range(count) for b in range(count)]
    )
    share = load_share(factor, trailing.reshape(-1, LANES), layers, col_tiles * tile // LANES)
    loaded_factor, share = lax.optimization_barrier((factor, share))
    line = gather_line(factor, loaded_factor, moved, count)
    plane = [moved]
    for step in range(1, count):
        sources = {
            (r, c): (partner(r, plane_mates(count, c)[step], count), c) for r in range(count) for c in range(count)
        }
        if count == 4 and step == 1:
            sources[0, 0], sources[1, 1] = (0, 1), (3, 0)
        plane.append(move(moved, sources, count))
    if count == 4:
        r, c = lax.axis_index("row"), lax.axis_index("col")
        plane[1] = jnp.where((r == c) & (r < 2), factor, plane[1])
    others = []
    for shift in range(1, layers):
        pairs = [((l + shift) % layers, l) for l in range(layers)]
        others += [lax.ppermute(piece, "layer", pairs) for piece in plane]
    share, own_columns, *rows = begin_update(plane, line[:-1], share, layers, tile)
    rows = [line[0], *rows, line[-1]]
    result = end_update(others, rows, own_columns, share, layers, tile)
    return result.reshape(half, 1, tile, col_tiles, 1, tile)


def solution(mesh):
    assert mesh.shape["row"] == mesh.shape["col"]
    return jax.shard_map(
        per_device,
        mesh=mesh,
        in_specs=(P(None, "row", None, None, "col", None), P(None, "row", "col", None), P()),
        out_specs=P("layer", "row", None, None, "col", None),
        check_vma=False,
    )
```

```python
import jax
import jax.numpy as jnp
from jax import lax
from jax.experimental import pallas as pl
from jax.experimental.pallas import tpu as pltpu
from jax.sharding import PartitionSpec as P

LANES = 128
VMEM_BYTES = 24 * 1024 * 1024
LOAD_VMEM_BYTES = 52000 * 1024
FACTOR_VMEM_BYTES = 55040 * 1024
AXES = ("row", "col", "layer")


def split(x):
    parts = []
    for _ in range(3):
        parts.append(x.astype(jnp.bfloat16))
        x = x - parts[-1].astype(jnp.float32)
    return parts


def factor_kernel(panel_ref, inverse_ref, factor_ref, panel_buf, inverse_buf, sems):
    half = factor_ref.shape[0]
    tile_rows = factor_ref.shape[1]
    width = factor_ref.shape[2]
    layer = lax.axis_index("layer")
    panel_copy = pltpu.make_async_copy(panel_ref.at[pl.ds(layer * half, half), 0], panel_buf, sems.at[0])
    inverse_copy = pltpu.make_async_copy(inverse_ref, inverse_buf, sems.at[1])
    inverse_copy.start()
    panel_copy.start()
    inverse_copy.wait()
    inverse = split(inverse_buf[...])
    panel_copy.wait()
    rows = half * tile_rows
    panel = split(panel_buf[...].reshape(rows, width))

    def times(parts, part):
        return lax.dot_general(
            jnp.concatenate(parts, axis=0), part, (((1,), (1,)), ((), ())), preferred_element_type=jnp.float32
        )

    high = times(panel, inverse[0])
    middle = times(panel[:2], inverse[1])
    low = times(panel[:1], inverse[2])
    product = (low + middle[rows:]) + high[2 * rows :]
    product = (product + (middle[:rows] + high[rows : 2 * rows])) + high[:rows]
    factor_ref[...] = product.astype(jnp.bfloat16).reshape(factor_ref.shape)


def make_factor(panel, inverse_factor, half):
    _, _, tile_rows, width = panel.shape
    return pl.pallas_call(
        factor_kernel,
        out_shape=jax.ShapeDtypeStruct((half, tile_rows, width), jnp.bfloat16),
        in_specs=[pl.BlockSpec(memory_space=pltpu.HBM)] * 2,
        out_specs=pl.BlockSpec(memory_space=pltpu.VMEM),
        scratch_shapes=[
            pltpu.VMEM((half, tile_rows, width), jnp.float32),
            pltpu.VMEM((width, width), jnp.float32),
            pltpu.SemaphoreType.DMA((2,)),
        ],
        compiler_params=pltpu.CompilerParams(vmem_limit_bytes=FACTOR_VMEM_BYTES),
        name="factor",
    )(panel, inverse_factor)


def partner(index, step, count):
    return index ^ step if count & (count - 1) == 0 else (index + step) % count


def plane_slots(count):
    if count == 4:
        return ((3, 0, 1, 2), (3, 0, 2, 1), (3, 2, 1, 0), (2, 3, 1, 0))
    return tuple(tuple(count - 1 - b for b in range(count)) for _ in range(count))


def plane_mates(count, plane):
    if count == 4:
        return ((0, 3, 1, 2), (0, 1, 2, 3), (0, 2, 1, 3), (0, 2, 1, 3))[plane]
    return tuple(range(count))


def slab_of(slots, plane, place):
    if len(slots) == 4:
        packed = sum(row.index(p) << 2 * (4 * at + p) for at, row in enumerate(slots) for p in range(4))
        packed -= (packed >> 31) << 32
        return (jnp.int32(packed) >> (2 * (4 * plane + place))) & 3
    slab = jnp.int32(0)
    for at, row in enumerate(slots):
        for b, slot in enumerate(row):
            slab = jnp.where((plane == at) & (place == slot), b, slab)
    return slab


def line_steps(count):
    return (0, 2, 1, 3) if count == 4 else tuple(range(count))


def move(x, sources, count):
    return lax.ppermute(x, ("row", "col"), [(a * count + b, r * count + c) for (r, c), (a, b) in sources.items()])


def gather_line(factor, late_factor, moved, count):
    if count != 4:
        line = [factor]
        for step in range(1, count):
            line.append(lax.ppermute(factor, "col", [(partner(b, step, count), b) for b in range(count)]))
        return line
    places = [(r, c) for r in range(count) for c in range(count)]
    near = move(late_factor, {(r, c): (r ^ 1, c) if r == c else (r, c ^ 1) for r, c in places}, count)
    far = move(late_factor, {(r, c): (r ^ 2, c) if r == c and r % 2 == 1 else (r, c ^ 2) for r, c in places}, count)
    r, c = lax.axis_index("row"), lax.axis_index("col")
    relayed = jnp.where((r == c) & (r % 2 == 1), moved, far)
    relayed = jnp.where(r == c ^ 1, near, relayed)
    last = move(relayed, {(r, c): (r, c ^ 1) for r, c in places}, count)
    return [factor, far, near, last]


def load_kernel(rows, after_ref, lines_ref, share_ref, sem):
    layer = lax.axis_index("layer")
    load = pltpu.make_async_copy(lines_ref.at[pl.ds(layer * rows, rows)], share_ref.at[pl.ds(0, rows)], sem)
    load.start()
    load.wait()


def load_share(after, lines, layers, per_row):
    rows = lines.shape[0] // layers

    def body(*refs):
        load_kernel(rows, *refs)

    return pl.pallas_call(
        body,
        out_shape=jax.ShapeDtypeStruct((rows + per_row, LANES), jnp.float32),
        in_specs=[pl.BlockSpec(memory_space=pl.ANY), pl.BlockSpec(memory_space=pltpu.HBM)],
        out_specs=pl.BlockSpec(memory_space=pltpu.VMEM),
        scratch_shapes=[pltpu.SemaphoreType.DMA],
        compiler_params=pltpu.CompilerParams(vmem_limit_bytes=LOAD_VMEM_BYTES),
        cost_estimate=pl.CostEstimate(flops=0, bytes_accessed=rows * LANES * 8, transcendentals=0),
        name="load_share",
    )(after, lines)


def fill_columns(columns_ref, pieces, slots, r, c, owner):
    half, tile_rows, _ = pieces[0].shape
    tile = tile_rows * len(pieces)
    for step, piece in enumerate(pieces):
        mate = jnp.int32(plane_mates(len(pieces), 0)[step])
        for plane in range(1, len(pieces) if len(pieces) == 4 else 1):
            mate = jnp.where(c == plane, plane_mates(len(pieces), plane)[step], mate)
        slab = slab_of(slots, c, partner(r, mate, len(pieces)))
        for k in range(half):
            at = pl.multiple_of(k * tile + slab * tile_rows, tile_rows)
            columns_ref[pl.ds(at, tile_rows), :] = piece[k]


def product_of(rows, columns):
    half, tile_rows, width = rows.shape
    return lax.dot_general(
        rows.reshape(half * tile_rows, width),
        columns,
        (((1,), (1,)), ((), ())),
        preferred_element_type=jnp.float32,
    )


def subtract(share_ref, product, k, tile, tile_rows, first_row, first_line, per_row):
    for part in range(product.shape[1] // LANES):
        start = (k * tile + first_row) * per_row + first_line + part
        at = pl.ds(start, tile_rows, stride=per_row)
        share_ref[at, :] -= product[k * tile_rows : (k + 1) * tile_rows, part * LANES : (part + 1) * LANES]


def take_rows(rows_ref, columns_ref, c, step, pieces):
    half, tile_rows, _ = rows_ref.shape
    for k in range(half):
        at = pl.multiple_of((k * pieces + partner(c, step, pieces)) * tile_rows, tile_rows)
        rows_ref[k] = columns_ref[pl.ds(at, tile_rows), :]


def begin_kernel(pieces, layers, tile, *refs):
    column_refs, row_refs, rest = refs[:pieces], refs[pieces : 2 * pieces - 1], refs[2 * pieces - 1 :]
    loaded_ref, share_ref, columns_ref, *line_refs = rest
    r, c, layer = (lax.axis_index(axis) for axis in AXES)
    half, tile_rows, _ = row_refs[0].shape
    own_lines = half * tile // LANES
    share_ref[...] = loaded_ref[...]
    fill_columns(columns_ref, column_refs, plane_slots(pieces), r, c, layer)
    for line_ref, row_ref in zip(line_refs, row_refs[1:]):
        line_ref[...] = row_ref[...]
    if pieces == 4:

        @pl.when(r == c)
        def _():
            for step, line_ref in zip(line_steps(pieces)[1:], line_refs):
                take_rows(line_ref, columns_ref, c, step, pieces)

    for step, row_ref in zip(line_steps(pieces), (row_refs[0], *line_refs)):
        first_row = partner(c, step, pieces) * tile_rows
        product = product_of(row_ref[...], columns_ref[...])
        for k in range(half):
            subtract(share_ref, product, k, tile, tile_rows, first_row, layer * own_lines, layers * own_lines)


def begin_update(column_pieces, row_pieces, share, layers, tile):
    pieces = len(column_pieces)
    half, _, width = row_pieces[0].shape

    def body(*refs):
        begin_kernel(pieces, layers, tile, *refs)

    return pl.pallas_call(
        body,
        out_shape=[
            jax.ShapeDtypeStruct(share.shape, jnp.float32),
            jax.ShapeDtypeStruct((half * tile, width), jnp.bfloat16),
            *[jax.ShapeDtypeStruct(row_pieces[0].shape, jnp.bfloat16)] * (pieces - 2),
        ],
        in_specs=[pl.BlockSpec(memory_space=pltpu.VMEM)] * (2 * pieces),
        out_specs=[pl.BlockSpec(memory_space=pltpu.VMEM)] * pieces,
        input_output_aliases={2 * pieces - 1: 0},
        compiler_params=pltpu.CompilerParams(vmem_limit_bytes=VMEM_BYTES),
        name="begin_update",
    )(*column_pieces, *row_pieces, share)


def end_kernel(pieces, layers, tile, *refs):
    others = pieces * (layers - 1)
    column_refs, row_refs, rest = refs[:others], refs[others : others + pieces], refs[others + pieces :]
    own_ref, share_ref, out_ref, _, columns_buf, last_buf, sems = rest
    r, c, layer = (lax.axis_index(axis) for axis in AXES)
    half, tile_rows, _ = row_refs[0].shape
    own_lines = half * tile // LANES
    per_row = layers * own_lines
    owners = [lax.rem(layer + shift, layers) for shift in range(1, layers)]
    for at, owner in enumerate(owners):
        fill_columns(
            columns_buf.at[at], column_refs[at * pieces : (at + 1) * pieces], plane_slots(pieces), r, c, owner
        )
    last_buf[...] = row_refs[-1][...]
    if pieces == 4:

        @pl.when(r == c)
        def _():
            take_rows(last_buf, own_ref, c, line_steps(pieces)[-1], pieces)

    stores = []
    for at_row, row_ref in enumerate((*row_refs[:-1], last_buf)):
        first_row = partner(c, line_steps(pieces)[at_row], pieces) * tile_rows
        rows = row_ref[...]
        products = [(product_of(rows, columns_buf[at]), owner) for at, owner in enumerate(owners)]
        if at_row == pieces - 1:
            products.append((product_of(rows, own_ref[...]), layer))
        for k in range(half):
            for product, owner in products:
                subtract(share_ref, product, k, tile, tile_rows, first_row, owner * own_lines, per_row)
            lines = tile_rows * per_row
            start = pl.multiple_of((k * tile + first_row) * per_row, lines)
            store = pltpu.make_async_copy(
                share_ref.at[pl.ds(start, lines)], out_ref.at[pl.ds(start, lines)], sems.at[at_row * half + k]
            )
            store.start()
            stores.append(store)
    for store in stores:
        store.wait()


def end_update(column_pieces, row_pieces, own_columns, share, layers, tile):
    pieces = len(row_pieces)
    half = row_pieces[0].shape[0]
    per_row = layers * own_columns.shape[0] // LANES
    operands = (*column_pieces, *row_pieces, own_columns, share)

    def body(*refs):
        end_kernel(pieces, layers, tile, *refs)

    result, _ = pl.pallas_call(
        body,
        out_shape=[
            jax.ShapeDtypeStruct((half * pieces * row_pieces[0].shape[1] * per_row, LANES), jnp.float32),
            jax.ShapeDtypeStruct(share.shape, jnp.float32),
        ],
        in_specs=[pl.BlockSpec(memory_space=pltpu.VMEM)] * len(operands),
        out_specs=[pl.BlockSpec(memory_space=pltpu.HBM), pl.BlockSpec(memory_space=pltpu.VMEM)],
        scratch_shapes=[
            pltpu.VMEM((layers - 1, *own_columns.shape), jnp.bfloat16),
            pltpu.VMEM(row_pieces[0].shape, jnp.bfloat16),
            pltpu.SemaphoreType.DMA((half * pieces,)),
        ],
        input_output_aliases={len(operands) - 1: 1},
        compiler_params=pltpu.CompilerParams(vmem_limit_bytes=VMEM_BYTES),
        name="end_update",
    )(*operands)
    return result


def per_device(trailing, panel, inverse_factor):
    layers = lax.axis_size("layer")
    count = lax.axis_size("row")
    row_tiles, _, tile, col_tiles, _, _ = trailing.shape
    half = row_tiles // layers
    slots = plane_slots(count)
    factor = make_factor(panel, inverse_factor, half)
    moved = lax.ppermute(
        factor, ("row", "col"), [(a * count + b, slots[a][b] * count + a) for a in range(count) for b in range(count)]
    )
    share = load_share(factor, trailing.reshape(-1, LANES), layers, col_tiles * tile // LANES)
    loaded_factor, share = lax.optimization_barrier((factor, share))
    line = gather_line(factor, loaded_factor, moved, count)
    plane = [moved]
    for step in range(1, count):
        sources = {
            (r, c): (partner(r, plane_mates(count, c)[step], count), c) for r in range(count) for c in range(count)
        }
        if count == 4 and step == 1:
            sources[0, 0], sources[1, 1] = (0, 1), (3, 0)
        plane.append(move(moved, sources, count))
    if count == 4:
        r, c = lax.axis_index("row"), lax.axis_index("col")
        plane[1] = jnp.where((r == c) & (r < 2), factor, plane[1])
    others = []
    for shift in range(1, layers):
        pairs = [((l + shift) % layers, l) for l in range(layers)]
        others += [lax.ppermute(piece, "layer", pairs) for piece in plane]
    share, own_columns, *rows = begin_update(plane, line[:-1], share, layers, tile)
    rows = [line[0], *rows, line[-1]]
    result = end_update(others, rows, own_columns, share, layers, tile)
    return result.reshape(half, 1, tile, col_tiles, 1, tile)


def solution(mesh):
    assert mesh.shape["row"] == mesh.shape["col"]
    return jax.shard_map(
        per_device,
        mesh=mesh,
        in_specs=(P(None, "row", None, None, "col", None), P(None, "row", "col", None), P()),
        out_specs=P("layer", "row", None, None, "col", None),
        check_vma=False,
    )
```

```python
import jax
import jax.numpy as jnp
from jax import lax
from jax.experimental import pallas as pl
from jax.experimental.pallas import tpu as pltpu
from jax.sharding import PartitionSpec as P

LANES = 128
VMEM_BYTES = 24 * 1024 * 1024
LOAD_VMEM_BYTES = 52000 * 1024
FACTOR_VMEM_BYTES = 55040 * 1024
AXES = ("row", "col", "layer")


def split(x):
    parts = []
    for _ in range(3):
        parts.append(x.astype(jnp.bfloat16))
        x = x - parts[-1].astype(jnp.float32)
    return parts


def factor_kernel(panel_ref, inverse_ref, factor_ref, panel_buf, inverse_buf, sems):
    half = factor_ref.shape[0]
    tile_rows = factor_ref.shape[1]
    width = factor_ref.shape[2]
    layer = lax.axis_index("layer")
    copies = [
        pltpu.make_async_copy(panel_ref.at[pl.ds(layer * half, half), 0], panel_buf, sems.at[0]),
        pltpu.make_async_copy(inverse_ref, inverse_buf, sems.at[1]),
    ]
    for copy in copies:
        copy.start()
    for copy in copies:
        copy.wait()
    rows = half * tile_rows
    panel = split(panel_buf[...].reshape(rows, width))
    inverse = split(inverse_buf[...])

    def times(parts, part):
        return lax.dot_general(
            jnp.concatenate(parts, axis=0), part, (((1,), (1,)), ((), ())), preferred_element_type=jnp.float32
        )

    high = times(panel, inverse[0])
    middle = times(panel[:2], inverse[1])
    low = times(panel[:1], inverse[2])
    product = (low + middle[rows:]) + high[2 * rows :]
    product = (product + (middle[:rows] + high[rows : 2 * rows])) + high[:rows]
    factor_ref[...] = product.astype(jnp.bfloat16).reshape(factor_ref.shape)


def make_factor(panel, inverse_factor, half):
    _, _, tile_rows, width = panel.shape
    return pl.pallas_call(
        factor_kernel,
        out_shape=jax.ShapeDtypeStruct((half, tile_rows, width), jnp.bfloat16),
        in_specs=[pl.BlockSpec(memory_space=pltpu.HBM)] * 2,
        out_specs=pl.BlockSpec(memory_space=pltpu.VMEM),
        scratch_shapes=[
            pltpu.VMEM((half, tile_rows, width), jnp.float32),
            pltpu.VMEM((width, width), jnp.float32),
            pltpu.SemaphoreType.DMA((2,)),
        ],
        compiler_params=pltpu.CompilerParams(vmem_limit_bytes=FACTOR_VMEM_BYTES),
        name="factor",
    )(panel, inverse_factor)


def partner(index, step, count):
    return index ^ step if count & (count - 1) == 0 else (index + step) % count


def plane_slots(count):
    if count == 4:
        return ((3, 0, 1, 2), (3, 0, 2, 1), (3, 2, 1, 0), (2, 3, 1, 0))
    return tuple(tuple(count - 1 - b for b in range(count)) for _ in range(count))


def plane_mates(count, plane):
    if count == 4:
        return ((0, 3, 1, 2), (0, 1, 2, 3), (0, 2, 1, 3), (0, 2, 1, 3))[plane]
    return tuple(range(count))


def slab_of(slots, plane, place):
    if len(slots) == 4:
        packed = sum(row.index(p) << 2 * (4 * at + p) for at, row in enumerate(slots) for p in range(4))
        packed -= (packed >> 31) << 32
        return (jnp.int32(packed) >> (2 * (4 * plane + place))) & 3
    slab = jnp.int32(0)
    for at, row in enumerate(slots):
        for b, slot in enumerate(row):
            slab = jnp.where((plane == at) & (place == slot), b, slab)
    return slab


def line_steps(count):
    return (0, 2, 1, 3) if count == 4 else tuple(range(count))


def move(x, sources, count):
    return lax.ppermute(x, ("row", "col"), [(a * count + b, r * count + c) for (r, c), (a, b) in sources.items()])


def gather_line(factor, late_factor, moved, count):
    if count != 4:
        line = [factor]
        for step in range(1, count):
            line.append(lax.ppermute(factor, "col", [(partner(b, step, count), b) for b in range(count)]))
        return line
    places = [(r, c) for r in range(count) for c in range(count)]
    near = move(late_factor, {(r, c): (r ^ 1, c) if r == c else (r, c ^ 1) for r, c in places}, count)
    far = move(late_factor, {(r, c): (r ^ 2, c) if r == c and r % 2 == 1 else (r, c ^ 2) for r, c in places}, count)
    r, c = lax.axis_index("row"), lax.axis_index("col")
    relayed = jnp.where((r == c) & (r % 2 == 1), moved, far)
    relayed = jnp.where(r == c ^ 1, near, relayed)
    last = move(relayed, {(r, c): (r, c ^ 1) for r, c in places}, count)
    return [factor, far, near, last]


def load_kernel(rows, after_ref, lines_ref, share_ref, sem):
    layer = lax.axis_index("layer")
    load = pltpu.make_async_copy(lines_ref.at[pl.ds(layer * rows, rows)], share_ref.at[pl.ds(0, rows)], sem)
    load.start()
    load.wait()


def load_share(after, lines, layers, per_row):
    rows = lines.shape[0] // layers

    def body(*refs):
        load_kernel(rows, *refs)

    return pl.pallas_call(
        body,
        out_shape=jax.ShapeDtypeStruct((rows + per_row, LANES), jnp.float32),
        in_specs=[pl.BlockSpec(memory_space=pl.ANY), pl.BlockSpec(memory_space=pltpu.HBM)],
        out_specs=pl.BlockSpec(memory_space=pltpu.VMEM),
        scratch_shapes=[pltpu.SemaphoreType.DMA],
        compiler_params=pltpu.CompilerParams(vmem_limit_bytes=LOAD_VMEM_BYTES),
        cost_estimate=pl.CostEstimate(flops=0, bytes_accessed=rows * LANES * 8, transcendentals=0),
        name="load_share",
    )(after, lines)


def fill_columns(columns_ref, pieces, slots, r, c, owner):
    half, tile_rows, _ = pieces[0].shape
    tile = tile_rows * len(pieces)
    for step, piece in enumerate(pieces):
        mate = jnp.int32(plane_mates(len(pieces), 0)[step])
        for plane in range(1, len(pieces) if len(pieces) == 4 else 1):
            mate = jnp.where(c == plane, plane_mates(len(pieces), plane)[step], mate)
        slab = slab_of(slots, c, partner(r, mate, len(pieces)))
        for k in range(half):
            at = pl.multiple_of(k * tile + slab * tile_rows, tile_rows)
            columns_ref[pl.ds(at, tile_rows), :] = piece[k]


def product_of(rows, columns):
    half, tile_rows, width = rows.shape
    return lax.dot_general(
        rows.reshape(half * tile_rows, width),
        columns,
        (((1,), (1,)), ((), ())),
        preferred_element_type=jnp.float32,
    )


def subtract(share_ref, product, k, tile, tile_rows, first_row, first_line, per_row):
    for part in range(product.shape[1] // LANES):
        start = (k * tile + first_row) * per_row + first_line + part
        at = pl.ds(start, tile_rows, stride=per_row)
        share_ref[at, :] -= product[k * tile_rows : (k + 1) * tile_rows, part * LANES : (part + 1) * LANES]


def take_rows(rows_ref, columns_ref, c, step, pieces):
    half, tile_rows, _ = rows_ref.shape
    for k in range(half):
        at = pl.multiple_of((k * pieces + partner(c, step, pieces)) * tile_rows, tile_rows)
        rows_ref[k] = columns_ref[pl.ds(at, tile_rows), :]


def begin_kernel(pieces, layers, tile, *refs):
    column_refs, row_refs, rest = refs[:pieces], refs[pieces : 2 * pieces - 1], refs[2 * pieces - 1 :]
    loaded_ref, share_ref, columns_ref, *line_refs = rest
    r, c, layer = (lax.axis_index(axis) for axis in AXES)
    half, tile_rows, _ = row_refs[0].shape
    own_lines = half * tile // LANES
    share_ref[...] = loaded_ref[...]
    fill_columns(columns_ref, column_refs, plane_slots(pieces), r, c, layer)
    for line_ref, row_ref in zip(line_refs, row_refs[1:]):
        line_ref[...] = row_ref[...]
    if pieces == 4:

        @pl.when(r == c)
        def _():
            for step, line_ref in zip(line_steps(pieces)[1:], line_refs):
                take_rows(line_ref, columns_ref, c, step, pieces)

    for step, row_ref in zip(line_steps(pieces), (row_refs[0], *line_refs)):
        first_row = partner(c, step, pieces) * tile_rows
        product = product_of(row_ref[...], columns_ref[...])
        for k in range(half):
            subtract(share_ref, product, k, tile, tile_rows, first_row, layer * own_lines, layers * own_lines)


def begin_update(column_pieces, row_pieces, share, layers, tile):
    pieces = len(column_pieces)
    half, _, width = row_pieces[0].shape

    def body(*refs):
        begin_kernel(pieces, layers, tile, *refs)

    return pl.pallas_call(
        body,
        out_shape=[
            jax.ShapeDtypeStruct(share.shape, jnp.float32),
            jax.ShapeDtypeStruct((half * tile, width), jnp.bfloat16),
            *[jax.ShapeDtypeStruct(row_pieces[0].shape, jnp.bfloat16)] * (pieces - 2),
        ],
        in_specs=[pl.BlockSpec(memory_space=pltpu.VMEM)] * (2 * pieces),
        out_specs=[pl.BlockSpec(memory_space=pltpu.VMEM)] * pieces,
        input_output_aliases={2 * pieces - 1: 0},
        compiler_params=pltpu.CompilerParams(vmem_limit_bytes=VMEM_BYTES),
        name="begin_update",
    )(*column_pieces, *row_pieces, share)


def end_kernel(pieces, layers, tile, *refs):
    others = pieces * (layers - 1)
    column_refs, row_refs, rest = refs[:others], refs[others : others + pieces], refs[others + pieces :]
    own_ref, share_ref, out_ref, _, columns_buf, last_buf, sems = rest
    r, c, layer = (lax.axis_index(axis) for axis in AXES)
    half, tile_rows, _ = row_refs[0].shape
    own_lines = half * tile // LANES
    per_row = layers * own_lines
    owners = [lax.rem(layer + shift, layers) for shift in range(1, layers)]
    for at, owner in enumerate(owners):
        fill_columns(
            columns_buf.at[at], column_refs[at * pieces : (at + 1) * pieces], plane_slots(pieces), r, c, owner
        )
    stores = []
    for at_row, row_ref in enumerate((*row_refs[:-1], last_buf)):
        first_row = partner(c, line_steps(pieces)[at_row], pieces) * tile_rows
        if at_row == pieces - 1:
            last_buf[...] = row_refs[-1][...]
            if pieces == 4:

                @pl.when(r == c)
                def _(step=line_steps(pieces)[-1]):
                    take_rows(last_buf, own_ref, c, step, pieces)

        rows = row_ref[...]
        products = [(product_of(rows, columns_buf[at]), owner) for at, owner in enumerate(owners)]
        if at_row == pieces - 1:
            products.append((product_of(rows, own_ref[...]), layer))
        for k in range(half):
            for product, owner in products:
                subtract(share_ref, product, k, tile, tile_rows, first_row, owner * own_lines, per_row)
            lines = tile_rows * per_row
            start = pl.multiple_of((k * tile + first_row) * per_row, lines)
            store = pltpu.make_async_copy(
                share_ref.at[pl.ds(start, lines)], out_ref.at[pl.ds(start, lines)], sems.at[at_row * half + k]
            )
            store.start()
            stores.append(store)
    for store in stores:
        store.wait()


def end_update(column_pieces, row_pieces, own_columns, share, layers, tile):
    pieces = len(row_pieces)
    half = row_pieces[0].shape[0]
    per_row = layers * own_columns.shape[0] // LANES
    operands = (*column_pieces, *row_pieces, own_columns, share)

    def body(*refs):
        end_kernel(pieces, layers, tile, *refs)

    result, _ = pl.pallas_call(
        body,
        out_shape=[
            jax.ShapeDtypeStruct((half * pieces * row_pieces[0].shape[1] * per_row, LANES), jnp.float32),
            jax.ShapeDtypeStruct(share.shape, jnp.float32),
        ],
        in_specs=[pl.BlockSpec(memory_space=pltpu.VMEM)] * len(operands),
        out_specs=[pl.BlockSpec(memory_space=pltpu.HBM), pl.BlockSpec(memory_space=pltpu.VMEM)],
        scratch_shapes=[
            pltpu.VMEM((layers - 1, *own_columns.shape), jnp.bfloat16),
            pltpu.VMEM(row_pieces[0].shape, jnp.bfloat16),
            pltpu.SemaphoreType.DMA((half * pieces,)),
        ],
        input_output_aliases={len(operands) - 1: 1},
        compiler_params=pltpu.CompilerParams(vmem_limit_bytes=VMEM_BYTES),
        name="end_update",
    )(*operands)
    return result


def per_device(trailing, panel, inverse_factor):
    layers = lax.axis_size("layer")
    count = lax.axis_size("row")
    row_tiles, _, tile, col_tiles, _, _ = trailing.shape
    half = row_tiles // layers
    slots = plane_slots(count)
    factor = make_factor(panel, inverse_factor, half)
    moved = lax.ppermute(
        factor, ("row", "col"), [(a * count + b, slots[a][b] * count + a) for a in range(count) for b in range(count)]
    )
    share = load_share(factor, trailing.reshape(-1, LANES), layers, col_tiles * tile // LANES)
    loaded_factor, share = lax.optimization_barrier((factor, share))
    line = gather_line(factor, loaded_factor, moved, count)
    plane = [moved]
    for step in range(1, count):
        sources = {
            (r, c): (partner(r, plane_mates(count, c)[step], count), c) for r in range(count) for c in range(count)
        }
        if count == 4 and step == 1:
            sources[0, 0], sources[1, 1] = (0, 1), (3, 0)
        plane.append(move(moved, sources, count))
    if count == 4:
        r, c = lax.axis_index("row"), lax.axis_index("col")
        plane[1] = jnp.where((r == c) & (r < 2), factor, plane[1])
    others = []
    for shift in range(1, layers):
        pairs = [((l + shift) % layers, l) for l in range(layers)]
        others += [lax.ppermute(piece, "layer", pairs) for piece in plane]
    share, own_columns, *rows = begin_update(plane, line[:-1], share, layers, tile)
    rows = [line[0], *rows, line[-1]]
    result = end_update(others, rows, own_columns, share, layers, tile)
    return result.reshape(half, 1, tile, col_tiles, 1, tile)


def solution(mesh):
    assert mesh.shape["row"] == mesh.shape["col"]
    return jax.shard_map(
        per_device,
        mesh=mesh,
        in_specs=(P(None, "row", None, None, "col", None), P(None, "row", "col", None), P()),
        out_specs=P("layer", "row", None, None, "col", None),
        check_vma=False,
    )
```

```python
import jax
import jax.numpy as jnp
from jax import lax
from jax.experimental import pallas as pl
from jax.experimental.pallas import tpu as pltpu
from jax.sharding import PartitionSpec as P

LANES = 128
VMEM_BYTES = 24 * 1024 * 1024
LOAD_VMEM_BYTES = 52000 * 1024
FACTOR_VMEM_BYTES = 55040 * 1024
AXES = ("row", "col", "layer")


def split(x):
    parts = []
    for _ in range(3):
        parts.append(x.astype(jnp.bfloat16))
        x = x - parts[-1].astype(jnp.float32)
    return parts


def factor_kernel(panel_ref, inverse_ref, factor_ref, panel_buf, inverse_buf, sems):
    half = factor_ref.shape[0]
    tile_rows = factor_ref.shape[1]
    width = factor_ref.shape[2]
    layer = lax.axis_index("layer")
    copies = [
        pltpu.make_async_copy(panel_ref.at[pl.ds(layer * half, half), 0], panel_buf, sems.at[0]),
        pltpu.make_async_copy(inverse_ref, inverse_buf, sems.at[1]),
    ]
    for copy in copies:
        copy.start()
    for copy in copies:
        copy.wait()
    rows = half * tile_rows
    panel = split(panel_buf[...].reshape(rows, width))
    inverse = split(inverse_buf[...])

    def times(parts, part):
        return lax.dot_general(
            jnp.concatenate(parts, axis=0), part, (((1,), (1,)), ((), ())), preferred_element_type=jnp.float32
        )

    high = times(panel, inverse[0])
    middle = times(panel[:2], inverse[1])
    low = times(panel[:1], inverse[2])
    product = (low + middle[rows:]) + high[2 * rows :]
    product = (product + (middle[:rows] + high[rows : 2 * rows])) + high[:rows]
    factor_ref[...] = product.astype(jnp.bfloat16).reshape(factor_ref.shape)


def make_factor(panel, inverse_factor, half):
    _, _, tile_rows, width = panel.shape
    return pl.pallas_call(
        factor_kernel,
        out_shape=jax.ShapeDtypeStruct((half, tile_rows, width), jnp.bfloat16),
        in_specs=[pl.BlockSpec(memory_space=pltpu.HBM)] * 2,
        out_specs=pl.BlockSpec(memory_space=pltpu.VMEM),
        scratch_shapes=[
            pltpu.VMEM((half, tile_rows, width), jnp.float32),
            pltpu.VMEM((width, width), jnp.float32),
            pltpu.SemaphoreType.DMA((2,)),
        ],
        compiler_params=pltpu.CompilerParams(vmem_limit_bytes=FACTOR_VMEM_BYTES),
        name="factor",
    )(panel, inverse_factor)


def partner(index, step, count):
    return index ^ step if count & (count - 1) == 0 else (index + step) % count


def plane_slots(count):
    if count == 4:
        return ((3, 0, 2, 1), (3, 0, 2, 1), (3, 2, 1, 0), (2, 3, 1, 0))
    return tuple(tuple(count - 1 - b for b in range(count)) for _ in range(count))


def plane_mates(count, plane):
    if count == 4:
        return ((0, 3, 2, 1), (0, 1, 2, 3), (0, 2, 1, 3), (0, 2, 1, 3))[plane]
    return tuple(range(count))


def slab_of(slots, plane, place):
    if len(slots) == 4:
        packed = sum(row.index(p) << 2 * (4 * at + p) for at, row in enumerate(slots) for p in range(4))
        packed -= (packed >> 31) << 32
        return (jnp.int32(packed) >> (2 * (4 * plane + place))) & 3
    slab = jnp.int32(0)
    for at, row in enumerate(slots):
        for b, slot in enumerate(row):
            slab = jnp.where((plane == at) & (place == slot), b, slab)
    return slab


def line_steps(count):
    return (0, 2, 1, 3) if count == 4 else tuple(range(count))


def move(x, sources, count):
    return lax.ppermute(x, ("row", "col"), [(a * count + b, r * count + c) for (r, c), (a, b) in sources.items()])


def gather_line(factor, late_factor, moved, count):
    if count != 4:
        line = [factor]
        for step in range(1, count):
            line.append(lax.ppermute(factor, "col", [(partner(b, step, count), b) for b in range(count)]))
        return line
    places = [(r, c) for r in range(count) for c in range(count)]
    near = move(late_factor, {(r, c): (r ^ 1, c) if r == c else (r, c ^ 1) for r, c in places}, count)
    far = move(late_factor, {(r, c): (r ^ 2, c) if r == c and r % 2 == 1 else (r, c ^ 2) for r, c in places}, count)
    r, c = lax.axis_index("row"), lax.axis_index("col")
    relayed = jnp.where((r == c) & (r % 2 == 1), moved, far)
    relayed = jnp.where(r == c ^ 1, near, relayed)
    last = move(relayed, {(r, c): (r, c ^ 1) for r, c in places}, count)
    return [factor, far, near, last]


def load_kernel(rows, after_ref, lines_ref, share_ref, sem):
    layer = lax.axis_index("layer")
    load = pltpu.make_async_copy(lines_ref.at[pl.ds(layer * rows, rows)], share_ref.at[pl.ds(0, rows)], sem)
    load.start()
    load.wait()


def load_share(after, lines, layers, per_row):
    rows = lines.shape[0] // layers

    def body(*refs):
        load_kernel(rows, *refs)

    return pl.pallas_call(
        body,
        out_shape=jax.ShapeDtypeStruct((rows + per_row, LANES), jnp.float32),
        in_specs=[pl.BlockSpec(memory_space=pl.ANY), pl.BlockSpec(memory_space=pltpu.HBM)],
        out_specs=pl.BlockSpec(memory_space=pltpu.VMEM),
        scratch_shapes=[pltpu.SemaphoreType.DMA],
        compiler_params=pltpu.CompilerParams(vmem_limit_bytes=LOAD_VMEM_BYTES),
        cost_estimate=pl.CostEstimate(flops=0, bytes_accessed=rows * LANES * 8, transcendentals=0),
        name="load_share",
    )(after, lines)


def fill_columns(columns_ref, pieces, slots, r, c, owner):
    half, tile_rows, _ = pieces[0].shape
    tile = tile_rows * len(pieces)
    for step, piece in enumerate(pieces):
        mate = jnp.int32(plane_mates(len(pieces), 0)[step])
        for plane in range(1, len(pieces) if len(pieces) == 4 else 1):
            mate = jnp.where(c == plane, plane_mates(len(pieces), plane)[step], mate)
        slab = slab_of(slots, c, partner(r, mate, len(pieces)))
        for k in range(half):
            at = pl.multiple_of(k * tile + slab * tile_rows, tile_rows)
            columns_ref[pl.ds(at, tile_rows), :] = piece[k]


def product_of(rows, columns):
    half, tile_rows, width = rows.shape
    return lax.dot_general(
        rows.reshape(half * tile_rows, width),
        columns,
        (((1,), (1,)), ((), ())),
        preferred_element_type=jnp.float32,
    )


def subtract(share_ref, product, k, tile, tile_rows, first_row, first_line, per_row):
    for part in range(product.shape[1] // LANES):
        start = (k * tile + first_row) * per_row + first_line + part
        at = pl.ds(start, tile_rows, stride=per_row)
        share_ref[at, :] -= product[k * tile_rows : (k + 1) * tile_rows, part * LANES : (part + 1) * LANES]


def take_rows(rows_ref, columns_ref, c, step, pieces):
    half, tile_rows, _ = rows_ref.shape
    for k in range(half):
        at = pl.multiple_of((k * pieces + partner(c, step, pieces)) * tile_rows, tile_rows)
        rows_ref[k] = columns_ref[pl.ds(at, tile_rows), :]


def begin_kernel(pieces, layers, tile, *refs):
    column_refs, row_refs, rest = refs[:pieces], refs[pieces : 2 * pieces - 1], refs[2 * pieces - 1 :]
    loaded_ref, share_ref, columns_ref, *line_refs = rest
    r, c, layer = (lax.axis_index(axis) for axis in AXES)
    half, tile_rows, _ = row_refs[0].shape
    own_lines = half * tile // LANES
    share_ref[...] = loaded_ref[...]
    fill_columns(columns_ref, column_refs, plane_slots(pieces), r, c, layer)
    for line_ref, row_ref in zip(line_refs, row_refs[1:]):
        line_ref[...] = row_ref[...]
    if pieces == 4:

        @pl.when(r == c)
        def _():
            for step, line_ref in zip(line_steps(pieces)[1:], line_refs):
                take_rows(line_ref, columns_ref, c, step, pieces)

    for step, row_ref in zip(line_steps(pieces), (row_refs[0], *line_refs)):
        first_row = partner(c, step, pieces) * tile_rows
        product = product_of(row_ref[...], columns_ref[...])
        for k in range(half):
            subtract(share_ref, product, k, tile, tile_rows, first_row, layer * own_lines, layers * own_lines)


def begin_update(column_pieces, row_pieces, share, layers, tile):
    pieces = len(column_pieces)
    half, _, width = row_pieces[0].shape

    def body(*refs):
        begin_kernel(pieces, layers, tile, *refs)

    return pl.pallas_call(
        body,
        out_shape=[
            jax.ShapeDtypeStruct(share.shape, jnp.float32),
            jax.ShapeDtypeStruct((half * tile, width), jnp.bfloat16),
            *[jax.ShapeDtypeStruct(row_pieces[0].shape, jnp.bfloat16)] * (pieces - 2),
        ],
        in_specs=[pl.BlockSpec(memory_space=pltpu.VMEM)] * (2 * pieces),
        out_specs=[pl.BlockSpec(memory_space=pltpu.VMEM)] * pieces,
        input_output_aliases={2 * pieces - 1: 0},
        compiler_params=pltpu.CompilerParams(vmem_limit_bytes=VMEM_BYTES),
        name="begin_update",
    )(*column_pieces, *row_pieces, share)


def end_kernel(pieces, layers, tile, *refs):
    others = pieces * (layers - 1)
    column_refs, row_refs, rest = refs[:others], refs[others : others + pieces], refs[others + pieces :]
    own_ref, share_ref, out_ref, _, columns_buf, last_buf, sems = rest
    r, c, layer = (lax.axis_index(axis) for axis in AXES)
    half, tile_rows, _ = row_refs[0].shape
    own_lines = half * tile // LANES
    per_row = layers * own_lines
    owners = [lax.rem(layer + shift, layers) for shift in range(1, layers)]
    for at, owner in enumerate(owners):
        fill_columns(
            columns_buf.at[at], column_refs[at * pieces : (at + 1) * pieces], plane_slots(pieces), r, c, owner
        )
    last_buf[...] = row_refs[-1][...]
    if pieces == 4:

        @pl.when(r == c)
        def _():
            take_rows(last_buf, own_ref, c, line_steps(pieces)[-1], pieces)

    stores = []
    for at_row, row_ref in enumerate((*row_refs[:-1], last_buf)):
        first_row = partner(c, line_steps(pieces)[at_row], pieces) * tile_rows
        rows = row_ref[...]
        products = [(product_of(rows, columns_buf[at]), owner) for at, owner in enumerate(owners)]
        if at_row == pieces - 1:
            products.append((product_of(rows, own_ref[...]), layer))
        for k in range(half):
            for product, owner in products:
                subtract(share_ref, product, k, tile, tile_rows, first_row, owner * own_lines, per_row)
            lines = tile_rows * per_row
            start = pl.multiple_of((k * tile + first_row) * per_row, lines)
            store = pltpu.make_async_copy(
                share_ref.at[pl.ds(start, lines)], out_ref.at[pl.ds(start, lines)], sems.at[at_row * half + k]
            )
            store.start()
            stores.append(store)
    for store in stores:
        store.wait()


def end_update(column_pieces, row_pieces, own_columns, share, layers, tile):
    pieces = len(row_pieces)
    half = row_pieces[0].shape[0]
    per_row = layers * own_columns.shape[0] // LANES
    operands = (*column_pieces, *row_pieces, own_columns, share)

    def body(*refs):
        end_kernel(pieces, layers, tile, *refs)

    result, _ = pl.pallas_call(
        body,
        out_shape=[
            jax.ShapeDtypeStruct((half * pieces * row_pieces[0].shape[1] * per_row, LANES), jnp.float32),
            jax.ShapeDtypeStruct(share.shape, jnp.float32),
        ],
        in_specs=[pl.BlockSpec(memory_space=pltpu.VMEM)] * len(operands),
        out_specs=[pl.BlockSpec(memory_space=pltpu.HBM), pl.BlockSpec(memory_space=pltpu.VMEM)],
        scratch_shapes=[
            pltpu.VMEM((layers - 1, *own_columns.shape), jnp.bfloat16),
            pltpu.VMEM(row_pieces[0].shape, jnp.bfloat16),
            pltpu.SemaphoreType.DMA((half * pieces,)),
        ],
        input_output_aliases={len(operands) - 1: 1},
        compiler_params=pltpu.CompilerParams(vmem_limit_bytes=VMEM_BYTES),
        name="end_update",
    )(*operands)
    return result


def per_device(trailing, panel, inverse_factor):
    layers = lax.axis_size("layer")
    count = lax.axis_size("row")
    row_tiles, _, tile, col_tiles, _, _ = trailing.shape
    half = row_tiles // layers
    slots = plane_slots(count)
    factor = make_factor(panel, inverse_factor, half)
    moved = lax.ppermute(
        factor, ("row", "col"), [(a * count + b, slots[a][b] * count + a) for a in range(count) for b in range(count)]
    )
    share = load_share(factor, trailing.reshape(-1, LANES), layers, col_tiles * tile // LANES)
    loaded_factor, share = lax.optimization_barrier((factor, share))
    line = gather_line(factor, loaded_factor, moved, count)
    plane = [moved]
    for step in range(1, count):
        sources = {
            (r, c): (partner(r, plane_mates(count, c)[step], count), c) for r in range(count) for c in range(count)
        }
        if count == 4 and step == 1:
            sources[0, 0], sources[1, 1] = (0, 1), (3, 0)
        plane.append(move(moved, sources, count))
    if count == 4:
        r, c = lax.axis_index("row"), lax.axis_index("col")
        plane[1] = jnp.where((r == c) & (r < 2), factor, plane[1])
    others = []
    for shift in range(1, layers):
        pairs = [((l + shift) % layers, l) for l in range(layers)]
        others += [lax.ppermute(piece, "layer", pairs) for piece in plane]
    share, own_columns, *rows = begin_update(plane, line[:-1], share, layers, tile)
    rows = [line[0], *rows, line[-1]]
    result = end_update(others, rows, own_columns, share, layers, tile)
    return result.reshape(half, 1, tile, col_tiles, 1, tile)


def solution(mesh):
    assert mesh.shape["row"] == mesh.shape["col"]
    return jax.shard_map(
        per_device,
        mesh=mesh,
        in_specs=(P(None, "row", None, None, "col", None), P(None, "row", "col", None), P()),
        out_specs=P("layer", "row", None, None, "col", None),
        check_vma=False,
    )
```

```python
import jax
import jax.numpy as jnp
from jax import lax
from jax.experimental import pallas as pl
from jax.experimental.pallas import tpu as pltpu
from jax.sharding import PartitionSpec as P

LANES = 128
VMEM_BYTES = 24 * 1024 * 1024
LOAD_VMEM_BYTES = 52000 * 1024
FACTOR_VMEM_BYTES = 55040 * 1024
AXES = ("row", "col", "layer")


def split(x):
    parts = []
    for _ in range(3):
        parts.append(x.astype(jnp.bfloat16))
        x = x - parts[-1].astype(jnp.float32)
    return parts


def factor_kernel(panel_ref, inverse_ref, factor_ref, panel_buf, inverse_buf, sems):
    half = factor_ref.shape[0]
    tile_rows = factor_ref.shape[1]
    width = factor_ref.shape[2]
    layer = lax.axis_index("layer")
    copies = [
        pltpu.make_async_copy(panel_ref.at[pl.ds(layer * half, half), 0], panel_buf, sems.at[0]),
        pltpu.make_async_copy(inverse_ref, inverse_buf, sems.at[1]),
    ]
    for copy in copies:
        copy.start()
    for copy in copies:
        copy.wait()
    rows = half * tile_rows
    panel = split(panel_buf[...].reshape(rows, width))
    inverse = split(inverse_buf[...])

    def times(parts, part):
        return lax.dot_general(
            jnp.concatenate(parts, axis=0), part, (((1,), (1,)), ((), ())), preferred_element_type=jnp.float32
        )

    high = times(panel, inverse[0])
    middle = times(panel[:2], inverse[1])
    low = times(panel[:1], inverse[2])
    product = (low + middle[rows:]) + high[2 * rows :]
    product = (product + (middle[:rows] + high[rows : 2 * rows])) + high[:rows]
    factor_ref[...] = product.astype(jnp.bfloat16).reshape(factor_ref.shape)


def make_factor(panel, inverse_factor, half):
    _, _, tile_rows, width = panel.shape
    return pl.pallas_call(
        factor_kernel,
        out_shape=jax.ShapeDtypeStruct((half, tile_rows, width), jnp.bfloat16),
        in_specs=[pl.BlockSpec(memory_space=pltpu.HBM)] * 2,
        out_specs=pl.BlockSpec(memory_space=pltpu.VMEM),
        scratch_shapes=[
            pltpu.VMEM((half, tile_rows, width), jnp.float32),
            pltpu.VMEM((width, width), jnp.float32),
            pltpu.SemaphoreType.DMA((2,)),
        ],
        compiler_params=pltpu.CompilerParams(vmem_limit_bytes=FACTOR_VMEM_BYTES),
        name="factor",
    )(panel, inverse_factor)


def partner(index, step, count):
    return index ^ step if count & (count - 1) == 0 else (index + step) % count


def plane_slots(count):
    if count == 4:
        return ((3, 0, 2, 1), (2, 0, 3, 1), (3, 2, 1, 0), (2, 3, 1, 0))
    return tuple(tuple(count - 1 - b for b in range(count)) for _ in range(count))


def plane_mates(count, plane):
    if count == 4:
        return ((0, 3, 2, 1), (0, 1, 2, 3), (0, 2, 1, 3), (0, 2, 1, 3))[plane]
    return tuple(range(count))


def slab_of(slots, plane, place):
    if len(slots) == 4:
        packed = sum(row.index(p) << 2 * (4 * at + p) for at, row in enumerate(slots) for p in range(4))
        packed -= (packed >> 31) << 32
        return (jnp.int32(packed) >> (2 * (4 * plane + place))) & 3
    slab = jnp.int32(0)
    for at, row in enumerate(slots):
        for b, slot in enumerate(row):
            slab = jnp.where((plane == at) & (place == slot), b, slab)
    return slab


def line_steps(count):
    return (0, 2, 1, 3) if count == 4 else tuple(range(count))


def move(x, sources, count):
    return lax.ppermute(x, ("row", "col"), [(a * count + b, r * count + c) for (r, c), (a, b) in sources.items()])


def gather_line(factor, late_factor, moved, count):
    if count != 4:
        line = [factor]
        for step in range(1, count):
            line.append(lax.ppermute(factor, "col", [(partner(b, step, count), b) for b in range(count)]))
        return line
    places = [(r, c) for r in range(count) for c in range(count)]
    near = move(late_factor, {(r, c): (r ^ 1, c) if r == c else (r, c ^ 1) for r, c in places}, count)
    far = move(late_factor, {(r, c): (r ^ 2, c) if r == c and r % 2 == 1 else (r, c ^ 2) for r, c in places}, count)
    r, c = lax.axis_index("row"), lax.axis_index("col")
    relayed = jnp.where((r == c) & (r % 2 == 1), moved, far)
    relayed = jnp.where(r == c ^ 1, near, relayed)
    last = move(relayed, {(r, c): (r, c ^ 1) for r, c in places}, count)
    return [factor, far, near, last]


def load_kernel(rows, after_ref, lines_ref, share_ref, sem):
    layer = lax.axis_index("layer")
    load = pltpu.make_async_copy(lines_ref.at[pl.ds(layer * rows, rows)], share_ref.at[pl.ds(0, rows)], sem)
    load.start()
    load.wait()


def load_share(after, lines, layers, per_row):
    rows = lines.shape[0] // layers

    def body(*refs):
        load_kernel(rows, *refs)

    return pl.pallas_call(
        body,
        out_shape=jax.ShapeDtypeStruct((rows + per_row, LANES), jnp.float32),
        in_specs=[pl.BlockSpec(memory_space=pl.ANY), pl.BlockSpec(memory_space=pltpu.HBM)],
        out_specs=pl.BlockSpec(memory_space=pltpu.VMEM),
        scratch_shapes=[pltpu.SemaphoreType.DMA],
        compiler_params=pltpu.CompilerParams(vmem_limit_bytes=LOAD_VMEM_BYTES),
        cost_estimate=pl.CostEstimate(flops=0, bytes_accessed=rows * LANES * 8, transcendentals=0),
        name="load_share",
    )(after, lines)


def fill_columns(columns_ref, pieces, slots, r, c, owner):
    half, tile_rows, _ = pieces[0].shape
    tile = tile_rows * len(pieces)
    for step, piece in enumerate(pieces):
        mate = jnp.int32(plane_mates(len(pieces), 0)[step])
        for plane in range(1, len(pieces) if len(pieces) == 4 else 1):
            mate = jnp.where(c == plane, plane_mates(len(pieces), plane)[step], mate)
        slab = slab_of(slots, c, partner(r, mate, len(pieces)))
        for k in range(half):
            at = pl.multiple_of(k * tile + slab * tile_rows, tile_rows)
            columns_ref[pl.ds(at, tile_rows), :] = piece[k]


def product_of(rows, columns):
    half, tile_rows, width = rows.shape
    return lax.dot_general(
        rows.reshape(half * tile_rows, width),
        columns,
        (((1,), (1,)), ((), ())),
        preferred_element_type=jnp.float32,
    )


def subtract(share_ref, product, k, tile, tile_rows, first_row, first_line, per_row):
    for part in range(product.shape[1] // LANES):
        start = (k * tile + first_row) * per_row + first_line + part
        at = pl.ds(start, tile_rows, stride=per_row)
        share_ref[at, :] -= product[k * tile_rows : (k + 1) * tile_rows, part * LANES : (part + 1) * LANES]


def take_rows(rows_ref, columns_ref, c, step, pieces):
    half, tile_rows, _ = rows_ref.shape
    for k in range(half):
        at = pl.multiple_of((k * pieces + partner(c, step, pieces)) * tile_rows, tile_rows)
        rows_ref[k] = columns_ref[pl.ds(at, tile_rows), :]


def begin_kernel(pieces, layers, tile, *refs):
    column_refs, row_refs, rest = refs[:pieces], refs[pieces : 2 * pieces - 1], refs[2 * pieces - 1 :]
    loaded_ref, share_ref, columns_ref, *line_refs = rest
    r, c, layer = (lax.axis_index(axis) for axis in AXES)
    half, tile_rows, _ = row_refs[0].shape
    own_lines = half * tile // LANES
    share_ref[...] = loaded_ref[...]
    fill_columns(columns_ref, column_refs, plane_slots(pieces), r, c, layer)
    for line_ref, row_ref in zip(line_refs, row_refs[1:]):
        line_ref[...] = row_ref[...]
    if pieces == 4:

        @pl.when(r == c)
        def _():
            for step, line_ref in zip(line_steps(pieces)[1:], line_refs):
                take_rows(line_ref, columns_ref, c, step, pieces)

    for step, row_ref in zip(line_steps(pieces), (row_refs[0], *line_refs)):
        first_row = partner(c, step, pieces) * tile_rows
        product = product_of(row_ref[...], columns_ref[...])
        for k in range(half):
            subtract(share_ref, product, k, tile, tile_rows, first_row, layer * own_lines, layers * own_lines)


def begin_update(column_pieces, row_pieces, share, layers, tile):
    pieces = len(column_pieces)
    half, _, width = row_pieces[0].shape

    def body(*refs):
        begin_kernel(pieces, layers, tile, *refs)

    return pl.pallas_call(
        body,
        out_shape=[
            jax.ShapeDtypeStruct(share.shape, jnp.float32),
            jax.ShapeDtypeStruct((half * tile, width), jnp.bfloat16),
            *[jax.ShapeDtypeStruct(row_pieces[0].shape, jnp.bfloat16)] * (pieces - 2),
        ],
        in_specs=[pl.BlockSpec(memory_space=pltpu.VMEM)] * (2 * pieces),
        out_specs=[pl.BlockSpec(memory_space=pltpu.VMEM)] * pieces,
        input_output_aliases={2 * pieces - 1: 0},
        compiler_params=pltpu.CompilerParams(vmem_limit_bytes=VMEM_BYTES),
        name="begin_update",
    )(*column_pieces, *row_pieces, share)


def end_kernel(pieces, layers, tile, *refs):
    others = pieces * (layers - 1)
    column_refs, row_refs, rest = refs[:others], refs[others : others + pieces], refs[others + pieces :]
    own_ref, share_ref, out_ref, _, columns_buf, last_buf, sems = rest
    r, c, layer = (lax.axis_index(axis) for axis in AXES)
    half, tile_rows, _ = row_refs[0].shape
    own_lines = half * tile // LANES
    per_row = layers * own_lines
    owners = [lax.rem(layer + shift, layers) for shift in range(1, layers)]
    for at, owner in enumerate(owners):
        fill_columns(
            columns_buf.at[at], column_refs[at * pieces : (at + 1) * pieces], plane_slots(pieces), r, c, owner
        )
    last_buf[...] = row_refs[-1][...]
    if pieces == 4:

        @pl.when(r == c)
        def _():
            take_rows(last_buf, own_ref, c, line_steps(pieces)[-1], pieces)

    stores = []
    for at_row, row_ref in enumerate((*row_refs[:-1], last_buf)):
        first_row = partner(c, line_steps(pieces)[at_row], pieces) * tile_rows
        rows = row_ref[...]
        products = [(product_of(rows, columns_buf[at]), owner) for at, owner in enumerate(owners)]
        if at_row == pieces - 1:
            products.append((product_of(rows, own_ref[...]), layer))
        for k in range(half):
            for product, owner in products:
                subtract(share_ref, product, k, tile, tile_rows, first_row, owner * own_lines, per_row)
            lines = tile_rows * per_row
            start = pl.multiple_of((k * tile + first_row) * per_row, lines)
            store = pltpu.make_async_copy(
                share_ref.at[pl.ds(start, lines)], out_ref.at[pl.ds(start, lines)], sems.at[at_row * half + k]
            )
            store.start()
            stores.append(store)
    for store in stores:
        store.wait()


def end_update(column_pieces, row_pieces, own_columns, share, layers, tile):
    pieces = len(row_pieces)
    half = row_pieces[0].shape[0]
    per_row = layers * own_columns.shape[0] // LANES
    operands = (*column_pieces, *row_pieces, own_columns, share)

    def body(*refs):
        end_kernel(pieces, layers, tile, *refs)

    result, _ = pl.pallas_call(
        body,
        out_shape=[
            jax.ShapeDtypeStruct((half * pieces * row_pieces[0].shape[1] * per_row, LANES), jnp.float32),
            jax.ShapeDtypeStruct(share.shape, jnp.float32),
        ],
        in_specs=[pl.BlockSpec(memory_space=pltpu.VMEM)] * len(operands),
        out_specs=[pl.BlockSpec(memory_space=pltpu.HBM), pl.BlockSpec(memory_space=pltpu.VMEM)],
        scratch_shapes=[
            pltpu.VMEM((layers - 1, *own_columns.shape), jnp.bfloat16),
            pltpu.VMEM(row_pieces[0].shape, jnp.bfloat16),
            pltpu.SemaphoreType.DMA((half * pieces,)),
        ],
        input_output_aliases={len(operands) - 1: 1},
        compiler_params=pltpu.CompilerParams(vmem_limit_bytes=VMEM_BYTES),
        name="end_update",
    )(*operands)
    return result


def per_device(trailing, panel, inverse_factor):
    layers = lax.axis_size("layer")
    count = lax.axis_size("row")
    row_tiles, _, tile, col_tiles, _, _ = trailing.shape
    half = row_tiles // layers
    slots = plane_slots(count)
    factor = make_factor(panel, inverse_factor, half)
    moved = lax.ppermute(
        factor, ("row", "col"), [(a * count + b, slots[a][b] * count + a) for a in range(count) for b in range(count)]
    )
    share = load_share(factor, trailing.reshape(-1, LANES), layers, col_tiles * tile // LANES)
    loaded_factor, share = lax.optimization_barrier((factor, share))
    line = gather_line(factor, loaded_factor, moved, count)
    plane = [moved]
    for step in range(1, count):
        sources = {
            (r, c): (partner(r, plane_mates(count, c)[step], count), c) for r in range(count) for c in range(count)
        }
        if count == 4 and step == 1:
            sources[0, 0], sources[1, 1] = (0, 1), (3, 0)
        plane.append(move(moved, sources, count))
    if count == 4:
        r, c = lax.axis_index("row"), lax.axis_index("col")
        plane[1] = jnp.where((r == c) & (r < 2), factor, plane[1])
    others = []
    for shift in range(1, layers):
        pairs = [((l + shift) % layers, l) for l in range(layers)]
        others += [lax.ppermute(piece, "layer", pairs) for piece in plane]
    share, own_columns, *rows = begin_update(plane, line[:-1], share, layers, tile)
    rows = [line[0], *rows, line[-1]]
    result = end_update(others, rows, own_columns, share, layers, tile)
    return result.reshape(half, 1, tile, col_tiles, 1, tile)


def solution(mesh):
    assert mesh.shape["row"] == mesh.shape["col"]
    return jax.shard_map(
        per_device,
        mesh=mesh,
        in_specs=(P(None, "row", None, None, "col", None), P(None, "row", "col", None), P()),
        out_specs=P("layer", "row", None, None, "col", None),
        check_vma=False,
    )
```
